32 devices in a mesh: dp: 8 (over z, x), tensor: 4 (over y, core).
Axes of the slice: x: 2, y: 2, z: 4, core: 2. Of those that a mesh axis runs over, the one named last changes fastest.
Arguments:
- tokens: bfloat16 [96, 196, 512], P('dp'), may hold values from -6 to 6
- cotangent: bfloat16 [96, 196, 512], P('dp'), may hold values from -6 to 6
- region_ids: int32 [196], replicated, may hold values from 0 to 3
- relative_index: int32 [49, 49], replicated, may hold values from 0 to 168
- shared_vectors: float32 [6, 512], replicated, may hold values from -1.5 to 2, as said below
- input_weight: float32 [512, 1536], P(None, 'tensor'), may hold values from -0.25 to 0.25
- head_bias: float32 [2, 512], P(None, 'tensor'), may hold values from -3 to 3
- output_weight: float32 [512, 512], P('tensor'), may hold values from -0.75 to 0.75
- expand_weight: float32 [512, 2048], P(None, 'tensor'), may hold values from -0.25 to 0.25
- expand_bias: float32 [2048], P('tensor'), may hold values from -3 to 3
- reduce_weight: float32 [2048, 512], P('tensor'), may hold values from -0.1875 to 0.1875
- bias_table: float32 [169, 16], P(None, 'tensor'), may hold values from -5 to 5
- moment_shared: float32 [6, 512], replicated, may hold values from -1 to 1
- moment_input: float32 [512, 1536], P(None, 'tensor'), may hold values from -1 to 1
- moment_head: float32 [2, 512], P(None, 'tensor'), may hold values from -1 to 1
- moment_output: float32 [512, 512], P('tensor'), may hold values from -1 to 1
- moment_expand: float32 [512, 2048], P(None, 'tensor'), may hold values from -1 to 1
- moment_bias: float32 [2048], P('tensor'), may hold values from -1 to 1
- moment_reduce: float32 [2048, 512], P('tensor'), may hold values from -1 to 1
- moment_table: float32 [169, 16], P(None, 'tensor'), may hold values from -1 to 1
Outputs:
- block_out: bfloat16 [96, 196, 512], P('dp')
- input_grad: float32 [96, 196, 512], P('dp')
- grad_shared: float32 [6, 512], replicated
- grad_input: float32 [512, 1536], P('dp', 'tensor')
- grad_head: float32 [2, 512], P(None, 'tensor')
- grad_output: float32 [512, 512], P('tensor', 'dp')
- grad_expand: float32 [512, 2048], P('dp', 'tensor')
- grad_bias: float32 [2048], P('tensor')
- grad_reduce: float32 [2048, 512], P('tensor', 'dp')
- grad_table: float32 [169, 16], P(None, 'tensor')
- update_shared: float32 [6, 512], replicated
- update_input: float32 [512, 1536], P('dp', 'tensor')
- update_head: float32 [2, 512], P(None, 'tensor')
- update_output: float32 [512, 512], P('tensor', 'dp')
- update_expand: float32 [512, 2048], P('dp', 'tensor')
- update_bias: float32 [2048], P('tensor')
- update_reduce: float32 [2048, 512], P('tensor', 'dp')
- update_table: float32 [169, 16], P(None, 'tensor')
- state_shared: float32 [6, 512], replicated
- state_input: float32 [512, 1536], P('dp', 'tensor')
- state_head: float32 [2, 512], P(None, 'tensor')
- state_output: float32 [512, 512], P('tensor', 'dp')
- state_expand: float32 [512, 2048], P('dp', 'tensor')
- state_bias: float32 [2048], P('tensor')
- state_reduce: float32 [2048, 512], P('tensor', 'dp')
- state_table: float32 [169, 16], P(None, 'tensor')
The draws below stay inside these ranges and needn't reach their ends.
Inputs may be any that keep to these rules, and one draw needn't show every extreme that they name: `shared_vectors`: rows 0 and 3 lie in 0.5 to 2.
All inputs are finite; a program needn't handle non-finite values.
Results may differ from the reference program's by a relative error of at most 0.012.
The reference program's roundings to bfloat16 on the way count: a program that leaves them out, or rounds other values in their place, can miss the bound.
Values sent between devices are 32-bit elements; how exact they have to be, the bound alone decides.
No kernel may reach another device: no remote copies, remote signals or barrier semaphores. Data moves between devices by JAX's collectives and lax.ppermute only.
A program may use at most 256 MiB of HBM per device.

```python
import math
import jax
import jax.numpy as jnp
from jax import lax

D = 512
FF = 2048
H = 16
HEAD = 32
IMG_DEV = 12
SIDE = 14
WIN = 7
SHIFT = 3
NS_STEPS = 5
L = 196
WIN2 = 49
TABLE = 169
IMGS = 96
TOKENS = 18816


def draw_shared_vectors(key, part):
    normal_part = jnp.clip(0.5 * jax.random.normal(jax.random.fold_in(key, 7), (6, D), jnp.float32), -1.5, 1.5)
    levels = jax.random.uniform(jax.random.fold_in(key, 8), (6, D), jnp.float32, 0.5, 2.0)
    gain_rows = (jnp.arange(6) % 3 == 0).astype(jnp.float32)[:, None]
    return gain_rows * levels + (1.0 - gain_rows) * normal_part


def place_ends(drawn, rng, least, high):
    longest = drawn.shape.index(max(drawn.shape))
    spots = []
    for shift in (0, 1):
        where = [jax.random.randint(jax.random.fold_in(rng, axis), (), 0, length) for axis, length in enumerate(drawn.shape)]
        where[longest] = (where[longest] + shift) % drawn.shape[longest]
        spots.append(tuple(where))
    return drawn.at[spots[0]].set(least).at[spots[1]].set(high)


def block_scale(stream_key, shape, cuts, least, top_value):
    def one(axis_at, shards_of):
        steps = jax.random.uniform(jax.random.fold_in(jax.random.fold_in(stream_key, 6), axis_at), (shards_of,), jnp.float32, least / len(cuts), top_value / len(cuts))
        return jnp.repeat(jnp.exp(steps), shape[axis_at] // shards_of).reshape((-1,) + (1,) * (len(shape) - axis_at - 1))

    loudness = one(*cuts[0])
    for cut in cuts[1:]:
        loudness = loudness * one(*cut)
    return loudness


def bell_draw(own_key, shape, scale, limit, cuts=(), dtype=jnp.bfloat16):
    level = block_scale(own_key, shape, cuts, -0.22, 0.18) if cuts else 1.0
    values = jax.random.normal(own_key, shape, jnp.float32) * scale * level
    return jnp.minimum(jnp.maximum(values, -limit), limit).astype(dtype)


def setup_inputs(seed: int = 0) -> dict:
    keys = jax.random.split(jax.random.key(seed), 21)
    tokens = bell_draw(keys[0], (IMGS, L, D), 1.0, 6.0, ((0, 8),))
    cotangent = bell_draw(keys[1], (IMGS, L, D), 1.0, 6.0, ((0, 8),))
    region_ids = place_ends(jax.random.randint(keys[2], (L,), 0, 4), jax.random.fold_in(keys[2], 1), 0, 3).astype(jnp.int32)
    relative_index = place_ends(jax.random.randint(keys[3], (WIN2, WIN2), 0, TABLE), jax.random.fold_in(keys[3], 1), 0, TABLE - 1).astype(jnp.int32)
    shared_vectors = draw_shared_vectors(jax.random.fold_in(keys[20], 71), 0)
    input_weight = bell_draw(keys[5], (D, 3 * D), D ** -0.5, 0.25, ((1, 4),), jnp.float32)
    head_bias = bell_draw(keys[6], (2, D), 0.5, 3.0, ((1, 4),), jnp.float32)
    output_weight = bell_draw(keys[7], (D, D), (D // 8) ** -0.5, 0.75, ((0, 4),), jnp.float32)
    expand_weight = bell_draw(keys[8], (D, FF), D ** -0.5, 0.25, ((1, 4),), jnp.float32)
    expand_bias = bell_draw(keys[9], (FF,), 0.5, 3.0, ((0, 4),), jnp.float32)
    reduce_weight = bell_draw(keys[10], (FF, D), (FF // 2) ** -0.5, 0.1875, ((0, 4),), jnp.float32)
    bias_table = bell_draw(keys[11], (TABLE, H), 1.0, 5.0, ((1, 4),), jnp.float32)
    moment_shared = bell_draw(keys[12], (6, D), 0.15, 1.0, (), jnp.float32)
    moment_input = bell_draw(keys[13], (D, 3 * D), 0.15, 1.0, ((1, 4),), jnp.float32)
    moment_head = bell_draw(keys[14], (2, D), 0.15, 1.0, ((1, 4),), jnp.float32)
    moment_output = bell_draw(keys[15], (D, D), 0.15, 1.0, ((0, 4),), jnp.float32)
    moment_expand = bell_draw(keys[16], (D, FF), 0.15, 1.0, ((1, 4),), jnp.float32)
    moment_bias = bell_draw(keys[17], (FF,), 0.15, 1.0, ((0, 4),), jnp.float32)
    moment_reduce = bell_draw(keys[18], (FF, D), 0.15, 1.0, ((0, 4),), jnp.float32)
    moment_table = bell_draw(keys[19], (TABLE, H), 0.15, 1.0, ((1, 4),), jnp.float32)
    return dict(tokens=tokens, cotangent=cotangent, region_ids=region_ids, relative_index=relative_index, shared_vectors=shared_vectors, input_weight=input_weight, head_bias=head_bias, output_weight=output_weight, expand_weight=expand_weight, expand_bias=expand_bias, reduce_weight=reduce_weight, bias_table=bias_table, moment_shared=moment_shared, moment_input=moment_input, moment_head=moment_head, moment_output=moment_output, moment_expand=moment_expand, moment_bias=moment_bias, moment_reduce=moment_reduce, moment_table=moment_table)


@jax.custom_vjp
def low(v):
    return lax.optimization_barrier(v.astype(jnp.bfloat16)).astype(jnp.float32)

@jax.custom_vjp
def low_back(v):
    return v

def low_keep(v):
    return (low(v), None)

def low_pass(kept, grad):
    return (grad,)

def back_keep(v):
    return (v, None)

def back_low(kept, grad):
    return (low(grad),)
low.defvjp(low_keep, low_pass)
low_back.defvjp(back_keep, back_low)
highest = lax.Precision.HIGHEST
norm_epsilon = 1e-05
moment_decay = 0.8
matrix_rate = 1.0
vector_rate = 1.0
quintic_coef = (3.4445, -4.775, 2.0315)
masked_logit = -1e+30

def layer_norm(values, gain_vector, offset):
    centred = values - lax.optimization_barrier(jnp.mean(values, axis=-1, keepdims=True))
    variance = lax.optimization_barrier(jnp.mean(centred * centred, axis=-1, keepdims=True))
    return centred * lax.rsqrt(variance + norm_epsilon) * gain_vector + offset

def gelu_exact(values):
    return 0.5 * values * (1.0 + lax.erf(values * (1.0 / math.sqrt(2.0))))

def roll_tokens(values, amount):
    image_grid = values.reshape(values.shape[0], SIDE, SIDE, values.shape[-1])
    return jnp.roll(image_grid, (amount, amount), axis=(1, 2)).reshape(values.shape)

def position_tables():
    position = jnp.arange(SIDE * SIDE)
    grid_row = position // SIDE
    grid_col = position % SIDE
    window = grid_row // WIN * (SIDE // WIN) + grid_col // WIN
    inside = grid_row % WIN * WIN + grid_col % WIN
    same_window = window[:, None] == window[None, :]
    placement = (inside[:, None] == jnp.arange(WIN * WIN)[None, :]).astype(jnp.float32)
    return (same_window, placement)

def full_bias(table, relative_index, placement):
    index_pick = (relative_index.reshape(-1)[:, None] == jnp.arange(table.shape[0])[None, :]).astype(jnp.float32)
    window_bias = jnp.dot(index_pick, table, precision=highest).reshape(WIN * WIN, WIN * WIN, table.shape[1])
    return jnp.einsum('pi,ijh,qj->hpq', placement, window_bias, placement, precision=highest)

def block_forward(inputs, shared_vectors, input_weight, head_bias, output_weight, expand_weight, expand_bias, reduce_weight, bias_table, region_ids, relative_index):
    count_images = inputs.shape[0]
    head_count = bias_table.shape[1]
    same_window, placement = position_tables()
    allowed = same_window & (region_ids[:, None] == region_ids[None, :])
    bias_all = full_bias(bias_table, relative_index, placement)
    normed = layer_norm(inputs, shared_vectors[0], shared_vectors[1])
    shifted = low(roll_tokens(normed, -SHIFT))
    projected = low_back(jnp.einsum('gpd,dc->gpc', shifted, low(input_weight), precision=highest))
    split_parts = projected.reshape(count_images, L, head_count, 3, HEAD)
    queries = low((split_parts[:, :, :, 0] + head_bias[0].reshape(head_count, HEAD)) * HEAD ** (-0.5))
    key_rows = low(split_parts[:, :, :, 1])
    value_rows = low(split_parts[:, :, :, 2] + head_bias[1].reshape(head_count, HEAD))
    logits = low_back(jnp.einsum('gphe,gqhe->ghpq', queries, key_rows, precision=highest)) + bias_all[None]
    logits = jnp.where(allowed[None, None], logits, masked_logit)
    row_peak = lax.optimization_barrier(jnp.max(logits, axis=-1, keepdims=True))
    log_total = row_peak + jnp.log(lax.optimization_barrier(jnp.sum(jnp.exp(logits - row_peak), axis=-1, keepdims=True)))
    attn_weights = jnp.exp(logits - log_total)
    context = jnp.einsum('ghpq,gqhe->gphe', low(attn_weights), value_rows, precision=highest)
    context = low(low_back(context)).reshape(count_images, L, D)
    attended = low_back(jnp.einsum('gpc,cd->gpd', context, low(output_weight), precision=highest)) + shared_vectors[2]
    middle = inputs + roll_tokens(attended, SHIFT)
    normed2 = low(layer_norm(middle, shared_vectors[3], shared_vectors[4]))
    hidden = low_back(jnp.einsum('gpd,df->gpf', normed2, low(expand_weight), precision=highest)) + expand_bias
    activated = low(gelu_exact(hidden))
    mixed_out = low_back(jnp.einsum('gpf,fd->gpd', activated, low(reduce_weight), precision=highest)) + shared_vectors[5]
    return middle + mixed_out

def orthogonalize(matrix):
    tall = matrix.shape[0] > matrix.shape[1]
    iterate = matrix.T if tall else matrix
    iterate = iterate * lax.rsqrt(jnp.sum(iterate * iterate) + 1e-07)
    for step_index in range(NS_STEPS):
        gram_matrix = jnp.dot(iterate, iterate.T, precision=highest)
        polynomial = quintic_coef[1] * gram_matrix + quintic_coef[2] * jnp.dot(gram_matrix, gram_matrix, precision=highest)
        iterate = quintic_coef[0] * iterate + jnp.dot(polynomial, iterate, precision=highest)
    return iterate.T if tall else iterate

def reference(tokens, cotangent, region_ids, relative_index, shared_vectors, input_weight, head_bias, output_weight, expand_weight, expand_bias, reduce_weight, bias_table, moment_shared, moment_input, moment_head, moment_output, moment_expand, moment_bias, moment_reduce, moment_table):
    params = (shared_vectors, input_weight, head_bias, output_weight, expand_weight, expand_bias, reduce_weight, bias_table)
    group_count = IMGS // IMG_DEV
    token_groups = tokens.reshape(group_count, IMG_DEV, L, D)
    cot_groups = cotangent.reshape(group_count, IMG_DEV, L, D)

    def one_group(carried, pair):
        group_tokens, group_cot = pair

        def forward(inputs, *weights):
            return block_forward(inputs, *weights, region_ids, relative_index)
        result, pullback = jax.vjp(forward, group_tokens.astype(jnp.float32), *params)
        pulled = pullback(group_cot.astype(jnp.float32))
        carried = tuple((summed + gradient for summed, gradient in zip(carried, pulled[1:])))
        return (carried, (result.astype(jnp.bfloat16), pulled[0]))
    zero_sums = tuple((jnp.zeros_like(weight) for weight in params))
    sums, (outputs, input_grads) = lax.scan(one_group, zero_sums, (token_groups, cot_groups))
    block_out = outputs.reshape(IMGS, L, D)
    input_grad = input_grads.reshape(IMGS, L, D)
    grad_scale = TOKENS ** (-0.5)
    gradients = [summed * grad_scale for summed in sums]
    moments = [moment_shared, moment_input, moment_head, moment_output, moment_expand, moment_bias, moment_reduce, moment_table]
    states = [moment_decay * moment + (1.0 - moment_decay) * gradient for moment, gradient in zip(moments, gradients)]
    updates = []
    for param_id in range(8):
        if param_id in (1, 3, 4, 6):
            new_state = states[param_id]
            factor = math.sqrt(max(1.0, new_state.shape[0] / new_state.shape[1]))
            updates.append(-matrix_rate * factor * orthogonalize(new_state))
        else:
            updates.append(-vector_rate * states[param_id])
    return (block_out, input_grad, gradients[0], gradients[1], gradients[2], gradients[3], gradients[4], gradients[5], gradients[6], gradients[7], updates[0], updates[1], updates[2], updates[3], updates[4], updates[5], updates[6], updates[7], states[0], states[1], states[2], states[3], states[4], states[5], states[6], states[7])
```

```python
import functools
import math

import jax
import jax.numpy as jnp
import numpy as np
from jax import lax
from jax.experimental import pallas as pl
from jax.experimental.pallas import tpu as pltpu
from jax.sharding import PartitionSpec as P

SIDE = 14
WIN = 7
SHIFT = 3
NS_STEPS = 5
WIN2 = WIN * WIN
LEN = SIDE * SIDE
ROWS = 208
WPAD = 64
WROWS = 4 * WPAD

highest = lax.Precision.HIGHEST
norm_epsilon = 1e-05
moment_decay = 0.8
matrix_rate = 1.0
vector_rate = 1.0
quintic_coef = (3.4445, -4.775, 2.0315)
masked_logit = -1e30
f32 = jnp.float32
bf16 = jnp.bfloat16
VMEM = pl.BlockSpec(memory_space=pltpu.VMEM)


def params(limit_mib=56, **kw):
    return pltpu.CompilerParams(vmem_limit_bytes=limit_mib * 1024 * 1024, **kw)


def nn(a, b, **kw):
    return lax.dot_general(a, b, (((1,), (0,)), ((), ())), preferred_element_type=f32, **kw)


def nt(a, b, **kw):
    return lax.dot_general(a, b, (((1,), (1,)), ((), ())), preferred_element_type=f32, **kw)


def tn(a, b, **kw):
    return lax.dot_general(a, b, (((0,), (0,)), ((), ())), preferred_element_type=f32, **kw)


def window_tables():
    pick = np.zeros((WROWS, LEN), np.float32)
    place = np.zeros((4, WIN2), np.int32)
    for r in range(SIDE):
        for c in range(SIDE):
            w = (r // WIN) * 2 + c // WIN
            i = (r % WIN) * WIN + c % WIN
            source = ((r + SHIFT) % SIDE) * SIDE + (c + SHIFT) % SIDE
            pick[w * WPAD + i, source] = 1.0
            place[w, i] = r * SIDE + c
    return pick, place


def column_order(heads, size):
    width = 3 * heads * size
    order = np.zeros((width, width), np.float32)
    for h in range(heads):
        for part in range(3):
            for e in range(size):
                order[(h * 3 + part) * size + e, part * heads * size + h * size + e] = 1.0
    return order


def norm_parts(x):
    centred = x - jnp.mean(x, axis=-1, keepdims=True)
    scale = lax.rsqrt(jnp.mean(centred * centred, axis=-1, keepdims=True) + norm_epsilon)
    return centred * scale, scale


def norm_back(n, scale, gain, u):
    w = u * gain
    return scale * (
        w - jnp.mean(w, axis=-1, keepdims=True) - n * jnp.mean(w * n, axis=-1, keepdims=True)
    )


def head_blocks(x, masks):
    return jnp.concatenate([x * m for m in masks], axis=0)


def head_diag(r, masks):
    rows = r.shape[0] // 4
    out = r[0:rows] * masks[0]
    for h in range(1, 4):
        out = out + r[h * rows : (h + 1) * rows] * masks[h]
    return out


def head_masks(dtype):
    lane = lax.broadcasted_iota(jnp.int32, (1, 128), 1) // 32
    return [jnp.where(lane == h, 1.0, 0.0).astype(dtype) for h in range(4)]


def attn_forward(scale, t_ref, tok, w0, w1, w2, w3, hb, sv, bias, mask, pick, order, p_out, qkv_out,
                 sht_out, ctx_out, wcol):
    @pl.when(pl.program_id(0) == 0)
    def _():
        for k, w in enumerate((w0, w1, w2, w3)):
            wcol[k] = nn(w[...].astype(bf16), order[...]).astype(bf16)

    n, _ = norm_parts(tok[0].astype(f32))
    normed = (n * sv[0:1] + sv[1:2]).astype(bf16)
    shifted_f = nn(pick[...], normed)
    shifted = shifted_f.astype(bf16)
    sht_out[0] = shifted_f.T.astype(bf16)
    low_masks = head_masks(bf16)
    masks = head_masks(f32)
    for k in range(4):
        proj = nn(shifted, wcol[k])
        q = ((proj[:, 0:128] + hb[k, 0:1]) * scale).astype(bf16)
        kk = proj[:, 128:256].astype(bf16)
        v = (proj[:, 256:384] + hb[k, 1:2]).astype(bf16)
        qkv_out[0, k, :, 0:128] = q
        qkv_out[0, k, :, 128:256] = kk
        qkv_out[0, k, :, 256:384] = v
        windows = []
        for w in range(4):
            rows = slice(w * WPAD, (w + 1) * WPAD)
            logits = nt(kk[rows], head_blocks(q[rows], low_masks)) + (bias[k] + mask[w])
            e = jnp.exp(logits - jnp.max(logits, axis=0, keepdims=True))
            p = e * (1.0 / jnp.sum(e, axis=0, keepdims=True))
            p_out[0, k, w] = p
            windows.append(head_diag(tn(p.astype(bf16), v[rows]), masks).astype(bf16))
        ctx = jnp.concatenate(windows, axis=0)
        ctx_out[0, 0:LEN, k * 128 : (k + 1) * 128] = tn(pick[...], ctx).astype(bf16)
        ctx_out[0, LEN:ROWS, k * 128 : (k + 1) * 128] = jnp.zeros((ROWS - LEN, 128), bf16)


def feed_forward(images, t_ref, ctx, tok, cot, o0, o1, o2, o3, e0, e1, e2, e3, r0, r1, r2, r3, eb, sv,
                 out_ref, gmid_ref, gctx_ref, grad_ref, geb_ref, small_ref,
                 we, wr, wo, x_s, cot_s, mid_s, n2_s, n2t_s, cott_s, mix_s, gn2_s):
    rows = x_s.shape[0]
    x_s[...] = jnp.zeros_like(x_s)
    for i in range(images):
        x_s[i * ROWS : i * ROWS + LEN] = tok[i].astype(f32)
    for k, (o, e, r) in enumerate(((o0, e0, r0), (o1, e1, r1), (o2, e2, r2), (o3, e3, r3))):
        wo[k * 128 : (k + 1) * 128] = o[...].astype(bf16)
        for half in range(2):
            we[2 * k + half] = e[:, half * 256 : (half + 1) * 256].astype(bf16)
            wr[2 * k + half] = r[half * 256 : (half + 1) * 256].astype(bf16)
    attended = jnp.concatenate(
        [ctx[...].reshape(images * ROWS, 512), jnp.zeros((rows - images * ROWS, 512), bf16)], axis=0
    )
    mid_s[...] = x_s[...] + nn(attended, wo[...]) + sv[2:3]
    n2, _ = norm_parts(mid_s[...])
    n2f = n2 * sv[3:4] + sv[4:5]
    n2_s[...] = n2f.astype(bf16)
    n2t_s[...] = n2f.T.astype(bf16)
    x_s[...] = jnp.zeros_like(x_s)
    for i in range(images):
        x_s[i * ROWS : i * ROWS + LEN] = cot[i].astype(f32)
    cot_s[...] = x_s[...].astype(bf16)
    cott_s[...] = x_s[...].T.astype(bf16)
    mix_s[...] = jnp.zeros_like(mix_s)
    gn2_s[...] = jnp.zeros_like(gn2_s)

    def body(j, carry):
        hidden = nn(n2_s[...], we[j]) + eb[j]
        cdf = 0.5 * (1.0 + lax.erf(hidden * (1.0 / math.sqrt(2.0))))
        act = (hidden * cdf).astype(bf16)
        slope = cdf + hidden * jnp.exp(-0.5 * hidden * hidden) * (1.0 / math.sqrt(2.0 * math.pi))
        mix_s[...] += nn(act, wr[j])
        g_hidden = nt(cot_s[...], wr[j]) * slope
        geb_ref[j] = jnp.sum(g_hidden, axis=0, keepdims=True)
        low = g_hidden.astype(bf16)
        gn2_s[...] += nt(low, we[j])
        at = pl.multiple_of(lax.rem(j, 2) * 256, 256)
        grad_ref[j // 2, :, pl.ds(128 + at, 256)] = nn(n2t_s[...], low)
        grad_ref[j // 2, :, pl.ds(640 + at, 256)] = nn(cott_s[...], act)
        return carry

    lax.fori_loop(0, 8, body, 0)
    result = mid_s[...] + mix_s[...] + sv[5:6]
    for i in range(images):
        out_ref[i] = result[i * ROWS : i * ROWS + LEN].astype(bf16).astype(f32)
    n2, scale2 = norm_parts(mid_s[...])
    u = gn2_s[...]
    gmid = x_s[...] + norm_back(n2, scale2, sv[3:4], u)
    gmid_ref[...] = gmid
    small_ref[0:1] = jnp.sum(gmid, axis=0, keepdims=True)
    small_ref[1:2] = jnp.sum(u * n2, axis=0, keepdims=True)
    small_ref[2:3] = jnp.sum(u, axis=0, keepdims=True)
    small_ref[3:4] = jnp.sum(x_s[...], axis=0, keepdims=True)
    small_ref[4:8] = jnp.zeros((4, 512), f32)
    att_low = gmid.astype(bf16)
    gctx_ref[...] = nt(att_low, wo[...]).astype(bf16)[0 : images * ROWS].reshape(images, ROWS, 512)
    att_t = gmid.T.astype(bf16)
    g_out = nn(att_t, attended)
    for k in range(4):
        grad_ref[k, :, 0:128] = g_out[:, k * 128 : (k + 1) * 128]


def attn_backward(scale, p_in, qkv, gctx, sht, pick, order, gi_ref, plow_ref, gbias_ref, ghead_ref):
    @pl.when(pl.program_id(0) == 0)
    def _():
        gi_ref[...] = jnp.zeros_like(gi_ref)
        gbias_ref[...] = jnp.zeros_like(gbias_ref)
        ghead_ref[...] = jnp.zeros_like(ghead_ref)

    gwin = nn(pick[...], gctx[0, 0:LEN]).astype(bf16)
    low_masks = head_masks(bf16)
    masks = head_masks(f32)
    for k in range(4):
        q = qkv[0, k, :, 0:128]
        kk = qkv[0, k, :, 128:256]
        v = qkv[0, k, :, 256:384]
        parts = []
        bias_sum = None
        q_sum = None
        v_sum = None
        for w in range(4):
            rows = slice(w * WPAD, (w + 1) * WPAD)
            gbd = head_blocks(gwin[rows, k * 128 : (k + 1) * 128], low_masks)
            p = p_in[0, k, w]
            gp = nt(v[rows], gbd)
            gl = p * (gp - jnp.sum(p * gp, axis=0, keepdims=True))
            low = gl.astype(bf16)
            gq = head_diag(tn(low, kk[rows]), masks) * scale
            gk = nn(low, head_blocks(q[rows], low_masks))
            gv = nn(p.astype(bf16), gbd)
            bias_sum = gl if w == 0 else bias_sum + gl
            sq = jnp.sum(gq, axis=0, keepdims=True)
            sv_ = jnp.sum(gv, axis=0, keepdims=True)
            q_sum = sq if w == 0 else q_sum + sq
            v_sum = sv_ if w == 0 else v_sum + sv_
            parts.append(jnp.concatenate([gq, gk, gv], axis=1).astype(bf16))
        gbias_ref[k] += bias_sum
        ghead_ref[k, 0:1] += q_sum
        ghead_ref[k, 1:2] += v_sum
        plow = nt(jnp.concatenate(parts, axis=0), order[...]).astype(bf16)
        gi_ref[k] += nn(sht[0], plow)
        plow_ref[0, k, 0:LEN] = tn(pick[...], plow).astype(bf16)
        plow_ref[0, k, LEN:ROWS] = jnp.zeros((ROWS - LEN, plow.shape[1]), bf16)


def input_backward(t_ref, tok, gmid, plow, w0, w1, w2, w3, sv, out_ref, small_ref, wlow):
    @pl.when(pl.program_id(0) == 0)
    def _():
        small_ref[...] = jnp.zeros_like(small_ref)
        for k, w in enumerate((w0, w1, w2, w3)):
            wlow[k] = w[...].astype(bf16)

    u = nt(plow[0, 0], wlow[0])
    for k in range(1, 4):
        u = u + nt(plow[0, k], wlow[k])
    u = u[0:LEN]
    n, scale = norm_parts(tok[0].astype(f32))
    small_ref[0:1] += jnp.sum(u * n, axis=0, keepdims=True)
    small_ref[1:2] += jnp.sum(u, axis=0, keepdims=True)
    out_ref[0] = gmid[0:LEN] + norm_back(n, scale, sv[0:1], u)


def assemble(t_ref, a0, a1, a2, a3, out):
    for k, a in enumerate((a0, a1, a2, a3)):
        @pl.when(pl.program_id(0) == k)
        def _(a=a):
            out[...] = a[...].astype(out.dtype)


def gram_kernel(cuts, m_ref, g_ref):
    for m, (start, stop) in enumerate(cuts):
        part = m_ref[:, start:stop]
        g_ref[m] = nt(part, part, precision=highest)


def newton_schulz(g_ref, q_ref, a_s, b_s):
    g = g_ref[...]
    size = g.shape[0]
    row = lax.broadcasted_iota(jnp.int32, (size, size), 0)
    col = lax.broadcasted_iota(jnp.int32, (size, size), 1)
    eye = jnp.where(row == col, 1.0, 0.0)
    inv = 1.0 / (jnp.sum(g * eye) + 1e-07)
    a_s[...] = g * inv
    c0, c1, c2 = quintic_coef
    for step in range(NS_STEPS):
        a = a_s[...]
        b_s[...] = c0 * eye + c1 * a + c2 * nn(a, a, precision=highest)
        if step == 0:
            q_ref[...] = b_s[...]
        else:
            q_ref[...] = nn(b_s[...], q_ref[...], precision=highest)
        if step < NS_STEPS - 1:
            a_s[...] = nn(b_s[...], nn(b_s[...], a_s[...], precision=highest), precision=highest)
    q_ref[...] = q_ref[...] * lax.rsqrt(jnp.full((1, 1), 1.0, f32) / inv)


def final_kernel(cuts, factors, q_ref, m_ref, u_ref):
    for m, (start, stop) in enumerate(cuts):
        u_ref[:, start:stop] = (-matrix_rate * factors[m]) * nn(
            q_ref[m], m_ref[:, start:stop], precision=highest
        )


def xor_tensor(x, k):
    return lax.ppermute(x, "tensor", [(i, i ^ k) for i in range(lax.axis_size("tensor"))])


def xor_dp(x, k):
    return lax.ppermute(x, "dp", [(i, i ^ k) for i in range(lax.axis_size("dp"))])


def gather_tensor(block):
    near = xor_tensor(block, 1)
    far = xor_tensor(block, 2)
    return [block, near, far, xor_tensor(far, 1)]


def scatter_tensor(blocks):
    got = xor_tensor(jnp.stack([blocks[1], blocks[3]]), 1)
    own = blocks[0] + got[0]
    far = blocks[2] + got[1]
    return own + xor_tensor(far, 2)


def scatter_dp(values):
    count = lax.axis_size("dp")
    piece = values.shape[0] // count
    me = lax.axis_index("dp")
    cut = values.reshape(count, piece, values.shape[1])
    bit = 1
    while bit < count:
        here = (me // bit) % 2
        cut = cut.reshape(cut.shape[0] // 2, 2, piece, values.shape[1])
        keep = lax.dynamic_index_in_dim(cut, here, 1, keepdims=False)
        send = lax.dynamic_index_in_dim(cut, 1 - here, 1, keepdims=False)
        cut = keep + xor_dp(send, bit)
        bit *= 2
    return cut.reshape(piece, values.shape[1])


def gather_dp(piece):
    count = lax.axis_size("dp")
    me = lax.axis_index("dp")
    rows, cols = piece.shape
    whole = piece.reshape(1, rows, cols)
    bit = count // 2
    while bit >= 1:
        here = (me // bit) % 2
        got = xor_dp(whole, bit)
        pair = jnp.where(here == 0, jnp.stack([whole, got], 1), jnp.stack([got, whole], 1))
        whole = pair.reshape(-1, rows, cols)
        bit //= 2
    return whole.reshape(count * rows, cols)


def join_images(t, parts, dtype):
    images, length, features = parts[0].shape

    def source(k):
        return lambda a, i, t_ref: (jnp.where(a == k, i, jnp.where(a < k, 0, images - 1)), 0, 0)

    return pl.pallas_call(
        assemble,
        grid_spec=pltpu.PrefetchScalarGridSpec(
            num_scalar_prefetch=1,
            grid=(4, images),
            in_specs=[pl.BlockSpec((1, length, features), source(k)) for k in range(4)],
            out_specs=pl.BlockSpec(
                (1, length, features), lambda a, i, t_ref: ((t_ref[0] ^ a) * images + i, 0, 0)
            ),
        ),
        out_shape=jax.ShapeDtypeStruct((4 * images, length, features), dtype),
        compiler_params=params(),
        name="join_images",
    )(t, *parts)


def local(
    tokens,
    cotangent,
    region_ids,
    relative_index,
    shared_vectors,
    input_weight,
    head_bias,
    output_weight,
    expand_weight,
    expand_bias,
    reduce_weight,
    bias_table,
    moment_shared,
    moment_input,
    moment_head,
    moment_output,
    moment_expand,
    moment_bias,
    moment_reduce,
    moment_table,
):
    nt_axis = lax.axis_size("tensor")
    me_t = lax.axis_index("tensor")
    me_d = lax.axis_index("dp")
    nd = lax.axis_size("dp")
    all_images, length, features = tokens.shape
    images = all_images // nt_axis
    heads = bias_table.shape[1]
    head_size = head_bias.shape[1] // heads
    width = heads * head_size
    hidden_here = expand_weight.shape[1]
    table_rows = bias_table.shape[0]
    query_scale = head_size ** (-0.5)
    t_arr = me_t.astype(jnp.int32).reshape(1)
    rows = -(-images * ROWS // 128) * 128

    small_in = jnp.concatenate(
        [
            bias_table.T.reshape(-1),
            head_bias.reshape(-1),
            expand_bias.reshape(-1),
            jnp.zeros((4 * 512 - table_rows * heads - 2 * width - hidden_here,), f32)
            if table_rows * heads + 2 * width + hidden_here < 2048
            else jnp.zeros((0,), f32),
        ]
    )
    smalls = gather_tensor(small_in)
    w_in = gather_tensor(input_weight)
    w_out = gather_tensor(output_weight)
    w_exp = gather_tensor(expand_weight)
    w_red = gather_tensor(reduce_weight)
    tables = jnp.concatenate([s[: table_rows * heads].reshape(heads, table_rows) for s in smalls])
    at = table_rows * heads
    hb = jnp.stack([s[at : at + 2 * width].reshape(2, width) for s in smalls])
    at += 2 * width
    eb = jnp.concatenate([s[at : at + hidden_here] for s in smalls]).reshape(8, 1, hidden_here // 2)

    pick_np, place_np = window_tables()
    pick = jnp.asarray(pick_np, bf16)
    order = jnp.asarray(column_order(heads, head_size), bf16)
    rel_t = jnp.pad(relative_index.T, ((0, 0), (0, WPAD - WIN2)), constant_values=-1)
    pick_table = (jnp.arange(table_rows)[:, None] == rel_t.reshape(1, -1)).astype(f32)
    bias = jnp.dot(tables, pick_table, precision=highest).reshape(4, heads, WIN2, WPAD)
    bias = jnp.pad(bias.transpose(0, 2, 1, 3), ((0, 0), (0, WPAD - WIN2), (0, 0), (0, 0)))
    bias = bias.reshape(4, WPAD, heads * WPAD)
    region = region_ids[place_np]
    allowed = jnp.pad(
        region[:, :, None] == region[:, None, :],
        ((0, 0), (0, 0), (0, WPAD - WIN2)),
        constant_values=True,
    )
    allowed = jnp.pad(allowed, ((0, 0), (0, WPAD - WIN2), (0, 0)))
    mask = jnp.tile(jnp.where(allowed, 0.0, masked_logit).astype(f32), (1, 1, heads))

    whole = lambda *shape: pl.BlockSpec(shape, lambda i, *_: (0,) * len(shape))
    one = lambda *shape: pl.BlockSpec((1,) + shape, lambda i, *_: (i,) + (0,) * len(shape))
    tok_one = pl.BlockSpec((1, length, features), lambda i, t: (t[0] * images + i, 0, 0))

    probs, qkv, sht, ctx = pl.pallas_call(
        functools.partial(attn_forward, query_scale),
        grid_spec=pltpu.PrefetchScalarGridSpec(
            num_scalar_prefetch=1,
            grid=(images,),
            in_specs=[tok_one]
            + [whole(features, 3 * width)] * 4
            + [
                whole(4, 2, width),
                whole(6, features),
                whole(4, WPAD, heads * WPAD),
                whole(4, WPAD, heads * WPAD),
                whole(WROWS, LEN),
                whole(3 * width, 3 * width),
            ],
            out_specs=[
                one(4, 4, WPAD, heads * WPAD),
                one(4, WROWS, 3 * width),
                one(features, WROWS),
                one(ROWS, 4 * width),
            ],
            scratch_shapes=[pltpu.VMEM((4, features, 3 * width), bf16)],
        ),
        out_shape=[
            jax.ShapeDtypeStruct((images, 4, 4, WPAD, heads * WPAD), f32),
            jax.ShapeDtypeStruct((images, 4, WROWS, 3 * width), bf16),
            jax.ShapeDtypeStruct((images, features, WROWS), bf16),
            jax.ShapeDtypeStruct((images, ROWS, 4 * width), bf16),
        ],
        compiler_params=params(),
        name="attn_forward",
    )(t_arr, tokens, *w_in, hb, shared_vectors, bias, mask, pick, order)

    tok_all = pl.BlockSpec((images, length, features), lambda i, t: (t[0], 0, 0))
    wide = width + 2 * hidden_here
    block_part, gmid, gctx, grads_a, geb, small_a = pl.pallas_call(
        functools.partial(feed_forward, images),
        grid_spec=pltpu.PrefetchScalarGridSpec(
            num_scalar_prefetch=1,
            grid=(1,),
            in_specs=[whole(images, ROWS, 4 * width), tok_all, tok_all]
            + [whole(width, features)] * 4
            + [whole(features, hidden_here)] * 4
            + [whole(hidden_here, features)] * 4
            + [whole(8, 1, hidden_here // 2), whole(6, features)],
            out_specs=[
                whole(images, length, features),
                whole(rows, features),
                whole(images, ROWS, 4 * width),
                whole(4, features, wide),
                whole(8, 1, hidden_here // 2),
                whole(8, features),
            ],
            scratch_shapes=[
                pltpu.VMEM((8, features, hidden_here // 2), bf16),
                pltpu.VMEM((8, hidden_here // 2, features), bf16),
                pltpu.VMEM((4 * width, features), bf16),
                pltpu.VMEM((rows, features), f32),
                pltpu.VMEM((rows, features), bf16),
                pltpu.VMEM((rows, features), f32),
                pltpu.VMEM((rows, features), bf16),
                pltpu.VMEM((features, rows), bf16),
                pltpu.VMEM((features, rows), bf16),
                pltpu.VMEM((rows, features), f32),
                pltpu.VMEM((rows, features), f32),
            ],
        ),
        out_shape=[
            jax.ShapeDtypeStruct((images, length, features), f32),
            jax.ShapeDtypeStruct((rows, features), f32),
            jax.ShapeDtypeStruct((images, ROWS, 4 * width), bf16),
            jax.ShapeDtypeStruct((4, features, wide), f32),
            jax.ShapeDtypeStruct((8, 1, hidden_here // 2), f32),
            jax.ShapeDtypeStruct((8, features), f32),
        ],
        compiler_params=params(),
        name="feed_forward",
    )(t_arr, ctx, tokens, cotangent, *w_out, *w_exp, *w_red, eb, shared_vectors)

    grads_i, plow, gbias, ghead = pl.pallas_call(
        functools.partial(attn_backward, query_scale),
        grid=(images,),
        in_specs=[
            one(4, 4, WPAD, heads * WPAD),
            one(4, WROWS, 3 * width),
            one(ROWS, 4 * width),
            one(features, WROWS),
            whole(WROWS, LEN),
            whole(3 * width, 3 * width),
        ],
        out_specs=[
            whole(4, features, 3 * width),
            one(4, ROWS, 3 * width),
            whole(4, WPAD, heads * WPAD),
            whole(4, 2, width),
        ],
        out_shape=[
            jax.ShapeDtypeStruct((4, features, 3 * width), f32),
            jax.ShapeDtypeStruct((images, 4, ROWS, 3 * width), bf16),
            jax.ShapeDtypeStruct((4, WPAD, heads * WPAD), f32),
            jax.ShapeDtypeStruct((4, 2, width), f32),
        ],
        compiler_params=params(),
        name="attn_backward",
    )(probs, qkv, gctx, sht, pick, order)

    grad_part, small_i = pl.pallas_call(
        input_backward,
        grid_spec=pltpu.PrefetchScalarGridSpec(
            num_scalar_prefetch=1,
            grid=(images,),
            in_specs=[
                tok_one,
                pl.BlockSpec((ROWS, features), lambda i, t: (i, 0)),
                one(4, ROWS, 3 * width),
            ]
            + [whole(features, 3 * width)] * 4
            + [whole(6, features)],
            out_specs=[one(length, features), whole(8, features)],
            scratch_shapes=[pltpu.VMEM((4, features, 3 * width), bf16)],
        ),
        out_shape=[
            jax.ShapeDtypeStruct((images, length, features), f32),
            jax.ShapeDtypeStruct((8, features), f32),
        ],
        compiler_params=params(),
        name="input_backward",
    )(t_arr, tokens, gmid, plow, *w_in, shared_vectors)

    block_out = join_images(t_arr, gather_tensor(block_part), bf16)
    input_grad = join_images(t_arr, gather_tensor(grad_part), f32)

    gb = gbias[:, :WIN2].reshape(4, WIN2, heads, WPAD).transpose(0, 2, 1, 3)
    gtable = lax.dot_general(
        gb.reshape(4 * heads, -1), pick_table, (((1,), (1,)), ((), ())), precision=highest
    ).reshape(4, heads * table_rows)
    shared_rows = jnp.concatenate([small_i[0:2], small_a[0:4]])
    block_small = jnp.concatenate(
        [gtable, ghead.reshape(4, -1), geb.reshape(4, hidden_here)], axis=1
    )
    got = xor_tensor(
        jnp.concatenate([block_small[1], block_small[3], shared_rows.reshape(-1)]), 1
    )
    n_small = block_small.shape[1]
    own_small = block_small[0] + got[:n_small]
    far_small = block_small[2] + got[n_small : 2 * n_small]
    shared_sum = shared_rows.reshape(-1) + got[2 * n_small :]
    got = xor_tensor(jnp.concatenate([far_small, shared_sum]), 2)
    vector = jnp.concatenate([own_small, shared_sum]) + got
    vector = lax.psum(vector, "dp")

    grad_scale = (all_images * length * nd) ** (-0.5)
    at = heads * table_rows
    gradients = {
        "table": vector[:at].reshape(heads, table_rows).T,
        "head": vector[at : at + 2 * width].reshape(2, width),
        "bias": vector[at + 2 * width : n_small],
        "shared": vector[n_small:].reshape(6, features),
    }
    moments = dict(table=moment_table, head=moment_head, bias=moment_bias, shared=moment_shared)
    gradients = {k: v * grad_scale for k, v in gradients.items()}
    states = {
        k: moment_decay * moments[k] + (1.0 - moment_decay) * gradients[k] for k in gradients
    }

    own = scatter_tensor(
        [jnp.concatenate([grads_i[k], grads_a[k]], axis=1) for k in range(4)]
    )
    grad_piece = scatter_dp(own) * grad_scale
    piece = features // nd
    row_at = me_d * piece
    moment_piece = jnp.concatenate(
        [
            lax.dynamic_slice_in_dim(moment_input, row_at, piece, 0),
            lax.dynamic_slice_in_dim(moment_output, row_at, piece, 1).T,
            lax.dynamic_slice_in_dim(moment_expand, row_at, piece, 0),
            lax.dynamic_slice_in_dim(moment_reduce, row_at, piece, 1).T,
        ],
        axis=1,
    )
    state_piece = moment_decay * moment_piece + (1.0 - moment_decay) * grad_piece
    state = gather_dp(state_piece)
    ends = np.cumsum([0, 3 * width, width, hidden_here, hidden_here])
    cuts = [(int(a), int(b)) for a, b in zip(ends[:-1], ends[1:])]
    grams = pl.pallas_call(
        functools.partial(gram_kernel, cuts),
        in_specs=[VMEM],
        out_specs=VMEM,
        out_shape=jax.ShapeDtypeStruct((4, features, features), f32),
        compiler_params=params(),
        name="gram",
    )(state)
    gram = scatter_tensor(
        [lax.dynamic_index_in_dim(grams, me_t ^ k, 0, keepdims=False) for k in range(4)]
    )
    poly = pl.pallas_call(
        newton_schulz,
        in_specs=[VMEM],
        out_specs=VMEM,
        out_shape=jax.ShapeDtypeStruct((features, features), f32),
        scratch_shapes=[pltpu.VMEM((features, features), f32)] * 2,
        compiler_params=params(),
        name="newton_schulz",
    )(gram)
    poly_rows = jnp.stack(gather_tensor(lax.dynamic_slice_in_dim(poly, row_at, piece, 0)))
    poly_rows = jnp.stack(
        [lax.dynamic_index_in_dim(poly_rows, me_t ^ m, 0, keepdims=False) for m in range(4)]
    )
    shapes = [
        (features, 3 * width * nt_axis),
        (width * nt_axis, features),
        (features, hidden_here * nt_axis),
        (hidden_here * nt_axis, features),
    ]
    factors = [math.sqrt(max(1.0, a / b)) for a, b in shapes]
    update = pl.pallas_call(
        functools.partial(final_kernel, cuts, factors),
        in_specs=[VMEM, VMEM],
        out_specs=VMEM,
        out_shape=jax.ShapeDtypeStruct((piece, ends[-1]), f32),
        compiler_params=params(),
        name="update",
    )(poly_rows, state)

    def split(values):
        a, b, c, d = [values[:, s:e] for s, e in cuts]
        return a, b.T, c, d.T

    grad_m = split(grad_piece)
    state_m = split(state_piece)
    update_m = split(update)
    return (
        block_out,
        input_grad,
        gradients["shared"],
        grad_m[0],
        gradients["head"],
        grad_m[1],
        grad_m[2],
        gradients["bias"],
        grad_m[3],
        gradients["table"],
        -vector_rate * states["shared"],
        update_m[0],
        -vector_rate * states["head"],
        update_m[1],
        update_m[2],
        -vector_rate * states["bias"],
        update_m[3],
        -vector_rate * states["table"],
        states["shared"],
        state_m[0],
        states["head"],
        state_m[1],
        state_m[2],
        states["bias"],
        state_m[3],
        states["table"],
    )


def solution(mesh):
    return jax.shard_map(
        local,
        mesh=mesh,
        in_specs=(
            P("dp", None, None),
            P("dp", None, None),
            P(),
            P(),
            P(),
            P(None, "tensor"),
            P(None, "tensor"),
            P("tensor", None),
            P(None, "tensor"),
            P("tensor"),
            P("tensor", None),
            P(None, "tensor"),
            P(),
            P(None, "tensor"),
            P(None, "tensor"),
            P("tensor", None),
            P(None, "tensor"),
            P("tensor"),
            P("tensor", None),
            P(None, "tensor"),
        ),
        out_specs=(
            P("dp", None, None),
            P("dp", None, None),
            P(),
            P("dp", "tensor"),
            P(None, "tensor"),
            P("tensor", "dp"),
            P("dp", "tensor"),
            P("tensor"),
            P("tensor", "dp"),
            P(None, "tensor"),
            P(),
            P("dp", "tensor"),
            P(None, "tensor"),
            P("tensor", "dp"),
            P("dp", "tensor"),
            P("tensor"),
            P("tensor", "dp"),
            P(None, "tensor"),
            P(),
            P("dp", "tensor"),
            P(None, "tensor"),
            P("tensor", "dp"),
            P("dp", "tensor"),
            P("tensor"),
            P("tensor", "dp"),
            P(None, "tensor"),
        ),
        check_vma=False,
    )
```

```python
import functools
import math

import jax
import jax.numpy as jnp
import numpy as np
from jax import lax
from jax.experimental import pallas as pl
from jax.experimental.pallas import tpu as pltpu
from jax.sharding import PartitionSpec as P

SIDE = 14
WIN = 7
SHIFT = 3
NS_STEPS = 5
WIN2 = WIN * WIN
LEN = SIDE * SIDE
TABLE = (2 * WIN - 1) ** 2
ROWS = 208
WPAD = 64
WROWS = 4 * WPAD

highest = lax.Precision.HIGHEST
norm_epsilon = 1e-05
moment_decay = 0.8
matrix_rate = 1.0
vector_rate = 1.0
quintic_coef = (3.4445, -4.775, 2.0315)
masked_logit = -1e30
f32 = jnp.float32
bf16 = jnp.bfloat16
VMEM = pl.BlockSpec(memory_space=pltpu.VMEM)
light = pl.CostEstimate(flops=1000, bytes_accessed=1000, transcendentals=0)


def params(limit_mib=56, **kw):
    return pltpu.CompilerParams(vmem_limit_bytes=limit_mib * 1024 * 1024, **kw)


def nn(a, b, **kw):
    return lax.dot_general(a, b, (((1,), (0,)), ((), ())), preferred_element_type=f32, **kw)


def nt(a, b, **kw):
    return lax.dot_general(a, b, (((1,), (1,)), ((), ())), preferred_element_type=f32, **kw)


def tn(a, b, **kw):
    return lax.dot_general(a, b, (((0,), (0,)), ((), ())), preferred_element_type=f32, **kw)


def window_tables():
    pick = np.zeros((WROWS, LEN), np.float32)
    place = np.zeros((4, WIN2), np.int32)
    for r in range(SIDE):
        for c in range(SIDE):
            w = (r // WIN) * 2 + c // WIN
            i = (r % WIN) * WIN + c % WIN
            source = ((r + SHIFT) % SIDE) * SIDE + (c + SHIFT) % SIDE
            pick[w * WPAD + i, source] = 1.0
            place[w, i] = r * SIDE + c
    return pick, place


def column_order(heads, size):
    width = 3 * heads * size
    order = np.zeros((width, width), np.float32)
    for h in range(heads):
        for part in range(3):
            for e in range(size):
                order[(h * 3 + part) * size + e, part * heads * size + h * size + e] = 1.0
    return order


def norm_parts(x):
    centred = x - jnp.mean(x, axis=-1, keepdims=True)
    scale = lax.rsqrt(jnp.mean(centred * centred, axis=-1, keepdims=True) + norm_epsilon)
    return centred * scale, scale


def norm_back(n, scale, gain, u):
    w = u * gain
    return scale * (
        w - jnp.mean(w, axis=-1, keepdims=True) - n * jnp.mean(w * n, axis=-1, keepdims=True)
    )


def head_blocks(x, masks):
    return jnp.concatenate([x * m for m in masks], axis=0)


def head_diag(r, masks):
    rows = r.shape[0] // 4
    out = r[0:rows] * masks[0]
    for h in range(1, 4):
        out = out + r[h * rows : (h + 1) * rows] * masks[h]
    return out


def head_masks(dtype):
    lane = lax.broadcasted_iota(jnp.int32, (1, 128), 1) // 32
    return [jnp.where(lane == h, 1.0, 0.0).astype(dtype) for h in range(4)]


def row_place(index, count):
    group = index // 2
    quarter = count // 4
    return (group // quarter) * (2 * quarter) + (index % 2) * quarter + group % quarter


def store_rows(ref, values, me, count, at=None):
    piece = values.shape[0] // count
    for p in range(count):
        place = pl.multiple_of(row_place(p ^ me, count) * piece, piece)
        block = values[p * piece : (p + 1) * piece]
        if at is None:
            ref[pl.ds(place, piece)] = block
        else:
            ref[at, pl.ds(place, piece)] = block


def bias_kernel(k0, k1, k2, k3, expand, rel, region, bias_ref, mask_ref, rows_s):
    size = rel.shape[1]
    tables = jnp.concatenate([k[0:4, 0:256] for k in (k0, k1, k2, k3)], axis=0)
    rows_s[...] = tn(tables, expand[...], precision=highest)
    index = rel[...]
    for k in range(4):
        def body(n, acc):
            return jnp.where(index == n, rows_s[pl.ds(n, 1), k * size : (k + 1) * size], acc)

        bias_ref[k] = lax.fori_loop(0, TABLE, body, jnp.zeros(index.shape, f32))
    row = lax.broadcasted_iota(jnp.int32, index.shape, 0)
    col = lax.broadcasted_iota(jnp.int32, index.shape, 1) % WPAD
    for w in range(4):
        same = region[w] == region[4 + w]
        ok = (row < WIN2) & ((col >= WIN2) | same)
        mask_ref[w] = jnp.where(ok, 0.0, masked_logit)


def attn_forward(scale, count, t_ref, tok, w0, w1, w2, w3, k0, k1, k2, k3, sv, bias, mask, pick, order, p_out,
                 qkv_out, sht_out, ctx_out, wcol):
    @pl.when(pl.program_id(0) == 0)
    def _():
        for k, w in enumerate((w0, w1, w2, w3)):
            wcol[k] = nn(w[...].astype(bf16), order[...]).astype(bf16)

    n, _ = norm_parts(tok[0].astype(f32))
    normed = (n * sv[0:1] + sv[1:2]).astype(bf16)
    shifted_f = nn(pick[...], normed)
    shifted = shifted_f.astype(bf16)
    store_rows(sht_out, shifted_f.T.astype(bf16), t_ref[1], count, 0)
    low_masks = head_masks(bf16)
    masks = head_masks(f32)
    for k in range(4):
        proj = nn(shifted, wcol[k])
        pack = (k0, k1, k2, k3)[k]
        q = ((proj[:, 0:128] + pack[4:5, 0:128]) * scale).astype(bf16)
        kk = proj[:, 128:256].astype(bf16)
        v = (proj[:, 256:384] + pack[4:5, 128:256]).astype(bf16)
        qkv_out[0, k, :, 0:128] = q
        qkv_out[0, k, :, 128:256] = kk
        qkv_out[0, k, :, 256:384] = v
        windows = []
        for w in range(4):
            rows = slice(w * WPAD, (w + 1) * WPAD)
            logits = nt(kk[rows], head_blocks(q[rows], low_masks)) + (bias[k] + mask[w])
            e = jnp.exp(logits - jnp.max(logits, axis=0, keepdims=True))
            p = e * (1.0 / jnp.sum(e, axis=0, keepdims=True))
            p_out[0, k, w] = p
            windows.append(head_diag(tn(p.astype(bf16), v[rows]), masks).astype(bf16))
        ctx = jnp.concatenate(windows, axis=0)
        ctx_out[0, 0:LEN, k * 128 : (k + 1) * 128] = tn(pick[...], ctx).astype(bf16)
        ctx_out[0, LEN:ROWS, k * 128 : (k + 1) * 128] = jnp.zeros((ROWS - LEN, 128), bf16)


def hidden_blocks(we, wr, eb, n2_s, n2t_s, cot_s, cott_s, mix_s, gn2_s, grads, geb_ref):
    def body(j, carry):
        hidden = nn(n2_s[...], we[j]) + eb[j]
        cdf = 0.5 * (1.0 + lax.erf(hidden * (1.0 / math.sqrt(2.0))))
        act = (hidden * cdf).astype(bf16)
        slope = cdf + hidden * jnp.exp(-0.5 * hidden * hidden) * (1.0 / math.sqrt(2.0 * math.pi))
        mix_s[...] += nn(act, wr[j])
        g_hidden = nt(cot_s[...], wr[j]) * slope
        geb_ref[j] = jnp.sum(g_hidden, axis=0, keepdims=True)
        low = g_hidden.astype(bf16)
        gn2_s[...] += nt(low, we[j])
        at = pl.multiple_of(lax.rem(j, 2) * 256, 256)
        g_exp = nn(n2t_s[...], low)
        g_red = nn(cott_s[...], act)
        for k in range(2):
            @pl.when(j // 2 == k)
            def _(k=k):
                grads[k][:, pl.ds(at, 256)] = g_exp
                grads[k][:, pl.ds(512 + at, 256)] = g_red
        return carry

    lax.fori_loop(0, 4, body, 0)


def load_bias(eb, packs):
    for k, pack in enumerate(packs):
        for half in range(2):
            eb[2 * k + half] = pack[5:6, half * 256 : (half + 1) * 256]


def load_hidden(we, wr, blocks):
    for k, (e, r) in enumerate(blocks):
        for half in range(2):
            we[2 * k + half] = e[:, half * 256 : (half + 1) * 256].astype(bf16)
            wr[2 * k + half] = r[half * 256 : (half + 1) * 256].astype(bf16)


def feed_first(images, count, t_ref, ctx, tok, cot, o0, o1, o2, o3, e0, e1, r0, r1, k0, k1, sv,
               wo, mid_s, n2_s, n2t_s, cot_s, cott_s, mix_s, gn2_s, keep_ref, send_ref, geb_ref,
               we, wr, eb, x_s):
    rows = x_s.shape[0]
    x_s[...] = jnp.zeros_like(x_s)
    for i in range(images):
        x_s[i * ROWS : i * ROWS + LEN] = tok[i].astype(f32)
    for k, o in enumerate((o0, o1, o2, o3)):
        wo[k * 128 : (k + 1) * 128] = o[...].astype(bf16)
    load_bias(eb, (k0, k1))
    load_hidden(we, wr, ((e0, r0), (e1, r1)))
    attended = jnp.concatenate(
        [ctx[...].reshape(images * ROWS, 512), jnp.zeros((rows - images * ROWS, 512), bf16)], axis=0
    )
    mid_s[...] = x_s[...] + nn(attended, wo[...]) + sv[2:3]
    n2, _ = norm_parts(mid_s[...])
    n2f = n2 * sv[3:4] + sv[4:5]
    n2_s[...] = n2f.astype(bf16)
    store_rows(n2t_s, n2f.T.astype(bf16), t_ref[1], count)
    x_s[...] = jnp.zeros_like(x_s)
    for i in range(images):
        x_s[i * ROWS : i * ROWS + LEN] = cot[i].astype(f32)
    cot_s[...] = x_s[...].astype(bf16)
    store_rows(cott_s, x_s[...].T.astype(bf16), t_ref[1], count)
    mix_s[...] = jnp.zeros_like(mix_s)
    gn2_s[...] = jnp.zeros_like(gn2_s)
    hidden_blocks(we, wr, eb, n2_s, n2t_s, cot_s, cott_s, mix_s, gn2_s, (keep_ref, send_ref), geb_ref)


def feed_second(images, count, t_ref, ctx, e2, e3, f2, f3, r2, r3, k2, k3, sv, wo, mid_s, n2_s, n2t_s, cot_s,
                cott_s, mix_in, gn2_in, out_ref, gmid_ref, gctx_ref, keep_ref, send_ref, keep_o,
                send_o, geb_ref, small_ref, we, wr, eb, mix_s, gn2_s, att_t):
    rows = mid_s.shape[0]
    load_bias(eb, (k2, k3))
    for k, (e, f, r) in enumerate(((e2, f2, r2), (e3, f3, r3))):
        we[2 * k + t_ref[2]] = e[...].astype(bf16)
        we[2 * k + 1 - t_ref[2]] = f[...].astype(bf16)
        for half in range(2):
            wr[2 * k + half] = r[half * 256 : (half + 1) * 256].astype(bf16)
    mix_s[...] = mix_in[...]
    gn2_s[...] = gn2_in[...]
    hidden_blocks(we, wr, eb, n2_s, n2t_s, cot_s, cott_s, mix_s, gn2_s, (keep_ref, send_ref), geb_ref)
    result = mid_s[...] + mix_s[...] + sv[5:6]
    for i in range(images):
        out_ref[i] = result[i * ROWS : i * ROWS + LEN].astype(bf16).astype(f32)
    n2, scale2 = norm_parts(mid_s[...])
    u = gn2_s[...]
    cot = cot_s[...].astype(f32)
    gmid = cot + norm_back(n2, scale2, sv[3:4], u)
    gmid_ref[...] = gmid
    small_ref[0:1] = jnp.sum(gmid, axis=0, keepdims=True)
    small_ref[1:2] = jnp.sum(u * n2, axis=0, keepdims=True)
    small_ref[2:3] = jnp.sum(u, axis=0, keepdims=True)
    small_ref[3:4] = jnp.sum(cot, axis=0, keepdims=True)
    small_ref[4:8] = jnp.zeros((4, 512), f32)
    att_low = gmid.astype(bf16)
    gctx_ref[...] = nt(att_low, wo[...]).astype(bf16)[0 : images * ROWS].reshape(images, ROWS, 512)
    store_rows(att_t, gmid.T.astype(bf16), t_ref[1], count)
    attended = jnp.concatenate(
        [ctx[...].reshape(images * ROWS, 512), jnp.zeros((rows - images * ROWS, 512), bf16)], axis=0
    )
    g_out = nn(att_t[...], attended)
    for k in range(4):
        (keep_o, send_o)[k % 2][k // 2] = g_out[:, k * 128 : (k + 1) * 128]


def attn_backward(scale, p_in, qkv, gctx, sht, pick, order, keep_ref, send_ref, plow_ref, gbias_ref,
                  ghead_ref):
    @pl.when(pl.program_id(0) == 0)
    def _():
        keep_ref[...] = jnp.zeros_like(keep_ref)
        send_ref[...] = jnp.zeros_like(send_ref)
        gbias_ref[...] = jnp.zeros_like(gbias_ref)
        ghead_ref[...] = jnp.zeros_like(ghead_ref)

    gwin = nn(pick[...], gctx[0, 0:LEN]).astype(bf16)
    low_masks = head_masks(bf16)
    masks = head_masks(f32)
    for k in range(4):
        q = qkv[0, k, :, 0:128]
        kk = qkv[0, k, :, 128:256]
        v = qkv[0, k, :, 256:384]
        parts = []
        bias_sum = None
        q_sum = None
        v_sum = None
        for w in range(4):
            rows = slice(w * WPAD, (w + 1) * WPAD)
            gbd = head_blocks(gwin[rows, k * 128 : (k + 1) * 128], low_masks)
            p = p_in[0, k, w]
            gp = nt(v[rows], gbd)
            gl = p * (gp - jnp.sum(p * gp, axis=0, keepdims=True))
            low = gl.astype(bf16)
            gq = head_diag(tn(low, kk[rows]), masks) * scale
            gk = nn(low, head_blocks(q[rows], low_masks))
            gv = nn(p.astype(bf16), gbd)
            bias_sum = gl if w == 0 else bias_sum + gl
            sq = jnp.sum(gq, axis=0, keepdims=True)
            sv_ = jnp.sum(gv, axis=0, keepdims=True)
            q_sum = sq if w == 0 else q_sum + sq
            v_sum = sv_ if w == 0 else v_sum + sv_
            parts.append(jnp.concatenate([gq, gk, gv], axis=1).astype(bf16))
        gbias_ref[k] += bias_sum
        ghead_ref[k, 0:1] += q_sum
        ghead_ref[k, 1:2] += v_sum
        plow = nt(jnp.concatenate(parts, axis=0), order[...]).astype(bf16)
        (keep_ref, send_ref)[k % 2][k // 2] += nn(sht[0], plow)
        plow_ref[0, k, 0:LEN] = tn(pick[...], plow).astype(bf16)
        plow_ref[0, k, LEN:ROWS] = jnp.zeros((ROWS - LEN, plow.shape[1]), bf16)


def input_backward(t_ref, tok, gmid, plow, w0, w1, w2, w3, sv, out_ref, small_ref, wlow):
    @pl.when(pl.program_id(0) == 0)
    def _():
        small_ref[...] = jnp.zeros_like(small_ref)
        for k, w in enumerate((w0, w1, w2, w3)):
            wlow[k] = w[...].astype(bf16)

    u = nt(plow[0, 0], wlow[0])
    for k in range(1, 4):
        u = u + nt(plow[0, k], wlow[k])
    u = u[0:LEN]
    n, scale = norm_parts(tok[0].astype(f32))
    small_ref[0:1] += jnp.sum(u * n, axis=0, keepdims=True)
    small_ref[1:2] += jnp.sum(u, axis=0, keepdims=True)
    out_ref[0] = gmid[0:LEN] + norm_back(n, scale, sv[0:1], u)


def assemble(t_ref, a0, a1, a2, a3, out):
    for k, a in enumerate((a0, a1, a2, a3)):
        @pl.when(pl.program_id(0) == k)
        def _(a=a):
            out[...] = a[...].astype(out.dtype)


def gram_kernel(places, t_ref, same_a, other_a, same_i, other_i, keep_ref, send_ref):
    for m, (group, start, stop) in enumerate(places):
        a = (same_i, same_a)[group][:, start:stop]
        b = (other_i, other_a)[group][:, start:stop]
        half = a.shape[0]
        k = m ^ t_ref[0]
        blocks = (
            nt(a, a, precision=highest),
            nt(a, b, precision=highest),
            nt(b, b, precision=highest),
        )
        for parity, ref in enumerate((keep_ref, send_ref)):
            @pl.when(k % 2 == parity)
            def _(ref=ref):
                for n, block in enumerate(blocks):
                    ref[k // 2, :, n * half : (n + 1) * half] = block


def split_low(x, parts):
    out = []
    for _ in range(parts):
        low = x.astype(bf16)
        out.append(low)
        x = x - low.astype(f32)
    return out


def spread_product(left, right, terms):
    total = None
    for i, j in terms:
        part = nn(left[i], right[j])
        total = part if total is None else total + part
    return total


def symmetric_product(out, left, right, terms):
    half = out.shape[0] // 2
    top = [x[:half] for x in left]
    bottom = [x[half:] for x in left]
    first = [x[:, :half] for x in right]
    second = [x[:, half:] for x in right]
    out[:half, :half] = spread_product(top, first, terms)
    cross = spread_product(top, second, terms)
    out[:half, half:] = cross
    out[half:, :half] = cross.T
    out[half:, half:] = spread_product(bottom, second, terms)


three_terms = ((1, 0), (0, 1), (0, 0))
six_terms = ((2, 0), (0, 2), (1, 1)) + three_terms


def newton_schulz(g0, g1, g2, rows_ref, a_s, p_s, t_s, q_s):
    g = g0[0] + g1[0] + g2[...]
    half = g.shape[0]
    size = 2 * half
    cross = g[:, half:size]
    a_s[:half, :half] = g[:, :half]
    a_s[:half, half:] = cross
    a_s[half:, :half] = cross.T
    a_s[half:, half:] = g[:, size:]
    row = lax.broadcasted_iota(jnp.int32, (size, size), 0)
    col = lax.broadcasted_iota(jnp.int32, (size, size), 1)
    eye = jnp.where(row == col, 1.0, 0.0)
    whole = a_s[...]
    inv = 1.0 / (jnp.sum(jnp.sum(whole * eye, axis=0, keepdims=True), axis=1, keepdims=True) + 1e-07)
    a_s[...] = whole * inv
    c0, c1, c2 = quintic_coef
    for step in range(NS_STEPS):
        exact = step < 3
        terms = six_terms if exact else three_terms
        parts = split_low(a_s[...], 3 if exact else 2)
        symmetric_product(t_s, parts, parts, terms)
        p_s[...] = c0 * eye + c1 * a_s[...] + c2 * t_s[...]
        poly = split_low(p_s[...], 3 if exact else 2)
        if step == 0:
            q_s[...] = p_s[...]
        else:
            symmetric_product(q_s, poly, split_low(q_s[...], 2), three_terms)
        if step < NS_STEPS - 1:
            symmetric_product(t_s, poly, parts, terms)
            symmetric_product(a_s, poly, split_low(t_s[...], 3 if exact else 2), terms)
    rows_ref[...] = q_s[0 : rows_ref.shape[0]] * jnp.sqrt(inv)


def final_kernel(places, factors, t_ref, q0, q1, q2, q3, same_a, other_a, same_i, other_i, u_in,
                 u_exp, u_red, u_out, q_s):
    for k, q in enumerate((q0, q1, q2, q3)):
        q_s[t_ref[0] ^ k] = q[...]
    for m, (group, start, stop) in enumerate(places):
        same = (same_i, same_a)[group][:, start:stop]
        other = (other_i, other_a)[group][:, start:stop]
        half = same.shape[0]
        u = (-matrix_rate * factors[m]) * (
            nn(q_s[m, :, 0:half], same, precision=highest)
            + nn(q_s[m, :, half:], other, precision=highest)
        )
        ref = (u_in, u_exp, u_red, u_out)[m]
        ref[...] = u if m < 2 else u.T


def after(value, *earlier):
    return lax.optimization_barrier((value, *earlier))[0]


def xor_tensor(x, k):
    return lax.ppermute(x, "tensor", [(i, i ^ k) for i in range(lax.axis_size("tensor"))])


def xor_dp(x, k):
    return lax.ppermute(x, "dp", [(i, i ^ k) for i in range(lax.axis_size("dp"))])


def gather_tensor(block, *earlier, late=None):
    near = xor_tensor(block, 1)
    far = xor_tensor(after(block, *earlier) if earlier else block, 2)
    return [block, near, far, xor_tensor(far if late is None else after(far, late), 1)]


def scatter_tensor(blocks):
    got = xor_tensor(jnp.stack([blocks[1], blocks[3]]), 1)
    own = blocks[0] + got[0]
    far = blocks[2] + got[1]
    return own + xor_tensor(far, 2)


def first_stage(own, far):
    half, quarter = own.shape[0] // 2, own.shape[0] // 4
    return far[:half], jnp.stack([own[half + quarter :], far[half + quarter :]])


def second_stage(own, far, got_t, got_d):
    half, quarter = own.shape[0] // 2, own.shape[0] // 4
    own_a = own[:half] + got_t
    return far[half : half + quarter] + got_d[1], own_a[quarter:], own_a[:quarter]


def third_stage(own, keep, got_d, last_t, last_d):
    half, quarter = own.shape[0] // 2, own.shape[0] // 4
    piece = own.shape[0] // lax.axis_size("dp")
    sum_a = keep + last_d
    sum_b = own[half : half + quarter] + got_d[0] + last_t
    pieces = [sum_a[i : i + piece] for i in range(0, quarter, piece)]
    return pieces + [sum_b[i : i + piece] for i in range(0, quarter, piece)]


def send_groups(pieces):
    return [xor_dp(p, 2 * g) for g, p in enumerate(pieces) if g > 0]


def barrier(*values):
    return lax.optimization_barrier(values)


def join_images(t, parts, dtype):
    images, length, features = parts[0].shape
    return pl.pallas_call(
        assemble,
        grid_spec=pltpu.PrefetchScalarGridSpec(
            num_scalar_prefetch=1,
            grid=(4,),
            in_specs=[pl.BlockSpec((images, length, features), lambda a, t_ref: (0, 0, 0))] * 4,
            out_specs=pl.BlockSpec(
                (images, length, features), lambda a, t_ref: (t_ref[0] ^ a, 0, 0)
            ),
        ),
        out_shape=jax.ShapeDtypeStruct((4 * images, length, features), dtype),
        compiler_params=params(),
        cost_estimate=light,
        name="join_images",
    )(t, *parts)


def local(
    tokens,
    cotangent,
    region_ids,
    relative_index,
    shared_vectors,
    input_weight,
    head_bias,
    output_weight,
    expand_weight,
    expand_bias,
    reduce_weight,
    bias_table,
    moment_shared,
    moment_input,
    moment_head,
    moment_output,
    moment_expand,
    moment_bias,
    moment_reduce,
    moment_table,
):
    nt_axis = lax.axis_size("tensor")
    me_t = lax.axis_index("tensor")
    me_d = lax.axis_index("dp")
    nd = lax.axis_size("dp")
    all_images, length, features = tokens.shape
    images = all_images // nt_axis
    heads = bias_table.shape[1]
    head_size = head_bias.shape[1] // heads
    width = heads * head_size
    hidden_here = expand_weight.shape[1]
    table_rows = bias_table.shape[0]
    query_scale = head_size ** (-0.5)
    low_d = me_d % 2
    t_arr = jnp.stack([me_t, me_d, low_d]).astype(jnp.int32)
    rows = -(-images * ROWS // 128) * 128
    lanes = heads * WPAD

    pad_lanes = lambda x: jnp.pad(x, ((0, 0), (0, features - x.shape[1])))
    pack = jnp.concatenate(
        [
            pad_lanes(bias_table.T),
            pad_lanes(head_bias.reshape(1, 2 * width)),
            pad_lanes(expand_bias.reshape(1, hidden_here)),
            jnp.zeros((2, features), f32),
        ]
    )
    near_pack = xor_tensor(pack, 1)
    far_pack = xor_tensor(pack, 2)
    packs = [pack, near_pack, far_pack, xor_tensor(near_pack, 2)]
    far_source = after(input_weight, near_pack)
    w_in = [input_weight, xor_tensor(input_weight, 1), xor_tensor(far_source, 2)]
    w_in.append(xor_tensor(w_in[2], 1))
    w_out = [output_weight, xor_tensor(output_weight, 1)]
    w_out.append(xor_tensor(after(output_weight, far_pack), 2))
    w_exp = [expand_weight, xor_tensor(expand_weight, 1)]
    w_red = [reduce_weight, xor_tensor(reduce_weight, 1)]
    half_exp = lax.dynamic_slice_in_dim(expand_weight, low_d * (hidden_here // 2), hidden_here // 2, 1)
    mine_exp = xor_tensor(after(half_exp, w_in[2]), 2)
    far_red = xor_tensor(after(reduce_weight, w_in[2]), 2)

    pick_np, place_np = window_tables()
    pick = jnp.asarray(pick_np, bf16)
    order = jnp.asarray(column_order(heads, head_size), bf16)
    rel_t = jnp.pad(relative_index.T, ((0, WPAD - WIN2), (0, WPAD - WIN2)), constant_values=-1)
    rel_wide = jnp.tile(rel_t, (1, heads))
    region = region_ids.reshape(2, WIN, 2, WIN).transpose(0, 2, 1, 3).reshape(4, WIN2)
    region = jnp.pad(region, ((0, 0), (0, WPAD - WIN2)))
    region_both = jnp.concatenate(
        [
            jnp.broadcast_to(region[:, :, None], (4, WPAD, lanes)),
            jnp.broadcast_to(jnp.tile(region, (1, heads))[:, None, :], (4, WPAD, lanes)),
        ]
    )
    spread = np.zeros((4 * heads, 4 * lanes), np.float32)
    for h in range(4 * heads):
        spread[h, h * WPAD : (h + 1) * WPAD] = 1.0
    bias, mask = pl.pallas_call(
        bias_kernel,
        in_specs=[VMEM] * 7,
        out_specs=[VMEM] * 2,
        out_shape=[jax.ShapeDtypeStruct((4, WPAD, lanes), f32)] * 2,
        scratch_shapes=[pltpu.VMEM((256, 4 * lanes), f32)],
        compiler_params=params(),
        cost_estimate=light,
        name="bias",
    )(*packs, jnp.asarray(spread), rel_wide, region_both)
    piece = features // nd
    row_at = me_d * piece
    moment_a = jnp.concatenate(
        [
            lax.dynamic_slice_in_dim(moment_expand, row_at, piece, 0),
            lax.dynamic_slice_in_dim(moment_reduce, row_at, piece, 1).T,
            lax.dynamic_slice_in_dim(moment_output, row_at, piece, 1).T,
        ],
        axis=1,
    )
    moment_i = lax.dynamic_slice_in_dim(moment_input, row_at, piece, 0)
    bias, mask, moment_a, moment_i = barrier(bias, mask, moment_a, moment_i)
    w_in[3] = barrier(w_in[3], bias)[0]

    whole = lambda *shape: pl.BlockSpec(shape, lambda i, *_: (0,) * len(shape))
    one = lambda *shape: pl.BlockSpec((1,) + shape, lambda i, *_: (i,) + (0,) * len(shape))
    tok_one = pl.BlockSpec((1, length, features), lambda i, t: (t[0] * images + i, 0, 0))
    sds = jax.ShapeDtypeStruct

    probs, qkv, sht, ctx = pl.pallas_call(
        functools.partial(attn_forward, query_scale, nd),
        grid_spec=pltpu.PrefetchScalarGridSpec(
            num_scalar_prefetch=1,
            grid=(images,),
            in_specs=[tok_one]
            + [whole(features, 3 * width)] * 4
            + [whole(8, features)] * 4
            + [
                whole(6, features),
                whole(4, WPAD, lanes),
                whole(4, WPAD, lanes),
                whole(WROWS, LEN),
                whole(3 * width, 3 * width),
            ],
            out_specs=[
                one(4, 4, WPAD, lanes),
                one(4, WROWS, 3 * width),
                one(features, WROWS),
                one(ROWS, 4 * width),
            ],
            scratch_shapes=[pltpu.VMEM((4, features, 3 * width), bf16)],
        ),
        out_shape=[
            sds((images, 4, 4, WPAD, lanes), f32),
            sds((images, 4, WROWS, 3 * width), bf16),
            sds((images, features, WROWS), bf16),
            sds((images, ROWS, 4 * width), bf16),
        ],
        compiler_params=params(),
        cost_estimate=light,
        name="attn_forward",
    )(t_arr, tokens, *w_in, *packs, shared_vectors, bias, mask, pick, order)

    w_out[2] = after(w_out[2], ctx)
    w_out.append(xor_tensor(w_out[2], 1))
    mine_exp = after(mine_exp, ctx)
    other_exp = xor_dp(mine_exp, 1)
    mine_last = xor_tensor(mine_exp, 1)
    tok_all = pl.BlockSpec((images, length, features), lambda i, t: (t[0], 0, 0))
    token_f = (rows, features)
    wide = 2 * hidden_here
    hidden_scratch = [
        pltpu.VMEM((4, features, hidden_here // 2), bf16),
        pltpu.VMEM((4, hidden_here // 2, features), bf16),
        pltpu.VMEM((4, 1, hidden_here // 2), f32),
    ]
    state_shapes = [
        ((4 * width, features), bf16),
        (token_f, f32),
        (token_f, bf16),
        (token_f[::-1], bf16),
        (token_f, bf16),
        (token_f[::-1], bf16),
        (token_f, f32),
        (token_f, f32),
    ]
    *carry, keep_0, send_1, geb_a = pl.pallas_call(
        functools.partial(feed_first, images, nd),
        grid_spec=pltpu.PrefetchScalarGridSpec(
            num_scalar_prefetch=1,
            grid=(1,),
            in_specs=[whole(images, ROWS, 4 * width), tok_all, tok_all]
            + [whole(width, features)] * 4
            + [whole(features, hidden_here)] * 2
            + [whole(hidden_here, features)] * 2
            + [whole(8, features)] * 2
            + [whole(6, features)],
            out_specs=[whole(*shape) for shape, _ in state_shapes]
            + [whole(features, wide), whole(features, wide), whole(4, 1, hidden_here // 2)],
            scratch_shapes=hidden_scratch + [pltpu.VMEM(token_f, f32)],
        ),
        out_shape=[sds(shape, dtype) for shape, dtype in state_shapes]
        + [sds((features, wide), f32)] * 2
        + [sds((4, 1, hidden_here // 2), f32)],
        compiler_params=params(),
        cost_estimate=light,
        name="feed_first",
    )(t_arr, ctx, tokens, cotangent, *w_out, *w_exp, *w_red, *packs[:2], shared_vectors)

    other_exp = after(other_exp, geb_a)
    other_last = xor_tensor(other_exp, 1)
    far_red = after(far_red, geb_a)
    w_red += [far_red, xor_tensor(far_red, 1)]
    got_1 = xor_tensor(send_1, 1)

    block_part, gmid, gctx, keep_2, send_3, keep_o, send_o, geb_b, small_a = pl.pallas_call(
        functools.partial(feed_second, images, nd),
        grid_spec=pltpu.PrefetchScalarGridSpec(
            num_scalar_prefetch=1,
            grid=(1,),
            in_specs=[whole(images, ROWS, 4 * width)]
            + [whole(features, hidden_here // 2)] * 4
            + [whole(hidden_here, features)] * 2
            + [whole(8, features)] * 2
            + [whole(6, features)]
            + [whole(*shape) for shape, _ in state_shapes],
            out_specs=[
                whole(images, length, features),
                whole(rows, features),
                whole(images, ROWS, 4 * width),
                whole(features, wide),
                whole(features, wide),
                whole(2, features, width),
                whole(2, features, width),
                whole(4, 1, hidden_here // 2),
                whole(8, features),
            ],
            scratch_shapes=hidden_scratch
            + [
                pltpu.VMEM(token_f, f32),
                pltpu.VMEM(token_f, f32),
                pltpu.VMEM(token_f[::-1], bf16),
            ],
        ),
        out_shape=[
            sds((images, length, features), f32),
            sds((rows, features), f32),
            sds((images, ROWS, 4 * width), bf16),
            sds((features, wide), f32),
            sds((features, wide), f32),
            sds((2, features, width), f32),
            sds((2, features, width), f32),
            sds((4, 1, hidden_here // 2), f32),
            sds((8, features), f32),
        ],
        compiler_params=params(),
        cost_estimate=light,
        name="feed_second",
    )(
        t_arr,
        ctx,
        mine_exp,
        mine_last,
        other_exp,
        other_last,
        *w_red[2:],
        *packs[2:],
        shared_vectors,
        *carry,
    )

    got_3 = xor_tensor(send_3, 1)
    got_o = xor_tensor(send_o, 1)
    own_a = jnp.concatenate([keep_0 + got_1, keep_o[0] + got_o[0]], axis=1)
    far_a = jnp.concatenate([keep_2 + got_3, keep_o[1] + got_o[1]], axis=1)
    t1_a, d1_a = first_stage(own_a, far_a)
    gctx, t1_a, d1_a = barrier(gctx, t1_a, d1_a)
    got_t1_a, got_d1_a = xor_tensor(t1_a, 2), xor_dp(d1_a, 1)

    keep_i, send_i, plow, gbias, ghead = pl.pallas_call(
        functools.partial(attn_backward, query_scale),
        grid=(images,),
        in_specs=[
            one(4, 4, WPAD, lanes),
            one(4, WROWS, 3 * width),
            one(ROWS, 4 * width),
            one(features, WROWS),
            whole(WROWS, LEN),
            whole(3 * width, 3 * width),
        ],
        out_specs=[
            whole(2, features, 3 * width),
            whole(2, features, 3 * width),
            one(4, ROWS, 3 * width),
            whole(4, WPAD, lanes),
            whole(4, 2, width),
        ],
        out_shape=[
            sds((2, features, 3 * width), f32),
            sds((2, features, 3 * width), f32),
            sds((images, 4, ROWS, 3 * width), bf16),
            sds((4, WPAD, lanes), f32),
            sds((4, 2, width), f32),
        ],
        compiler_params=params(),
        cost_estimate=light,
        name="attn_backward",
    )(probs, qkv, gctx, sht, pick, order)

    got_i = xor_tensor(send_i, 1)

    grad_part, small_i = pl.pallas_call(
        input_backward,
        grid_spec=pltpu.PrefetchScalarGridSpec(
            num_scalar_prefetch=1,
            grid=(images,),
            in_specs=[
                tok_one,
                pl.BlockSpec((ROWS, features), lambda i, t: (i, 0)),
                one(4, ROWS, 3 * width),
            ]
            + [whole(features, 3 * width)] * 4
            + [whole(6, features)],
            out_specs=[one(length, features), whole(8, features)],
            scratch_shapes=[pltpu.VMEM((4, features, 3 * width), bf16)],
        ),
        out_shape=[sds((images, length, features), f32), sds((8, features), f32)],
        compiler_params=params(),
        cost_estimate=light,
        name="input_backward",
    )(t_arr, tokens, gmid, plow, *w_in, shared_vectors)

    got_t1_a, got_d1_a, send_small_i = barrier(got_t1_a, got_d1_a, small_i)
    small_i = send_small_i
    t2_a, d2_a, kept_a = second_stage(own_a, far_a, got_t1_a, got_d1_a)
    got_t2_a, got_d2_a = xor_tensor(t2_a, 2), xor_dp(d2_a, 1)
    got_i = barrier(got_i, t2_a, d2_a)[0]
    own_i = keep_i[0] + got_i[0]
    far_i = keep_i[1] + got_i[1]
    t1_i, d1_i = first_stage(own_i, far_i)
    got_t1_i, got_d1_i = xor_tensor(t1_i, 2), xor_dp(d1_i, 1)
    gbias, ghead, small_i, geb_a, geb_b, small_a = barrier(
        gbias, ghead, small_i, geb_a, geb_b, small_a, t1_i, d1_i
    )[:6]

    pick_table = (
        jnp.arange(table_rows)[:, None] == rel_t[:WIN2].reshape(1, -1)
    ).astype(f32)
    gb = gbias[:, :WIN2].reshape(4, WIN2, heads, WPAD).transpose(0, 2, 1, 3)
    gtable = lax.dot_general(
        gb.reshape(4 * heads, -1), pick_table, (((1,), (1,)), ((), ())), precision=highest
    ).reshape(4, heads * table_rows)
    shared_rows = jnp.concatenate([small_i[0:2], small_a[0:4]])
    geb = jnp.concatenate([geb_a, geb_b]).reshape(4, hidden_here)
    block_small = jnp.concatenate([gtable, ghead.reshape(4, -1), geb], axis=1)
    n_small = block_small.shape[1]
    small_send = jnp.concatenate([block_small[1], block_small[3], shared_rows.reshape(-1)])
    got_small = xor_tensor(small_send, 1)
    got_t2_a, got_d2_a = barrier(got_t2_a, got_d2_a, small_send)[:2]
    pieces_a = third_stage(own_a, kept_a, got_d1_a, got_t2_a, got_d2_a)
    got_a = send_groups(pieces_a)
    got_t1_i, got_d1_i = barrier(got_t1_i, got_d1_i, *pieces_a)[:2]
    t2_i, d2_i, kept_i = second_stage(own_i, far_i, got_t1_i, got_d1_i)
    got_t2_i, got_d2_i = xor_tensor(t2_i, 2), xor_dp(d2_i, 1)
    got_small = barrier(got_small, t2_i, d2_i)[0]
    own_small = block_small[0] + got_small[:n_small]
    far_small = block_small[2] + got_small[n_small : 2 * n_small]
    shared_sum = shared_rows.reshape(-1) + got_small[2 * n_small :]
    small_send = jnp.concatenate([far_small, shared_sum])
    got_small = xor_tensor(small_send, 2)
    got_t2_i, got_d2_i, block_part = barrier(got_t2_i, got_d2_i, block_part, small_send)[:3]
    block_parts = [block_part, xor_tensor(block_part, 1), xor_tensor(block_part, 2)]
    pieces_i = third_stage(own_i, kept_i, got_d1_i, got_t2_i, got_d2_i)
    got_i = send_groups(pieces_i)
    got_small = barrier(got_small, *pieces_i)[0]
    vector = jnp.concatenate([own_small, shared_sum]) + got_small
    got_small = xor_dp(vector, 1)
    got_a = barrier(*got_a, vector)[: len(got_a)]
    grad_a = sum(got_a, pieces_a[0])
    got_small, grad_a = barrier(got_small, grad_a)
    vector = vector + got_small
    small_parts = send_groups([vector] * (nd // 2))

    grad_scale = (all_images * length * nd) ** (-0.5)
    grad_a = grad_a * grad_scale
    state_a = moment_decay * moment_a + (1.0 - moment_decay) * grad_a
    same_a = [state_a] + send_groups([state_a] * (nd // 2))
    got_i = barrier(*got_i, state_a)[: len(got_i)]
    grad_i = sum(got_i, pieces_i[0]) * grad_scale
    state_i = moment_decay * moment_i + (1.0 - moment_decay) * grad_i
    same_i = [state_i] + send_groups([state_i] * (nd // 2))
    same_a = barrier(*same_a, state_i)[: len(same_a)]
    same_a = jnp.concatenate(same_a)
    other_a = xor_dp(same_a, 1)
    same_i = barrier(*same_i, same_a)[: len(same_i)]
    same_i = jnp.concatenate(same_i)
    other_i = xor_dp(same_i, 1)
    far_block, grad_part = barrier(block_parts[2], grad_part, same_i)[:2]
    block_parts = [block_parts[0], block_parts[1], far_block, xor_tensor(far_block, 1)]
    grad_parts = [grad_part, xor_tensor(grad_part, 1), xor_tensor(grad_part, 2)]
    block_parts[1], block_parts[3] = barrier(block_parts[1], block_parts[3], grad_part)[:2]
    block_out = join_images(t_arr, block_parts, bf16)
    other_a, other_i = barrier(other_a, other_i, block_out)[:2]

    places = [
        (0, 0, 3 * width),
        (1, 0, hidden_here),
        (1, hidden_here, wide),
        (1, wide, wide + width),
    ]
    half = features // 2
    scalars = pl.BlockSpec(memory_space=pltpu.SMEM)
    gram_keep, gram_send = pl.pallas_call(
        functools.partial(gram_kernel, places),
        in_specs=[scalars] + [VMEM] * 4,
        out_specs=[VMEM] * 2,
        out_shape=[sds((2, half, 3 * half), f32)] * 2,
        compiler_params=params(),
        cost_estimate=light,
        name="gram",
    )(t_arr, same_a, other_a, same_i, other_i)
    gram_near = xor_tensor(gram_send, 1)
    gram_send = gram_keep[1] + gram_near[1]
    gram_far = xor_tensor(gram_send, 2)
    grad_far = barrier(grad_parts[2], gram_send)[0]
    input_grad = join_images(
        t_arr, [grad_parts[0], grad_parts[1], grad_far, xor_tensor(grad_far, 1)], f32
    )
    gram_far = barrier(gram_far, input_grad)[0]
    own_rows = pl.pallas_call(
        newton_schulz,
        in_specs=[VMEM] * 3,
        out_specs=VMEM,
        out_shape=sds((piece, features), f32),
        scratch_shapes=[pltpu.VMEM((features, features), f32)] * 4,
        compiler_params=params(),
        cost_estimate=light,
        name="newton_schulz",
    )(gram_keep[:1], gram_near[:1], gram_far)
    near_rows = xor_tensor(own_rows, 1)
    far_rows = xor_tensor(own_rows, 2)
    factor = lambda a, b: math.sqrt(max(1.0, a / b))
    update_m = pl.pallas_call(
        functools.partial(
            final_kernel,
            places,
            [
                factor(features, 3 * width * nt_axis),
                factor(features, hidden_here * nt_axis),
                factor(hidden_here * nt_axis, features),
                factor(width * nt_axis, features),
            ],
        ),
        in_specs=[scalars] + [VMEM] * 8,
        out_specs=[VMEM] * 4,
        out_shape=[
            sds((piece, 3 * width), f32),
            sds((piece, hidden_here), f32),
            sds((hidden_here, piece), f32),
            sds((width, piece), f32),
        ],
        scratch_shapes=[pltpu.VMEM((4, piece, features), f32)],
        compiler_params=params(),
        cost_estimate=light,
        name="update",
    )(
        t_arr,
        own_rows,
        near_rows,
        far_rows,
        xor_tensor(far_rows, 1),
        same_a,
        other_a,
        same_i,
        other_i,
    )
    update_m = (update_m[0], update_m[3], update_m[1], update_m[2])

    for part in barrier(*small_parts, state_i)[: len(small_parts)]:
        vector = vector + part
    at = heads * table_rows
    gradients = {
        "table": vector[:at].reshape(heads, table_rows).T,
        "head": vector[at : at + 2 * width].reshape(2, width),
        "bias": vector[at + 2 * width : n_small],
        "shared": vector[n_small:].reshape(6, features),
    }
    moments = dict(table=moment_table, head=moment_head, bias=moment_bias, shared=moment_shared)
    gradients = {k: v * grad_scale for k, v in gradients.items()}
    states = {
        k: moment_decay * moments[k] + (1.0 - moment_decay) * gradients[k] for k in gradients
    }

    def split(part_i, part_a):
        b, c, d = [part_a[:, s:e] for _, s, e in places[1:]]
        return part_i, d.T, b, c.T

    grad_m = split(grad_i, grad_a)
    state_m = split(state_i, state_a)
    return (
        block_out,
        input_grad,
        gradients["shared"],
        grad_m[0],
        gradients["head"],
        grad_m[1],
        grad_m[2],
        gradients["bias"],
        grad_m[3],
        gradients["table"],
        -vector_rate * states["shared"],
        update_m[0],
        -vector_rate * states["head"],
        update_m[1],
        update_m[2],
        -vector_rate * states["bias"],
        update_m[3],
        -vector_rate * states["table"],
        states["shared"],
        state_m[0],
        states["head"],
        state_m[1],
        state_m[2],
        states["bias"],
        state_m[3],
        states["table"],
    )


def solution(mesh):
    return jax.shard_map(
        local,
        mesh=mesh,
        in_specs=(
            P("dp", None, None),
            P("dp", None, None),
            P(),
            P(),
            P(),
            P(None, "tensor"),
            P(None, "tensor"),
            P("tensor", None),
            P(None, "tensor"),
            P("tensor"),
            P("tensor", None),
            P(None, "tensor"),
            P(),
            P(None, "tensor"),
            P(None, "tensor"),
            P("tensor", None),
            P(None, "tensor"),
            P("tensor"),
            P("tensor", None),
            P(None, "tensor"),
        ),
        out_specs=(
            P("dp", None, None),
            P("dp", None, None),
            P(),
            P("dp", "tensor"),
            P(None, "tensor"),
            P("tensor", "dp"),
            P("dp", "tensor"),
            P("tensor"),
            P("tensor", "dp"),
            P(None, "tensor"),
            P(),
            P("dp", "tensor"),
            P(None, "tensor"),
            P("tensor", "dp"),
            P("dp", "tensor"),
            P("tensor"),
            P("tensor", "dp"),
            P(None, "tensor"),
            P(),
            P("dp", "tensor"),
            P(None, "tensor"),
            P("tensor", "dp"),
            P("dp", "tensor"),
            P("tensor"),
            P("tensor", "dp"),
            P(None, "tensor"),
        ),
        check_vma=False,
    )
```

```python
import functools
import math

import jax
import jax.numpy as jnp
import numpy as np
from jax import lax
from jax.experimental import pallas as pl
from jax.experimental.pallas import tpu as pltpu
from jax.sharding import PartitionSpec as P

SIDE = 14
WIN = 7
SHIFT = 3
NS_STEPS = 5
WIN2 = WIN * WIN
LEN = SIDE * SIDE
TABLE = (2 * WIN - 1) ** 2
ROWS = 208
WPAD = 64
WROWS = 4 * WPAD

highest = lax.Precision.HIGHEST
norm_epsilon = 1e-05
moment_decay = 0.8
matrix_rate = 1.0
vector_rate = 1.0
quintic_coef = (3.4445, -4.775, 2.0315)
masked_logit = -1e30
f32 = jnp.float32
bf16 = jnp.bfloat16
VMEM = pl.BlockSpec(memory_space=pltpu.VMEM)
light = pl.CostEstimate(flops=1000, bytes_accessed=1000, transcendentals=0)
heavy = pl.CostEstimate(flops=10_000_000_000, bytes_accessed=10_000_000, transcendentals=0)


def params(limit_mib=56, **kw):
    return pltpu.CompilerParams(vmem_limit_bytes=limit_mib * 1024 * 1024, **kw)


def nn(a, b, **kw):
    return lax.dot_general(a, b, (((1,), (0,)), ((), ())), preferred_element_type=f32, **kw)


def nt(a, b, **kw):
    return lax.dot_general(a, b, (((1,), (1,)), ((), ())), preferred_element_type=f32, **kw)


def tn(a, b, **kw):
    return lax.dot_general(a, b, (((0,), (0,)), ((), ())), preferred_element_type=f32, **kw)


def window_tables():
    pick = np.zeros((WROWS, LEN), np.float32)
    place = np.zeros((4, WIN2), np.int32)
    for r in range(SIDE):
        for c in range(SIDE):
            w = (r // WIN) * 2 + c // WIN
            i = (r % WIN) * WIN + c % WIN
            source = ((r + SHIFT) % SIDE) * SIDE + (c + SHIFT) % SIDE
            pick[w * WPAD + i, source] = 1.0
            place[w, i] = r * SIDE + c
    return pick, place


def column_order(heads, size):
    width = 3 * heads * size
    order = np.zeros((width, width), np.float32)
    for h in range(heads):
        for part in range(3):
            for e in range(size):
                order[(h * 3 + part) * size + e, part * heads * size + h * size + e] = 1.0
    return order


def norm_parts(x):
    centred = x - jnp.mean(x, axis=-1, keepdims=True)
    scale = lax.rsqrt(jnp.mean(centred * centred, axis=-1, keepdims=True) + norm_epsilon)
    return centred * scale, scale


def norm_back(n, scale, gain, u):
    w = u * gain
    return scale * (
        w - jnp.mean(w, axis=-1, keepdims=True) - n * jnp.mean(w * n, axis=-1, keepdims=True)
    )


def head_blocks(x, masks):
    return jnp.concatenate([x * m for m in masks], axis=0)


def head_diag(r, masks):
    rows = r.shape[0] // 4
    out = r[0:rows] * masks[0]
    for h in range(1, 4):
        out = out + r[h * rows : (h + 1) * rows] * masks[h]
    return out


def head_masks(dtype):
    lane = lax.broadcasted_iota(jnp.int32, (1, 128), 1) // 32
    return [jnp.where(lane == h, 1.0, 0.0).astype(dtype) for h in range(4)]


def row_place(index, count):
    group = index // 2
    quarter = count // 4
    return (group // quarter) * (2 * quarter) + (index % 2) * quarter + group % quarter


def store_rows(ref, values, me, count, at=None):
    piece = values.shape[0] // count
    for p in range(count):
        place = pl.multiple_of(row_place(p ^ me, count) * piece, piece)
        block = values[p * piece : (p + 1) * piece]
        if at is None:
            ref[pl.ds(place, piece)] = block
        else:
            ref[at, pl.ds(place, piece)] = block


def bias_kernel(k0, k1, expand, rel, bias_ref, rows_s):
    size = rel.shape[1]
    tables = jnp.concatenate([k[0:4, 0:256] for k in (k0, k1)], axis=0)
    rows_s[...] = tn(tables, expand[...], precision=highest)
    index = rel[...]
    step = 2 * WIN - 1
    for k in range(2):
        def body(n, acc):
            for m in range(step):
                at = n * step + m
                acc = jnp.where(index == at, rows_s[pl.ds(at, 1), k * size : (k + 1) * size], acc)
            return acc

        bias_ref[k] = lax.fori_loop(0, step, body, jnp.zeros(index.shape, f32))


def mask_kernel(region, mask_ref):
    shape = mask_ref.shape[1:]
    row = lax.broadcasted_iota(jnp.int32, shape, 0)
    col = lax.broadcasted_iota(jnp.int32, shape, 1) % WPAD
    for w in range(4):
        same = region[w] == region[4 + w]
        ok = (row < WIN2) & ((col >= WIN2) | same)
        mask_ref[w] = jnp.where(ok, 0.0, masked_logit)


def attn_forward(scale, count, t_ref, tok, w0, w1, w2, w3, sv, bias_a, bias_b, mask, pick, order, p_out,
                 qkv_out, sht_out, ctx_out, wcol):
    @pl.when(pl.program_id(0) == 0)
    def _():
        for k, w in enumerate((w0, w1, w2, w3)):
            wcol[k] = nn(w[0:512].astype(bf16), order[...]).astype(bf16)

    n, _ = norm_parts(tok[0].astype(f32))
    normed = (n * sv[0:1] + sv[1:2]).astype(bf16)
    shifted_f = nn(pick[...], normed)
    shifted = shifted_f.astype(bf16)
    store_rows(sht_out, shifted_f.T.astype(bf16), t_ref[1], count, 0)
    low_masks = head_masks(bf16)
    masks = head_masks(f32)
    for k in range(4):
        proj = nn(shifted, wcol[k])
        pack = (w0, w1, w2, w3)[k]
        bias = (bias_a, bias_b)[k // 2][k % 2]
        q = ((proj[:, 0:128] + pack[516:517, 0:128]) * scale).astype(bf16)
        kk = proj[:, 128:256].astype(bf16)
        v = (proj[:, 256:384] + pack[516:517, 128:256]).astype(bf16)
        qkv_out[0, k, :, 0:128] = q
        qkv_out[0, k, :, 128:256] = kk
        qkv_out[0, k, :, 256:384] = v
        spans = [slice(w * WPAD, (w + 1) * WPAD) for w in range(4)]
        logits = [
            nt(kk[rows], head_blocks(q[rows], low_masks)) + (bias + mask[w])
            for w, rows in enumerate(spans)
        ]
        exps = [jnp.exp(x - jnp.max(x, axis=0, keepdims=True)) for x in logits]
        probs = [e * (1.0 / jnp.sum(e, axis=0, keepdims=True)) for e in exps]
        mixes = [tn(p.astype(bf16), v[rows]) for p, rows in zip(probs, spans)]
        for w, p in enumerate(probs):
            p_out[0, k, w] = p
        windows = [head_diag(r, masks).astype(bf16) for r in mixes]
        ctx = jnp.concatenate(windows, axis=0)
        ctx_out[0, 0:LEN, k * 128 : (k + 1) * 128] = tn(pick[...], ctx).astype(bf16)
        ctx_out[0, LEN:ROWS, k * 128 : (k + 1) * 128] = jnp.zeros((ROWS - LEN, 128), bf16)


def hidden_blocks(we, wr, eb, hid_s, act_s, low_s, n2_s, n2t_s, cot_s, cott_s, mix_s, gn2_s, grads,
                  geb_ref):
    rows = hid_s.shape[1]
    chunk = 64

    def body(j, carry):
        hid_s[0] = nn(n2_s[...], we[j])
        hid_s[1] = nt(cot_s[...], wr[j])
        total = None
        for r in range(0, rows, chunk):
            hidden = hid_s[0, r : r + chunk] + eb[j]
            cdf = 0.5 * (1.0 + lax.erf(hidden * (1.0 / math.sqrt(2.0))))
            bell = jnp.exp(-0.5 * hidden * hidden) * (1.0 / math.sqrt(2.0 * math.pi))
            act_s[r : r + chunk] = (hidden * cdf).astype(bf16)
            g_hidden = hid_s[1, r : r + chunk] * (cdf + hidden * bell)
            low_s[r : r + chunk] = g_hidden.astype(bf16)
            total = g_hidden if r == 0 else total + g_hidden
        geb_ref[j] = jnp.sum(total, axis=0, keepdims=True)
        mix_s[...] += nn(act_s[...], wr[j])
        gn2_s[...] += nt(low_s[...], we[j])
        at = pl.multiple_of(lax.rem(j, 2) * 256, 256)
        g_exp = nn(n2t_s[...], low_s[...])
        g_red = nn(cott_s[...], act_s[...])
        for k in range(2):
            @pl.when(j // 2 == k)
            def _(k=k):
                grads[k][:, pl.ds(at, 256)] = g_exp
                grads[k][:, pl.ds(512 + at, 256)] = g_red
        return carry

    lax.fori_loop(0, 4, body, 0)


def load_bias(eb, packs):
    for k, pack in enumerate(packs):
        eb[2 * k] = pack[5:6, 0:256]
        eb[2 * k + 1] = jnp.concatenate([pack[5:6, 256:384], pack[6:7, 0:128]], axis=1)


def load_hidden(we, wr, blocks):
    for k, (e, r) in enumerate(blocks):
        for half in range(2):
            we[2 * k + half] = e[:, half * 256 : (half + 1) * 256].astype(bf16)
            wr[2 * k + half] = r[half * 256 : (half + 1) * 256].astype(bf16)


def feed_first(images, count, t_ref, ctx, tok, cot, o0, o1, o2, o3, e0, e1, r0, r1, k0, k1, sv,
               wo, mid_s, n2_s, n2t_s, cot_s, cott_s, mix_s, gn2_s, keep_ref, send_ref, geb_ref,
               we, wr, eb, hid_s, act_s, low_s, x_s):
    rows = x_s.shape[0]
    x_s[...] = jnp.zeros_like(x_s)
    for i in range(images):
        x_s[i * ROWS : i * ROWS + LEN] = tok[i].astype(f32)
    for k, o in enumerate((o0, o1, o2, o3)):
        wo[k * 128 : (k + 1) * 128] = o[...].astype(bf16)
    load_bias(eb, (k0, k1))
    load_hidden(we, wr, ((e0, r0), (e1, r1)))
    attended = jnp.concatenate(
        [ctx[...].reshape(images * ROWS, 512), jnp.zeros((rows - images * ROWS, 512), bf16)], axis=0
    )
    mid_s[...] = x_s[...] + nn(attended, wo[...]) + sv[2:3]
    n2, _ = norm_parts(mid_s[...])
    n2f = n2 * sv[3:4] + sv[4:5]
    n2_s[...] = n2f.astype(bf16)
    store_rows(n2t_s, n2f.T.astype(bf16), t_ref[1], count)
    x_s[...] = jnp.zeros_like(x_s)
    for i in range(images):
        x_s[i * ROWS : i * ROWS + LEN] = cot[i].astype(f32)
    cot_s[...] = x_s[...].astype(bf16)
    store_rows(cott_s, x_s[...].T.astype(bf16), t_ref[1], count)
    mix_s[...] = jnp.zeros_like(mix_s)
    gn2_s[...] = jnp.zeros_like(gn2_s)
    hidden_blocks(
        we, wr, eb, hid_s, act_s, low_s, n2_s, n2t_s, cot_s, cott_s, mix_s, gn2_s,
        (keep_ref, send_ref), geb_ref,
    )


def feed_second(t_ref, e2, e3, f2, f3, r2, r3, k2, k3, n2_s, n2t_s, cot_s, cott_s, mix_in, gn2_in,
                mix_s, gn2_s, keep_ref, send_ref, geb_ref, we, wr, eb, hid_s,
                act_s, low_s):
    load_bias(eb, (k2, k3))
    for k, (e, f, r) in enumerate(((e2, f2, r2), (e3, f3, r3))):
        we[2 * k + t_ref[2]] = e[...].astype(bf16)
        we[2 * k + 1 - t_ref[2]] = f[...].astype(bf16)
        for half in range(2):
            wr[2 * k + half] = r[half * 256 : (half + 1) * 256].astype(bf16)
    mix_s[...] = mix_in[...]
    gn2_s[...] = gn2_in[...]
    hidden_blocks(
        we, wr, eb, hid_s, act_s, low_s, n2_s, n2t_s, cot_s, cott_s, mix_s, gn2_s,
        (keep_ref, send_ref), geb_ref,
    )


def feed_last(images, count, t_ref, ctx, sv, wo, mid_s, cot_s, mix_s, gn2_s, out_ref, gmid_ref,
              gctx_ref, keep_o, send_o, small_ref, att_t):
    rows = mid_s.shape[0]
    result = mid_s[...] + mix_s[...] + sv[5:6]
    for i in range(images):
        out_ref[i] = result[i * ROWS : i * ROWS + LEN].astype(bf16).astype(f32)
    n2, scale2 = norm_parts(mid_s[...])
    u = gn2_s[...]
    cot = cot_s[...].astype(f32)
    gmid = cot + norm_back(n2, scale2, sv[3:4], u)
    gmid_ref[...] = gmid
    small_ref[0:1] = jnp.sum(gmid, axis=0, keepdims=True)
    small_ref[1:2] = jnp.sum(u * n2, axis=0, keepdims=True)
    small_ref[2:3] = jnp.sum(u, axis=0, keepdims=True)
    small_ref[3:4] = jnp.sum(cot, axis=0, keepdims=True)
    small_ref[4:8] = jnp.zeros((4, 512), f32)
    att_low = gmid.astype(bf16)
    gctx_ref[...] = nt(att_low, wo[...]).astype(bf16)[0 : images * ROWS].reshape(images, ROWS, 512)
    store_rows(att_t, gmid.T.astype(bf16), t_ref[1], count)
    attended = jnp.concatenate(
        [ctx[...].reshape(images * ROWS, 512), jnp.zeros((rows - images * ROWS, 512), bf16)], axis=0
    )
    g_out = nn(att_t[...], attended)
    for k in range(4):
        (keep_o, send_o)[k % 2][k // 2] = g_out[:, k * 128 : (k + 1) * 128]


def attn_backward(scale, p_in, qkv, gctx, sht, pick, order, keep_ref, send_ref, plow_ref, gbias_ref,
                  ghead_ref):
    @pl.when(pl.program_id(0) == 0)
    def _():
        keep_ref[...] = jnp.zeros_like(keep_ref)
        send_ref[...] = jnp.zeros_like(send_ref)
        gbias_ref[...] = jnp.zeros_like(gbias_ref)
        ghead_ref[...] = jnp.zeros_like(ghead_ref)

    gwin = nn(pick[...], gctx[0, 0:LEN]).astype(bf16)
    low_masks = head_masks(bf16)
    masks = head_masks(f32)
    for k in range(4):
        q = qkv[0, k, :, 0:128]
        kk = qkv[0, k, :, 128:256]
        v = qkv[0, k, :, 256:384]
        spans = [slice(w * WPAD, (w + 1) * WPAD) for w in range(4)]
        blocks = [head_blocks(gwin[rows, k * 128 : (k + 1) * 128], low_masks) for rows in spans]
        probs = [p_in[0, k, w] for w in range(4)]
        gps = [nt(v[rows], gbd) for rows, gbd in zip(spans, blocks)]
        gvs = [nn(p.astype(bf16), gbd) for p, gbd in zip(probs, blocks)]
        prods = [p * gp for p, gp in zip(probs, gps)]
        gls = [x - p * jnp.sum(x, axis=0, keepdims=True) for p, x in zip(probs, prods)]
        lows = [gl.astype(bf16) for gl in gls]
        gks = [nn(low, head_blocks(q[rows], low_masks)) for low, rows in zip(lows, spans)]
        gqs = [head_diag(tn(low, kk[rows]), masks) * scale for low, rows in zip(lows, spans)]
        bias_sum = gls[0] + gls[1] + gls[2] + gls[3]
        q_sum = jnp.sum(gqs[0] + gqs[1] + gqs[2] + gqs[3], axis=0, keepdims=True)
        v_sum = jnp.sum(gvs[0] + gvs[1] + gvs[2] + gvs[3], axis=0, keepdims=True)
        parts = [
            jnp.concatenate([gq, gk, gv], axis=1).astype(bf16) for gq, gk, gv in zip(gqs, gks, gvs)
        ]
        gbias_ref[k] += bias_sum
        ghead_ref[k, 0:1] += q_sum
        ghead_ref[k, 1:2] += v_sum
        plow = nt(jnp.concatenate(parts, axis=0), order[...]).astype(bf16)
        (keep_ref, send_ref)[k % 2][k // 2] += nn(sht[0], plow)
        plow_ref[0, k, 0:LEN] = tn(pick[...], plow).astype(bf16)
        plow_ref[0, k, LEN:ROWS] = jnp.zeros((ROWS - LEN, plow.shape[1]), bf16)


def input_backward(t_ref, tok, gmid, plow, w0, w1, w2, w3, sv, out_ref, small_ref, wlow):
    @pl.when(pl.program_id(0) == 0)
    def _():
        small_ref[...] = jnp.zeros_like(small_ref)
        for k, w in enumerate((w0, w1, w2, w3)):
            wlow[k] = w[...].astype(bf16)

    u = nt(plow[0, 0], wlow[0])
    for k in range(1, 4):
        u = u + nt(plow[0, k], wlow[k])
    u = u[0:LEN]
    n, scale = norm_parts(tok[0].astype(f32))
    small_ref[0:1] += jnp.sum(u * n, axis=0, keepdims=True)
    small_ref[1:2] += jnp.sum(u, axis=0, keepdims=True)
    out_ref[0] = gmid[0:LEN] + norm_back(n, scale, sv[0:1], u)


def assemble(t_ref, a0, a1, a2, a3, out):
    for k, a in enumerate((a0, a1, a2, a3)):
        @pl.when(pl.program_id(0) == k)
        def _(a=a):
            out[...] = a[...].astype(out.dtype)


def split_low(x, parts):
    out = []
    for _ in range(parts):
        low = x.astype(bf16)
        out.append(low)
        x = x - low.astype(f32)
    return out


def spread_product(left, right, terms, product=nn):
    total = None
    for i, j in terms:
        part = product(left[i], right[j])
        total = part if total is None else total + part
    return total


def symmetric_product(out, left, right, terms):
    half = out.shape[0] // 2
    top = [x[:half] for x in left]
    bottom = [x[half:] for x in left]
    first = [x[:, :half] for x in right]
    second = [x[:, half:] for x in right]
    out[:half, :half] = spread_product(top, first, terms)
    cross = spread_product(top, second, terms)
    out[:half, half:] = cross
    out[half:, :half] = cross.T
    out[half:, half:] = spread_product(bottom, second, terms)


three_terms = ((1, 0), (0, 1), (0, 0))
six_terms = ((2, 0), (0, 2), (1, 1)) + three_terms


def gram_kernel(spans, flip, t_ref, same, other, g_ref):
    for n, (start, stop) in enumerate(spans):
        a = split_low(same[:, start:stop], 3)
        b = split_low(other[:, start:stop], 3)
        half = same.shape[0]
        place = (t_ref[0] % 2) ^ (n ^ flip)
        for m, (left, right) in enumerate(((a, a), (a, b), (b, b))):
            g_ref[place, :, m * half : (m + 1) * half] = spread_product(left, right, six_terms, nt)


def newton_schulz(t_ref, keep_a, near_a, far_a, keep_i, near_i, far_i, rows_ref, a_s, p_s, t_s, q_s):
    inner = (t_ref[0] == 1) | (t_ref[0] == 2)
    g = jnp.where(
        inner, keep_a[0] + near_a[...] + far_a[...], keep_i[0] + near_i[...] + far_i[...]
    )
    half = g.shape[0]
    size = 2 * half
    cross = g[:, half:size]
    a_s[:half, :half] = g[:, :half]
    a_s[:half, half:] = cross
    a_s[half:, :half] = cross.T
    a_s[half:, half:] = g[:, size:]
    row = lax.broadcasted_iota(jnp.int32, (size, size), 0)
    col = lax.broadcasted_iota(jnp.int32, (size, size), 1)
    eye = jnp.where(row == col, 1.0, 0.0)
    whole = a_s[...]
    inv = 1.0 / (jnp.sum(jnp.sum(whole * eye, axis=0, keepdims=True), axis=1, keepdims=True) + 1e-07)
    a_s[...] = whole * inv
    c0, c1, c2 = quintic_coef
    for step in range(NS_STEPS):
        exact = step < 3
        terms = six_terms if exact else three_terms
        parts = split_low(a_s[...], 3 if exact else 2)
        symmetric_product(t_s, parts, parts, terms)
        p_s[...] = c0 * eye + c1 * a_s[...] + c2 * t_s[...]
        poly = split_low(p_s[...], 3 if exact else 2)
        if step == 0:
            q_s[...] = p_s[...]
        else:
            symmetric_product(q_s, poly, split_low(q_s[...], 2), three_terms)
        if step < NS_STEPS - 1:
            symmetric_product(t_s, poly, parts, terms)
            symmetric_product(a_s, poly, split_low(t_s[...], 3 if exact else 2), terms)
    rows_ref[...] = q_s[0 : rows_ref.shape[0]] * jnp.sqrt(inv)


def final_kernel(places, factors, t_ref, q0, q1, q2, q3, same_a, other_a, same_i, other_i, u_in,
                 u_exp, u_red, u_out, q_s):
    for k, q in enumerate((q0, q1, q2, q3)):
        q_s[t_ref[0] ^ k] = q[...]
    for m, (group, start, stop) in enumerate(places):
        same = (same_i, same_a)[group][:, start:stop]
        other = (other_i, other_a)[group][:, start:stop]
        half = same.shape[0]
        u = (-matrix_rate * factors[m]) * (
            nn(q_s[m, :, 0:half], same, precision=highest)
            + nn(q_s[m, :, half:], other, precision=highest)
        )
        ref = (u_in, u_exp, u_red, u_out)[m]
        ref[...] = u


def after(value, *earlier):
    return lax.optimization_barrier((value, *earlier))[0]


def xor_tensor(x, k):
    return lax.ppermute(x, "tensor", [(i, i ^ k) for i in range(lax.axis_size("tensor"))])


def xor_dp(x, k):
    return lax.ppermute(x, "dp", [(i, i ^ k) for i in range(lax.axis_size("dp"))])


def gather_tensor(block, *earlier, late=None):
    near = xor_tensor(block, 1)
    far = xor_tensor(after(block, *earlier) if earlier else block, 2)
    return [block, near, far, xor_tensor(far if late is None else after(far, late), 1)]


def scatter_tensor(blocks):
    got = xor_tensor(jnp.stack([blocks[1], blocks[3]]), 1)
    own = blocks[0] + got[0]
    far = blocks[2] + got[1]
    return own + xor_tensor(far, 2)


def first_stage(own, far):
    rows = lax.axis_size("dp") * own.piece
    half, quarter = rows // 2, rows // 4
    return far(0, half), jnp.stack([own(half + quarter, rows), far(half + quarter, rows)])


def second_stage(own, far, got_t, got_d):
    rows = lax.axis_size("dp") * own.piece
    half, quarter = rows // 2, rows // 4
    last = own(quarter, half) + got_t[quarter:]
    return far(half, half + quarter) + got_d[1], last, own(0, quarter) + got_t[:quarter]


def third_stage(own, keep, got_d, last_t, last_d):
    piece = own.piece
    rows = lax.axis_size("dp") * piece
    half, quarter = rows // 2, rows // 4
    pieces = [keep[i : i + piece] + last_d[i : i + piece] for i in range(0, quarter, piece)]
    for i in range(0, quarter, piece):
        start = half + i
        pieces.append(
            own(start, start + piece) + got_d[0, i : i + piece] + last_t[i : i + piece]
        )
    return pieces


class Summed:
    def __init__(self, piece, *groups):
        self.piece = piece
        self.groups = groups

    def __call__(self, start, stop):
        return jnp.concatenate([a[start:stop] + b[start:stop] for a, b in self.groups], axis=1)


def send_groups(pieces):
    return [xor_dp(p, 2 * g) for g, p in enumerate(pieces) if g > 0]


def barrier(*values):
    return lax.optimization_barrier(values)


def join_images(t, parts, dtype):
    images, length, features = parts[0].shape
    return pl.pallas_call(
        assemble,
        grid_spec=pltpu.PrefetchScalarGridSpec(
            num_scalar_prefetch=1,
            grid=(4,),
            in_specs=[pl.BlockSpec((images, length, features), lambda a, t_ref: (0, 0, 0))] * 4,
            out_specs=pl.BlockSpec(
                (images, length, features), lambda a, t_ref: (t_ref[0] ^ a, 0, 0)
            ),
        ),
        out_shape=jax.ShapeDtypeStruct((4 * images, length, features), dtype),
        compiler_params=params(),
        cost_estimate=heavy,
        name="join_images",
    )(t, *parts)


def local(
    tokens,
    cotangent,
    region_ids,
    relative_index,
    shared_vectors,
    input_weight,
    head_bias,
    output_weight,
    expand_weight,
    expand_bias,
    reduce_weight,
    bias_table,
    moment_shared,
    moment_input,
    moment_head,
    moment_output,
    moment_expand,
    moment_bias,
    moment_reduce,
    moment_table,
):
    nt_axis = lax.axis_size("tensor")
    me_t = lax.axis_index("tensor")
    me_d = lax.axis_index("dp")
    nd = lax.axis_size("dp")
    all_images, length, features = tokens.shape
    images = all_images // nt_axis
    heads = bias_table.shape[1]
    head_size = head_bias.shape[1] // heads
    width = heads * head_size
    hidden_here = expand_weight.shape[1]
    table_rows = bias_table.shape[0]
    query_scale = head_size ** (-0.5)
    low_d = me_d % 2
    t_arr = jnp.stack([me_t, me_d, low_d]).astype(jnp.int32)
    rows = -(-images * ROWS // 128) * 128
    lanes = heads * WPAD

    pad_lanes = lambda x: jnp.pad(x, ((0, 0), (0, 3 * width - x.shape[1])))
    eb_row = expand_bias.reshape(1, hidden_here)
    packed = jnp.concatenate(
        [
            input_weight,
            pad_lanes(bias_table.T),
            pad_lanes(head_bias.reshape(1, 2 * width)),
            eb_row[:, : 3 * width],
            pad_lanes(eb_row[:, 3 * width :]),
            jnp.zeros((9, 3 * width), f32),
        ]
    )
    w_in = [packed, xor_tensor(packed, 1), xor_tensor(packed, 2)]
    w_out = [output_weight, xor_tensor(output_weight, 1), xor_tensor(output_weight, 2)]
    w_exp = [expand_weight, xor_tensor(expand_weight, 1)]
    w_red = [reduce_weight, xor_tensor(reduce_weight, 1)]
    half_exp = lax.dynamic_slice_in_dim(expand_weight, low_d * (hidden_here // 2), hidden_here // 2, 1)
    mine_exp = xor_tensor(after(half_exp, w_in[1]), 2)

    pick_np, place_np = window_tables()
    pick = jnp.asarray(pick_np, bf16)
    order = jnp.asarray(column_order(heads, head_size), bf16)
    rel_t = jnp.pad(relative_index.T, ((0, WPAD - WIN2), (0, WPAD - WIN2)), constant_values=-1)
    rel_wide = jnp.tile(rel_t, (1, heads))
    region = region_ids.reshape(2, WIN, 2, WIN).transpose(0, 2, 1, 3).reshape(4, WIN2)
    region = jnp.pad(region, ((0, 0), (0, WPAD - WIN2)))
    region_both = jnp.concatenate(
        [
            jnp.broadcast_to(region[:, :, None], (4, WPAD, lanes)),
            jnp.broadcast_to(jnp.tile(region, (1, heads))[:, None, :], (4, WPAD, lanes)),
        ]
    )
    spread = np.zeros((2 * heads, 2 * lanes), np.float32)
    for h in range(2 * heads):
        spread[h, h * WPAD : (h + 1) * WPAD] = 1.0
    sds = jax.ShapeDtypeStruct
    pack_spec = pl.BlockSpec((16, 3 * width), lambda i, *_: (features // 16, 0))

    def bias_of(blocks):
        return pl.pallas_call(
            bias_kernel,
            grid=(1,),
            in_specs=[pack_spec] * 2
            + [
                pl.BlockSpec((2 * heads, 2 * lanes), lambda i: (0, 0)),
                pl.BlockSpec((WPAD, lanes), lambda i: (0, 0)),
            ],
            out_specs=pl.BlockSpec((2, WPAD, lanes), lambda i: (0, 0, 0)),
            out_shape=sds((2, WPAD, lanes), f32),
            scratch_shapes=[pltpu.VMEM((256, 2 * lanes), f32)],
            compiler_params=params(),
            cost_estimate=light,
            name="bias",
        )(*blocks, jnp.asarray(spread), rel_wide)

    mask = pl.pallas_call(
        mask_kernel,
        in_specs=[VMEM],
        out_specs=VMEM,
        out_shape=sds((4, WPAD, lanes), f32),
        compiler_params=params(),
        cost_estimate=light,
        name="mask",
    )(region_both)
    bias_a = bias_of(w_in[:2])
    piece = features // nd
    row_at = me_d * piece
    moment_a = jnp.concatenate(
        [
            lax.dynamic_slice_in_dim(moment_expand, row_at, piece, 0),
            lax.dynamic_slice_in_dim(moment_reduce, row_at, piece, 1).T,
        ],
        axis=1,
    )
    moment_i = jnp.concatenate(
        [
            lax.dynamic_slice_in_dim(moment_input, row_at, piece, 0),
            lax.dynamic_slice_in_dim(moment_output, row_at, piece, 1).T,
        ],
        axis=1,
    )
    w_in[2], w_out[2], bias_a, mask, moment_a, moment_i = barrier(
        w_in[2], w_out[2], bias_a, mask, moment_a, moment_i
    )
    w_in.append(xor_tensor(w_in[2], 1))
    w_out.append(xor_tensor(w_out[2], 1))
    bias_b = bias_of(w_in[2:])
    far_red = xor_tensor(after(reduce_weight, bias_b), 2)

    whole = lambda *shape: pl.BlockSpec(shape, lambda i, *_: (0,) * len(shape))
    one = lambda *shape: pl.BlockSpec((1,) + shape, lambda i, *_: (i,) + (0,) * len(shape))
    tok_one = pl.BlockSpec((1, length, features), lambda i, t: (t[0] * images + i, 0, 0))
    probs, qkv, sht, ctx = pl.pallas_call(
        functools.partial(attn_forward, query_scale, nd),
        grid_spec=pltpu.PrefetchScalarGridSpec(
            num_scalar_prefetch=1,
            grid=(images,),
            in_specs=[tok_one]
            + [whole(features + 16, 3 * width)] * 4
            + [
                whole(6, features),
                whole(2, WPAD, lanes),
                whole(2, WPAD, lanes),
                whole(4, WPAD, lanes),
                whole(WROWS, LEN),
                whole(3 * width, 3 * width),
            ],
            out_specs=[
                one(4, 4, WPAD, lanes),
                one(4, WROWS, 3 * width),
                one(features, WROWS),
                one(ROWS, 4 * width),
            ],
            scratch_shapes=[pltpu.VMEM((4, features, 3 * width), bf16)],
        ),
        out_shape=[
            sds((images, 4, 4, WPAD, lanes), f32),
            sds((images, 4, WROWS, 3 * width), bf16),
            sds((images, features, WROWS), bf16),
            sds((images, ROWS, 4 * width), bf16),
        ],
        compiler_params=params(),
        cost_estimate=heavy,
        name="attn_forward",
    )(t_arr, tokens, *w_in, shared_vectors, bias_a, bias_b, mask, pick, order)

    mine_exp = after(mine_exp, ctx)
    other_exp = xor_dp(mine_exp, 1)
    mine_last = xor_tensor(mine_exp, 1)
    tok_all = pl.BlockSpec((images, length, features), lambda i, t: (t[0], 0, 0))
    token_f = (rows, features)
    wide = 2 * hidden_here
    hidden_scratch = [
        pltpu.VMEM((4, features, hidden_here // 2), bf16),
        pltpu.VMEM((4, hidden_here // 2, features), bf16),
        pltpu.VMEM((4, 1, hidden_here // 2), f32),
        pltpu.VMEM((2, rows, hidden_here // 2), f32),
        pltpu.VMEM((rows, hidden_here // 2), bf16),
        pltpu.VMEM((rows, hidden_here // 2), bf16),
    ]
    state_shapes = [
        ((4 * width, features), bf16),
        (token_f, f32),
        (token_f, bf16),
        (token_f[::-1], bf16),
        (token_f, bf16),
        (token_f[::-1], bf16),
        (token_f, f32),
        (token_f, f32),
    ]
    *carry, keep_0, send_1, geb_a = pl.pallas_call(
        functools.partial(feed_first, images, nd),
        grid_spec=pltpu.PrefetchScalarGridSpec(
            num_scalar_prefetch=1,
            grid=(1,),
            in_specs=[whole(images, ROWS, 4 * width), tok_all, tok_all]
            + [whole(width, features)] * 4
            + [whole(features, hidden_here)] * 2
            + [whole(hidden_here, features)] * 2
            + [pack_spec] * 2
            + [whole(6, features)],
            out_specs=[whole(*shape) for shape, _ in state_shapes]
            + [whole(features, wide), whole(features, wide), whole(4, 1, hidden_here // 2)],
            scratch_shapes=hidden_scratch + [pltpu.VMEM(token_f, f32)],
        ),
        out_shape=[sds(shape, dtype) for shape, dtype in state_shapes]
        + [sds((features, wide), f32)] * 2
        + [sds((4, 1, hidden_here // 2), f32)],
        compiler_params=params(),
        cost_estimate=heavy,
        name="feed_first",
    )(t_arr, ctx, tokens, cotangent, *w_out, *w_exp, *w_red, *w_in[:2], shared_vectors)

    other_exp = after(other_exp, geb_a)
    other_last = xor_tensor(other_exp, 1)
    far_red = after(far_red, geb_a)
    w_red += [far_red, xor_tensor(far_red, 1)]
    got_1 = xor_tensor(send_1, 1)

    wo_low, mid, n2_low, n2_t, cot_low, cot_t, mix, gn2 = carry
    mix, gn2, keep_2, send_3, geb_b = pl.pallas_call(
        feed_second,
        grid_spec=pltpu.PrefetchScalarGridSpec(
            num_scalar_prefetch=1,
            grid=(1,),
            in_specs=[whole(features, hidden_here // 2)] * 4
            + [whole(hidden_here, features)] * 2
            + [pack_spec] * 2
            + [whole(*shape) for shape, _ in state_shapes[2:]],
            out_specs=[
                whole(rows, features),
                whole(rows, features),
                whole(features, wide),
                whole(features, wide),
                whole(4, 1, hidden_here // 2),
            ],
            scratch_shapes=hidden_scratch,
        ),
        out_shape=[
            sds((rows, features), f32),
            sds((rows, features), f32),
            sds((features, wide), f32),
            sds((features, wide), f32),
            sds((4, 1, hidden_here // 2), f32),
        ],
        compiler_params=params(),
        cost_estimate=light,
        name="feed_second",
    )(
        t_arr,
        mine_exp,
        mine_last,
        other_exp,
        other_last,
        *w_red[2:],
        *w_in[2:],
        n2_low,
        n2_t,
        cot_low,
        cot_t,
        mix,
        gn2,
    )
    got_3 = xor_tensor(send_3, 1)

    block_part, gmid, gctx, keep_o, send_o, small_a = pl.pallas_call(
        functools.partial(feed_last, images, nd),
        grid_spec=pltpu.PrefetchScalarGridSpec(
            num_scalar_prefetch=1,
            grid=(1,),
            in_specs=[
                whole(images, ROWS, 4 * width),
                whole(6, features),
                whole(4 * width, features),
            ]
            + [whole(rows, features)] * 4,
            out_specs=[
                whole(images, length, features),
                whole(rows, features),
                whole(images, ROWS, 4 * width),
                whole(2, features, width),
                whole(2, features, width),
                whole(8, features),
            ],
            scratch_shapes=[pltpu.VMEM(token_f[::-1], bf16)],
        ),
        out_shape=[
            sds((images, length, features), f32),
            sds((rows, features), f32),
            sds((images, ROWS, 4 * width), bf16),
            sds((2, features, width), f32),
            sds((2, features, width), f32),
            sds((8, features), f32),
        ],
        compiler_params=params(),
        cost_estimate=light,
        name="feed_last",
    )(t_arr, ctx, shared_vectors, wo_low, mid, cot_low, mix, gn2)

    got_o = xor_tensor(send_o, 1)
    got_3, gctx = barrier(got_3, gctx)
    own_a = Summed(piece, (keep_0, got_1))
    far_a = Summed(piece, (keep_2, got_3))
    t1_a, d1_a = first_stage(own_a, far_a)
    gctx, t1_a, d1_a = barrier(gctx, t1_a, d1_a)
    got_t1_a, got_d1_a = xor_tensor(t1_a, 2), xor_dp(d1_a, 1)

    keep_i, send_i, plow, gbias, ghead = pl.pallas_call(
        functools.partial(attn_backward, query_scale),
        grid=(images,),
        in_specs=[
            one(4, 4, WPAD, lanes),
            one(4, WROWS, 3 * width),
            one(ROWS, 4 * width),
            one(features, WROWS),
            whole(WROWS, LEN),
            whole(3 * width, 3 * width),
        ],
        out_specs=[
            whole(2, features, 3 * width),
            whole(2, features, 3 * width),
            one(4, ROWS, 3 * width),
            whole(4, WPAD, lanes),
            whole(4, 2, width),
        ],
        out_shape=[
            sds((2, features, 3 * width), f32),
            sds((2, features, 3 * width), f32),
            sds((images, 4, ROWS, 3 * width), bf16),
            sds((4, WPAD, lanes), f32),
            sds((4, 2, width), f32),
        ],
        compiler_params=params(),
        cost_estimate=light,
        name="attn_backward",
    )(probs, qkv, gctx, sht, pick, order)

    got_i = xor_tensor(send_i, 1)

    grad_part, small_i = pl.pallas_call(
        input_backward,
        grid_spec=pltpu.PrefetchScalarGridSpec(
            num_scalar_prefetch=1,
            grid=(images,),
            in_specs=[
                tok_one,
                pl.BlockSpec((ROWS, features), lambda i, t: (i, 0)),
                one(4, ROWS, 3 * width),
            ]
            + [whole(features, 3 * width)] * 4
            + [whole(6, features)],
            out_specs=[one(length, features), whole(8, features)],
            scratch_shapes=[pltpu.VMEM((4, features, 3 * width), bf16)],
        ),
        out_shape=[sds((images, length, features), f32), sds((8, features), f32)],
        compiler_params=params(),
        cost_estimate=light,
        name="input_backward",
    )(t_arr, tokens, gmid, plow, *w_in, shared_vectors)

    got_t1_a, got_d1_a, send_small_i = barrier(got_t1_a, got_d1_a, small_i)
    small_i = send_small_i
    t2_a, d2_a, kept_a = second_stage(own_a, far_a, got_t1_a, got_d1_a)
    got_t2_a, got_d2_a = xor_tensor(t2_a, 2), xor_dp(d2_a, 1)
    got_i = barrier(got_i, t2_a, d2_a)[0]
    own_i = Summed(piece, (keep_i[0], got_i[0]), (keep_o[0], got_o[0]))
    far_i = Summed(piece, (keep_i[1], got_i[1]), (keep_o[1], got_o[1]))
    t1_i, d1_i = first_stage(own_i, far_i)
    got_t1_i, got_d1_i = xor_tensor(t1_i, 2), xor_dp(d1_i, 1)
    got_t2_a, got_d2_a, t1_i, d1_i = barrier(got_t2_a, got_d2_a, t1_i, d1_i)
    pieces_a = third_stage(own_a, kept_a, got_d1_a, got_t2_a, got_d2_a)
    got_a = send_groups(pieces_a)
    got_t1_i, got_d1_i = barrier(got_t1_i, got_d1_i, *got_a)[:2]
    t2_i, d2_i, kept_i = second_stage(own_i, far_i, got_t1_i, got_d1_i)
    got_t2_i, got_d2_i = xor_tensor(t2_i, 2), xor_dp(d2_i, 1)
    block_part = after(block_part, *pieces_a)
    block_parts = [block_part, xor_tensor(block_part, 1), xor_tensor(block_part, 2)]
    gbias, ghead, small_i, geb_a, geb_b, small_a = barrier(
        gbias, ghead, small_i, geb_a, geb_b, small_a, *pieces_a
    )[:6]

    pick_table = (
        jnp.arange(table_rows)[:, None] == rel_t[:WIN2].reshape(1, -1)
    ).astype(f32)
    gb = gbias[:, :WIN2].reshape(4, WIN2, heads, WPAD).transpose(0, 2, 1, 3)
    gtable = lax.dot_general(
        gb.reshape(4 * heads, -1), pick_table, (((1,), (1,)), ((), ())), precision=highest
    ).reshape(4, heads * table_rows)
    shared_rows = jnp.concatenate([small_i[0:2], small_a[0:4]])
    geb = jnp.concatenate([geb_a, geb_b]).reshape(4, hidden_here)
    block_small = jnp.concatenate([gtable, ghead.reshape(4, -1), geb], axis=1)
    n_small = block_small.shape[1]
    small_send = jnp.concatenate([block_small[1], block_small[3], shared_rows.reshape(-1)])
    got_small = xor_tensor(small_send, 1)
    got_a = barrier(*got_a, small_send)[: len(got_a)]
    grad_scale = (all_images * length * nd) ** (-0.5)
    grad_a = sum(got_a, pieces_a[0]) * grad_scale
    state_a = moment_decay * moment_a + (1.0 - moment_decay) * grad_a
    same_a = [state_a] + send_groups([state_a] * (nd // 2))
    got_small = barrier(got_small, state_a)[0]
    own_small = block_small[0] + got_small[:n_small]
    far_small = block_small[2] + got_small[n_small : 2 * n_small]
    shared_sum = shared_rows.reshape(-1) + got_small[2 * n_small :]
    small_send = jnp.concatenate([far_small, shared_sum])
    got_small = xor_tensor(small_send, 2)
    grad_part = after(grad_part, small_send)
    grad_parts = [grad_part, xor_tensor(grad_part, 1), xor_tensor(grad_part, 2)]
    same_a = jnp.concatenate(barrier(*same_a, t2_i, d2_i, small_send)[: len(same_a)])
    other_a = xor_dp(same_a, 1)
    got_t2_i, got_d2_i, got_small, far_block = barrier(
        got_t2_i, got_d2_i, got_small, block_parts[2], same_a
    )[:4]
    pieces_i = third_stage(own_i, kept_i, got_d1_i, got_t2_i, got_d2_i)
    got_i = send_groups(pieces_i)
    block_parts = [block_parts[0], block_parts[1], far_block, xor_tensor(far_block, 1)]
    vector = jnp.concatenate([own_small, shared_sum]) + got_small
    *got_i, vector = barrier(*got_i, vector, other_a)[: len(got_i) + 1]
    got_small = xor_dp(vector, 1)
    grad_i = sum(got_i, pieces_i[0]) * grad_scale
    state_i = moment_decay * moment_i + (1.0 - moment_decay) * grad_i
    same_i = [state_i] + send_groups([state_i] * (nd // 2))
    block_parts[1], block_parts[3] = barrier(block_parts[1], block_parts[3], state_i)[:2]
    block_out = join_images(t_arr, block_parts, bf16)

    places = [
        (0, 0, 3 * width),
        (1, 0, hidden_here),
        (1, hidden_here, wide),
        (0, 3 * width, 4 * width),
    ]
    half = features // 2
    scalars = pl.BlockSpec(memory_space=pltpu.SMEM)

    def grams(group, *operands):
        spans = [(b, c) for a, b, c in places if a == group]
        return pl.pallas_call(
            functools.partial(gram_kernel, spans, group),
            in_specs=[scalars] + [VMEM] * 2,
            out_specs=VMEM,
            out_shape=sds((2, half, 3 * half), f32),
            compiler_params=params(),
            cost_estimate=light,
            name="gram",
        )(t_arr, *operands)

    def far_sums(kept, near, pairs):
        return lax.ppermute(kept[0] + near, "tensor", pairs)

    gram_a = grams(1, same_a, other_a)
    near_a = xor_tensor(gram_a[1], 1)
    same_i = jnp.concatenate(barrier(*same_i, block_out, gram_a)[: len(same_i)])
    other_i = xor_dp(same_i, 1)
    near_a, got_small = barrier(near_a, got_small, same_i)[:2]
    far_a = far_sums(gram_a, near_a, [(0, 2), (3, 1)])
    vector = vector + got_small
    small_parts = send_groups([vector] * (nd // 2))
    other_i, grad_far = barrier(other_i, grad_parts[2], vector)[:2]
    gram_i = grams(0, same_i, other_i)
    near_i = xor_tensor(gram_i[1], 1)
    grad_far = after(grad_far, gram_i)
    grad_last = xor_tensor(grad_far, 1)
    far_i = far_sums(gram_i, near_i, [(2, 0), (1, 3)])
    grad_near, grad_last = barrier(grad_parts[1], grad_last, near_i)[:2]
    input_grad = join_images(t_arr, [grad_parts[0], grad_near, grad_far, grad_last], f32)
    far_i, far_a = barrier(far_i, far_a, input_grad)[:2]
    own_rows = pl.pallas_call(
        newton_schulz,
        in_specs=[scalars] + [VMEM] * 6,
        out_specs=VMEM,
        out_shape=sds((piece, features), f32),
        scratch_shapes=[pltpu.VMEM((features, features), f32)] * 4,
        compiler_params=params(),
        cost_estimate=light,
        name="newton_schulz",
    )(t_arr, gram_a, near_a, far_a, gram_i, near_i, far_i)
    near_rows = xor_tensor(own_rows, 1)
    far_rows = xor_tensor(own_rows, 2)
    factor = lambda a, b: math.sqrt(max(1.0, a / b))
    update_m = pl.pallas_call(
        functools.partial(
            final_kernel,
            places,
            [
                factor(features, 3 * width * nt_axis),
                factor(features, hidden_here * nt_axis),
                factor(hidden_here * nt_axis, features),
                factor(width * nt_axis, features),
            ],
        ),
        in_specs=[scalars] + [VMEM] * 8,
        out_specs=[VMEM] * 4,
        out_shape=[
            sds((piece, 3 * width), f32),
            sds((piece, hidden_here), f32),
            sds((piece, hidden_here), f32),
            sds((piece, width), f32),
        ],
        scratch_shapes=[pltpu.VMEM((4, piece, features), f32)],
        compiler_params=params(),
        cost_estimate=light,
        name="update",
    )(
        t_arr,
        own_rows,
        near_rows,
        far_rows,
        xor_tensor(far_rows, 1),
        same_a,
        other_a,
        same_i,
        other_i,
    )
    update_m = (update_m[0], update_m[3].T, update_m[1], update_m[2].T)

    for part in barrier(*small_parts, near_i)[: len(small_parts)]:
        vector = vector + part
    at = heads * table_rows
    gradients = {
        "table": vector[:at].reshape(heads, table_rows).T,
        "head": vector[at : at + 2 * width].reshape(2, width),
        "bias": vector[at + 2 * width : n_small],
        "shared": vector[n_small:].reshape(6, features),
    }
    moments = dict(table=moment_table, head=moment_head, bias=moment_bias, shared=moment_shared)
    gradients = {k: v * grad_scale for k, v in gradients.items()}
    states = {
        k: moment_decay * moments[k] + (1.0 - moment_decay) * gradients[k] for k in gradients
    }

    def split(part_i, part_a):
        a, b, c, d = [(part_i, part_a)[g][:, s:e] for g, s, e in places]
        return a, d.T, b, c.T

    grad_m = split(grad_i, grad_a)
    state_m = split(state_i, state_a)
    return (
        block_out,
        input_grad,
        gradients["shared"],
        grad_m[0],
        gradients["head"],
        grad_m[1],
        grad_m[2],
        gradients["bias"],
        grad_m[3],
        gradients["table"],
        -vector_rate * states["shared"],
        update_m[0],
        -vector_rate * states["head"],
        update_m[1],
        update_m[2],
        -vector_rate * states["bias"],
        update_m[3],
        -vector_rate * states["table"],
        states["shared"],
        state_m[0],
        states["head"],
        state_m[1],
        state_m[2],
        states["bias"],
        state_m[3],
        states["table"],
    )


def solution(mesh):
    return jax.shard_map(
        local,
        mesh=mesh,
        in_specs=(
            P("dp", None, None),
            P("dp", None, None),
            P(),
            P(),
            P(),
            P(None, "tensor"),
            P(None, "tensor"),
            P("tensor", None),
            P(None, "tensor"),
            P("tensor"),
            P("tensor", None),
            P(None, "tensor"),
            P(),
            P(None, "tensor"),
            P(None, "tensor"),
            P("tensor", None),
            P(None, "tensor"),
            P("tensor"),
            P("tensor", None),
            P(None, "tensor"),
        ),
        out_specs=(
            P("dp", None, None),
            P("dp", None, None),
            P(),
            P("dp", "tensor"),
            P(None, "tensor"),
            P("tensor", "dp"),
            P("dp", "tensor"),
            P("tensor"),
            P("tensor", "dp"),
            P(None, "tensor"),
            P(),
            P("dp", "tensor"),
            P(None, "tensor"),
            P("tensor", "dp"),
            P("dp", "tensor"),
            P("tensor"),
            P("tensor", "dp"),
            P(None, "tensor"),
            P(),
            P("dp", "tensor"),
            P(None, "tensor"),
            P("tensor", "dp"),
            P("dp", "tensor"),
            P("tensor"),
            P("tensor", "dp"),
            P(None, "tensor"),
        ),
        check_vma=False,
    )
```

```python
import functools
import math

import jax
import jax.numpy as jnp
import numpy as np
from jax import lax
from jax.experimental import pallas as pl
from jax.experimental.pallas import tpu as pltpu
from jax.sharding import PartitionSpec as P

SIDE = 14
WIN = 7
SHIFT = 3
NS_STEPS = 5
WIN2 = WIN * WIN
LEN = SIDE * SIDE
TABLE = (2 * WIN - 1) ** 2
ROWS = 208
WPAD = 64
WROWS = 4 * WPAD

highest = lax.Precision.HIGHEST
norm_epsilon = 1e-05
moment_decay = 0.8
matrix_rate = 1.0
vector_rate = 1.0
quintic_coef = (3.4445, -4.775, 2.0315)
masked_logit = -1e30
f32 = jnp.float32
bf16 = jnp.bfloat16
VMEM = pl.BlockSpec(memory_space=pltpu.VMEM)
light = pl.CostEstimate(flops=1000, bytes_accessed=1000, transcendentals=0)
heavy = pl.CostEstimate(flops=10_000_000_000, bytes_accessed=10_000_000, transcendentals=0)


def params(limit_mib=56, **kw):
    return pltpu.CompilerParams(vmem_limit_bytes=limit_mib * 1024 * 1024, **kw)


def nn(a, b, **kw):
    return lax.dot_general(a, b, (((1,), (0,)), ((), ())), preferred_element_type=f32, **kw)


def nt(a, b, **kw):
    return lax.dot_general(a, b, (((1,), (1,)), ((), ())), preferred_element_type=f32, **kw)


def tn(a, b, **kw):
    return lax.dot_general(a, b, (((0,), (0,)), ((), ())), preferred_element_type=f32, **kw)


def window_tables():
    pick = np.zeros((WROWS, LEN), np.float32)
    place = np.zeros((4, WIN2), np.int32)
    for r in range(SIDE):
        for c in range(SIDE):
            w = (r // WIN) * 2 + c // WIN
            i = (r % WIN) * WIN + c % WIN
            source = ((r + SHIFT) % SIDE) * SIDE + (c + SHIFT) % SIDE
            pick[w * WPAD + i, source] = 1.0
            place[w, i] = r * SIDE + c
    return pick, place


def column_order(heads, size):
    width = 3 * heads * size
    order = np.zeros((width, width), np.float32)
    for h in range(heads):
        for part in range(3):
            for e in range(size):
                order[(h * 3 + part) * size + e, part * heads * size + h * size + e] = 1.0
    return order


def norm_parts(x):
    centred = x - jnp.mean(x, axis=-1, keepdims=True)
    scale = lax.rsqrt(jnp.mean(centred * centred, axis=-1, keepdims=True) + norm_epsilon)
    return centred * scale, scale


def norm_back(n, scale, gain, u):
    w = u * gain
    return scale * (
        w - jnp.mean(w, axis=-1, keepdims=True) - n * jnp.mean(w * n, axis=-1, keepdims=True)
    )


def head_blocks(x, masks):
    return jnp.concatenate([x * m for m in masks], axis=0)


def head_diag(r, masks):
    rows = r.shape[0] // 4
    out = r[0:rows] * masks[0]
    for h in range(1, 4):
        out = out + r[h * rows : (h + 1) * rows] * masks[h]
    return out


def head_masks(dtype):
    lane = lax.broadcasted_iota(jnp.int32, (1, 128), 1) // 32
    return [jnp.where(lane == h, 1.0, 0.0).astype(dtype) for h in range(4)]


def row_place(index, count):
    group = index // 2
    quarter = count // 4
    return (group // quarter) * (2 * quarter) + (index % 2) * quarter + group % quarter


def store_rows(ref, values, me, count, at=None):
    piece = values.shape[0] // count
    for p in range(count):
        place = pl.multiple_of(row_place(p ^ me, count) * piece, piece)
        block = values[p * piece : (p + 1) * piece]
        if at is None:
            ref[pl.ds(place, piece)] = block
        else:
            ref[at, pl.ds(place, piece)] = block


def bias_kernel(k0, k1, expand, rel, bias_ref, rows_s):
    size = rel.shape[1]
    tables = jnp.concatenate([k[0:4, 0:256] for k in (k0, k1)], axis=0)
    rows_s[...] = tn(tables, expand[...], precision=highest)
    index = rel[...]
    step = 2 * WIN - 1
    for k in range(2):
        def body(n, acc):
            for m in range(step):
                at = n * step + m
                acc = jnp.where(index == at, rows_s[pl.ds(at, 1), k * size : (k + 1) * size], acc)
            return acc

        bias_ref[k] = lax.fori_loop(0, step, body, jnp.zeros(index.shape, f32))


def mask_kernel(region, mask_ref):
    shape = mask_ref.shape[1:]
    row = lax.broadcasted_iota(jnp.int32, shape, 0)
    col = lax.broadcasted_iota(jnp.int32, shape, 1) % WPAD
    for w in range(4):
        same = region[w] == region[4 + w]
        ok = (row < WIN2) & ((col >= WIN2) | same)
        mask_ref[w] = jnp.where(ok, 0.0, masked_logit)


def attn_forward(scale, count, t_ref, tok, w0, w1, w2, w3, k0, k1, k2, k3, sv, bias_a, bias_b, mask, pick, order, p_out,
                 qkv_out, sht_out, ctx_out, wcol):
    @pl.when(pl.program_id(0) == 0)
    def _():
        for k, w in enumerate((w0, w1, w2, w3)):
            wcol[k] = nn(w[...].astype(bf16), order[...]).astype(bf16)

    n, _ = norm_parts(tok[0].astype(f32))
    normed = (n * sv[0:1] + sv[1:2]).astype(bf16)
    shifted_f = nn(pick[...], normed)
    shifted = shifted_f.astype(bf16)
    store_rows(sht_out, shifted_f.T.astype(bf16), t_ref[1], count, 0)
    low_masks = head_masks(bf16)
    masks = head_masks(f32)
    for k in range(4):
        proj = nn(shifted, wcol[k])
        pack = (k0, k1, k2, k3)[k]
        bias = (bias_a, bias_b)[k // 2][k % 2]
        q = ((proj[:, 0:128] + pack[4:5, 0:128]) * scale).astype(bf16)
        kk = proj[:, 128:256].astype(bf16)
        v = (proj[:, 256:384] + pack[4:5, 128:256]).astype(bf16)
        qkv_out[0, k, :, 0:128] = q
        qkv_out[0, k, :, 128:256] = kk
        qkv_out[0, k, :, 256:384] = v
        spans = [slice(w * WPAD, (w + 1) * WPAD) for w in range(4)]
        logits = [
            nt(kk[rows], head_blocks(q[rows], low_masks)) + (bias + mask[w])
            for w, rows in enumerate(spans)
        ]
        exps = [jnp.exp(x - jnp.max(x, axis=0, keepdims=True)) for x in logits]
        probs = [e * (1.0 / jnp.sum(e, axis=0, keepdims=True)) for e in exps]
        mixes = [tn(p.astype(bf16), v[rows]) for p, rows in zip(probs, spans)]
        for w, p in enumerate(probs):
            p_out[0, k, w] = p
        windows = [head_diag(r, masks).astype(bf16) for r in mixes]
        ctx = jnp.concatenate(windows, axis=0)
        ctx_out[0, 0:LEN, k * 128 : (k + 1) * 128] = tn(pick[...], ctx).astype(bf16)
        ctx_out[0, LEN:ROWS, k * 128 : (k + 1) * 128] = jnp.zeros((ROWS - LEN, 128), bf16)


def hidden_blocks(we, wr, eb, hid_s, act_s, low_s, n2_s, n2t_s, cot_s, cott_s, mix_s, gn2_s, grads,
                  geb_ref):
    rows = hid_s.shape[1]
    chunk = 64

    def body(j, carry):
        hid_s[0] = nn(n2_s[...], we[j])
        hid_s[1] = nt(cot_s[...], wr[j])
        total = None
        for r in range(0, rows, chunk):
            hidden = hid_s[0, r : r + chunk] + eb[j]
            cdf = 0.5 * (1.0 + lax.erf(hidden * (1.0 / math.sqrt(2.0))))
            bell = jnp.exp(-0.5 * hidden * hidden) * (1.0 / math.sqrt(2.0 * math.pi))
            act_s[r : r + chunk] = (hidden * cdf).astype(bf16)
            g_hidden = hid_s[1, r : r + chunk] * (cdf + hidden * bell)
            low_s[r : r + chunk] = g_hidden.astype(bf16)
            total = g_hidden if r == 0 else total + g_hidden
        geb_ref[j] = jnp.sum(total, axis=0, keepdims=True)
        mix_s[...] += nn(act_s[...], wr[j])
        gn2_s[...] += nt(low_s[...], we[j])
        at = pl.multiple_of(lax.rem(j, 2) * 256, 256)
        g_exp = nn(n2t_s[...], low_s[...])
        g_red = nn(cott_s[...], act_s[...])
        for k in range(2):
            @pl.when(j // 2 == k)
            def _(k=k):
                grads[k][:, pl.ds(at, 256)] = g_exp
                grads[k][:, pl.ds(512 + at, 256)] = g_red
        return carry

    lax.fori_loop(0, 4, body, 0)


def load_bias(eb, packs):
    for k, pack in enumerate(packs):
        for half in range(2):
            eb[2 * k + half] = pack[5:6, half * 256 : (half + 1) * 256]


def load_hidden(we, wr, blocks):
    for k, (e, r) in enumerate(blocks):
        for half in range(2):
            we[2 * k + half] = e[:, half * 256 : (half + 1) * 256].astype(bf16)
            wr[2 * k + half] = r[half * 256 : (half + 1) * 256].astype(bf16)


def feed_first(images, count, t_ref, ctx, tok, cot, o0, o1, o2, o3, e0, e1, r0, r1, k0, k1, sv,
               wo, mid_s, n2_s, n2t_s, cot_s, cott_s, mix_s, gn2_s, keep_ref, send_ref, geb_ref,
               we, wr, eb, hid_s, act_s, low_s, x_s):
    rows = x_s.shape[0]
    x_s[...] = jnp.zeros_like(x_s)
    for i in range(images):
        x_s[i * ROWS : i * ROWS + LEN] = tok[i].astype(f32)
    for k, o in enumerate((o0, o1, o2, o3)):
        wo[k * 128 : (k + 1) * 128] = o[...].astype(bf16)
    load_bias(eb, (k0, k1))
    load_hidden(we, wr, ((e0, r0), (e1, r1)))
    attended = jnp.concatenate(
        [ctx[...].reshape(images * ROWS, 512), jnp.zeros((rows - images * ROWS, 512), bf16)], axis=0
    )
    mid_s[...] = x_s[...] + nn(attended, wo[...]) + sv[2:3]
    n2, _ = norm_parts(mid_s[...])
    n2f = n2 * sv[3:4] + sv[4:5]
    n2_s[...] = n2f.astype(bf16)
    store_rows(n2t_s, n2f.T.astype(bf16), t_ref[1], count)
    x_s[...] = jnp.zeros_like(x_s)
    for i in range(images):
        x_s[i * ROWS : i * ROWS + LEN] = cot[i].astype(f32)
    cot_s[...] = x_s[...].astype(bf16)
    store_rows(cott_s, x_s[...].T.astype(bf16), t_ref[1], count)
    mix_s[...] = jnp.zeros_like(mix_s)
    gn2_s[...] = jnp.zeros_like(gn2_s)
    hidden_blocks(
        we, wr, eb, hid_s, act_s, low_s, n2_s, n2t_s, cot_s, cott_s, mix_s, gn2_s,
        (keep_ref, send_ref), geb_ref,
    )


def feed_second(t_ref, e2, e3, r2, r3, k2, k3, n2_s, n2t_s, cot_s, cott_s, mix_in, gn2_in,
                mix_s, gn2_s, keep_ref, send_ref, geb_ref, we, wr, eb, hid_s,
                act_s, low_s):
    load_bias(eb, (k2, k3))
    load_hidden(we, wr, ((e2, r2), (e3, r3)))
    mix_s[...] = mix_in[...]
    gn2_s[...] = gn2_in[...]
    hidden_blocks(
        we, wr, eb, hid_s, act_s, low_s, n2_s, n2t_s, cot_s, cott_s, mix_s, gn2_s,
        (keep_ref, send_ref), geb_ref,
    )


def feed_last(images, count, t_ref, ctx, sv, wo, mid_s, cot_s, mix_s, gn2_s, out_ref, gmid_ref,
              gctx_ref, keep_o, send_o, small_ref, att_t):
    rows = mid_s.shape[0]
    result = mid_s[...] + mix_s[...] + sv[5:6]
    for i in range(images):
        out_ref[i] = result[i * ROWS : i * ROWS + LEN].astype(bf16).astype(f32)
    n2, scale2 = norm_parts(mid_s[...])
    u = gn2_s[...]
    cot = cot_s[...].astype(f32)
    gmid = cot + norm_back(n2, scale2, sv[3:4], u)
    gmid_ref[...] = gmid
    small_ref[0:1] = jnp.sum(gmid, axis=0, keepdims=True)
    small_ref[1:2] = jnp.sum(u * n2, axis=0, keepdims=True)
    small_ref[2:3] = jnp.sum(u, axis=0, keepdims=True)
    small_ref[3:4] = jnp.sum(cot, axis=0, keepdims=True)
    small_ref[4:8] = jnp.zeros((4, 512), f32)
    att_low = gmid.astype(bf16)
    gctx_ref[...] = nt(att_low, wo[...]).astype(bf16)[0 : images * ROWS].reshape(images, ROWS, 512)
    store_rows(att_t, gmid.T.astype(bf16), t_ref[1], count)
    attended = jnp.concatenate(
        [ctx[...].reshape(images * ROWS, 512), jnp.zeros((rows - images * ROWS, 512), bf16)], axis=0
    )
    g_out = nn(att_t[...], attended)
    for k in range(4):
        (keep_o, send_o)[k % 2][k // 2] = g_out[:, k * 128 : (k + 1) * 128]


def attn_backward(scale, p_in, qkv, gctx, sht, pick, order, keep_ref, send_ref, plow_ref, gbias_ref,
                  ghead_ref):
    @pl.when(pl.program_id(0) == 0)
    def _():
        keep_ref[...] = jnp.zeros_like(keep_ref)
        send_ref[...] = jnp.zeros_like(send_ref)
        gbias_ref[...] = jnp.zeros_like(gbias_ref)
        ghead_ref[...] = jnp.zeros_like(ghead_ref)

    gwin = nn(pick[...], gctx[0, 0:LEN]).astype(bf16)
    low_masks = head_masks(bf16)
    masks = head_masks(f32)
    for k in range(4):
        q = qkv[0, k, :, 0:128]
        kk = qkv[0, k, :, 128:256]
        v = qkv[0, k, :, 256:384]
        spans = [slice(w * WPAD, (w + 1) * WPAD) for w in range(4)]
        blocks = [head_blocks(gwin[rows, k * 128 : (k + 1) * 128], low_masks) for rows in spans]
        probs = [p_in[0, k, w] for w in range(4)]
        gps = [nt(v[rows], gbd) for rows, gbd in zip(spans, blocks)]
        gvs = [nn(p.astype(bf16), gbd) for p, gbd in zip(probs, blocks)]
        prods = [p * gp for p, gp in zip(probs, gps)]
        gls = [x - p * jnp.sum(x, axis=0, keepdims=True) for p, x in zip(probs, prods)]
        lows = [gl.astype(bf16) for gl in gls]
        gks = [nn(low, head_blocks(q[rows], low_masks)) for low, rows in zip(lows, spans)]
        gqs = [head_diag(tn(low, kk[rows]), masks) * scale for low, rows in zip(lows, spans)]
        bias_sum = gls[0] + gls[1] + gls[2] + gls[3]
        q_sum = jnp.sum(gqs[0] + gqs[1] + gqs[2] + gqs[3], axis=0, keepdims=True)
        v_sum = jnp.sum(gvs[0] + gvs[1] + gvs[2] + gvs[3], axis=0, keepdims=True)
        parts = [
            jnp.concatenate([gq, gk, gv], axis=1).astype(bf16) for gq, gk, gv in zip(gqs, gks, gvs)
        ]
        gbias_ref[k] += bias_sum
        ghead_ref[k, 0:1] += q_sum
        ghead_ref[k, 1:2] += v_sum
        plow = nt(jnp.concatenate(parts, axis=0), order[...]).astype(bf16)
        (keep_ref, send_ref)[k % 2][k // 2] += nn(sht[0], plow)
        plow_ref[0, k, 0:LEN] = tn(pick[...], plow).astype(bf16)
        plow_ref[0, k, LEN:ROWS] = jnp.zeros((ROWS - LEN, plow.shape[1]), bf16)


def input_backward(t_ref, tok, gmid, plow, w0, w1, w2, w3, sv, out_ref, small_ref, wlow):
    @pl.when(pl.program_id(0) == 0)
    def _():
        small_ref[...] = jnp.zeros_like(small_ref)
        for k, w in enumerate((w0, w1, w2, w3)):
            wlow[k] = w[...].astype(bf16)

    u = nt(plow[0, 0], wlow[0])
    for k in range(1, 4):
        u = u + nt(plow[0, k], wlow[k])
    u = u[0:LEN]
    n, scale = norm_parts(tok[0].astype(f32))
    small_ref[0:1] += jnp.sum(u * n, axis=0, keepdims=True)
    small_ref[1:2] += jnp.sum(u, axis=0, keepdims=True)
    out_ref[0] = gmid[0:LEN] + norm_back(n, scale, sv[0:1], u)


def assemble(t_ref, a0, a1, a2, a3, out):
    for k, a in enumerate((a0, a1, a2, a3)):
        @pl.when(pl.program_id(0) == k)
        def _(a=a):
            out[...] = a[...].astype(out.dtype)


def split_low(x, parts):
    out = []
    for _ in range(parts):
        low = x.astype(bf16)
        out.append(low)
        x = x - low.astype(f32)
    return out


def spread_product(left, right, terms, product=nn):
    total = None
    for i, j in terms:
        part = product(left[i], right[j])
        total = part if total is None else total + part
    return total


def symmetric_product(out, left, right, terms):
    half = out.shape[0] // 2
    top = [x[:half] for x in left]
    bottom = [x[half:] for x in left]
    first = [x[:, :half] for x in right]
    second = [x[:, half:] for x in right]
    out[:half, :half] = spread_product(top, first, terms)
    cross = spread_product(top, second, terms)
    out[:half, half:] = cross
    out[half:, :half] = cross.T
    out[half:, half:] = spread_product(bottom, second, terms)


three_terms = ((1, 0), (0, 1), (0, 0))
six_terms = ((2, 0), (0, 2), (1, 1)) + three_terms


def gram_kernel(spans, flip, t_ref, same, other, g_ref):
    for n, (start, stop) in enumerate(spans):
        a = split_low(same[:, start:stop], 3)
        b = split_low(other[:, start:stop], 3)
        half = same.shape[0]
        place = (t_ref[0] % 2) ^ (n ^ flip)
        for m, (left, right) in enumerate(((a, a), (a, b), (b, b))):
            g_ref[place, :, m * half : (m + 1) * half] = spread_product(left, right, six_terms, nt)


def newton_schulz(t_ref, keep_a, near_a, far_a, keep_i, near_i, far_i, rows_ref, a_s, p_s, t_s, q_s):
    inner = (t_ref[0] == 1) | (t_ref[0] == 2)
    g = jnp.where(
        inner, keep_a[0] + near_a[...] + far_a[...], keep_i[0] + near_i[...] + far_i[...]
    )
    half = g.shape[0]
    size = 2 * half
    cross = g[:, half:size]
    a_s[:half, :half] = g[:, :half]
    a_s[:half, half:] = cross
    a_s[half:, :half] = cross.T
    a_s[half:, half:] = g[:, size:]
    row = lax.broadcasted_iota(jnp.int32, (size, size), 0)
    col = lax.broadcasted_iota(jnp.int32, (size, size), 1)
    eye = jnp.where(row == col, 1.0, 0.0)
    whole = a_s[...]
    inv = 1.0 / (jnp.sum(jnp.sum(whole * eye, axis=0, keepdims=True), axis=1, keepdims=True) + 1e-07)
    a_s[...] = whole * inv
    c0, c1, c2 = quintic_coef
    for step in range(NS_STEPS - 1):
        exact = step < 3
        terms = six_terms if exact else three_terms
        parts = split_low(a_s[...], 3 if exact else 2)
        symmetric_product(t_s, parts, parts, terms)
        p_s[...] = c0 * eye + c1 * a_s[...] + c2 * t_s[...]
        poly = split_low(p_s[...], 3 if exact else 2)
        if step == 0:
            q_s[...] = p_s[...]
        else:
            symmetric_product(q_s, poly, split_low(q_s[...], 2), three_terms)
        symmetric_product(t_s, poly, parts, terms)
        symmetric_product(a_s, poly, split_low(t_s[...], 3 if exact else 2), terms)
    count = rows_ref.shape[0]
    parts = split_low(a_s[...], 2)
    square = spread_product([x[:count] for x in parts], parts, three_terms)
    poly = split_low(c0 * eye[:count] + c1 * a_s[0:count] + c2 * square, 2)
    rows_ref[...] = spread_product(poly, split_low(q_s[...], 2), three_terms) * jnp.sqrt(inv)


def final_kernel(places, factors, t_ref, q0, q1, q2, q3, same_a, other_a, same_i, other_i, u_in,
                 u_exp, u_red, u_out, q_s):
    for k, q in enumerate((q0, q1, q2, q3)):
        q_s[t_ref[0] ^ k] = q[...]
    for m, (group, start, stop) in enumerate(places):
        same = (same_i, same_a)[group][:, start:stop]
        other = (other_i, other_a)[group][:, start:stop]
        half = same.shape[0]
        u = (-matrix_rate * factors[m]) * (
            nn(q_s[m, :, 0:half], same, precision=highest)
            + nn(q_s[m, :, half:], other, precision=highest)
        )
        ref = (u_in, u_exp, u_red, u_out)[m]
        ref[...] = u


def after(value, *earlier):
    return lax.optimization_barrier((value, *earlier))[0]


def xor_tensor(x, k):
    return lax.ppermute(x, "tensor", [(i, i ^ k) for i in range(lax.axis_size("tensor"))])


def xor_dp(x, k):
    return lax.ppermute(x, "dp", [(i, i ^ k) for i in range(lax.axis_size("dp"))])


def gather_tensor(block, *earlier, late=None):
    near = xor_tensor(block, 1)
    far = xor_tensor(after(block, *earlier) if earlier else block, 2)
    return [block, near, far, xor_tensor(far if late is None else after(far, late), 1)]


def scatter_tensor(blocks):
    got = xor_tensor(jnp.stack([blocks[1], blocks[3]]), 1)
    own = blocks[0] + got[0]
    far = blocks[2] + got[1]
    return own + xor_tensor(far, 2)


def first_stage(own, far):
    rows = lax.axis_size("dp") * own.piece
    half, quarter = rows // 2, rows // 4
    return far(0, half), jnp.stack([own(half + quarter, rows), far(half + quarter, rows)])


def second_stage(own, far, got_t, got_d):
    rows = lax.axis_size("dp") * own.piece
    half, quarter = rows // 2, rows // 4
    last = own(quarter, half) + got_t[quarter:]
    return far(half, half + quarter) + got_d[1], last, own(0, quarter) + got_t[:quarter]


def third_stage(own, keep, got_d, last_t, last_d):
    piece = own.piece
    rows = lax.axis_size("dp") * piece
    half, quarter = rows // 2, rows // 4
    pieces = [keep[i : i + piece] + last_d[i : i + piece] for i in range(0, quarter, piece)]
    for i in range(0, quarter, piece):
        start = half + i
        pieces.append(
            own(start, start + piece) + got_d[0, i : i + piece] + last_t[i : i + piece]
        )
    return pieces


class Summed:
    def __init__(self, piece, *groups):
        self.piece = piece
        self.groups = groups

    def __call__(self, start, stop):
        return jnp.concatenate([a[start:stop] + b[start:stop] for a, b in self.groups], axis=1)


def send_groups(pieces):
    return [xor_dp(p, 2 * g) for g, p in enumerate(pieces) if g > 0]


def barrier(*values):
    return lax.optimization_barrier(values)


def join_images(t, parts, dtype):
    images, length, features = parts[0].shape
    return pl.pallas_call(
        assemble,
        grid_spec=pltpu.PrefetchScalarGridSpec(
            num_scalar_prefetch=1,
            grid=(4,),
            in_specs=[pl.BlockSpec((images, length, features), lambda a, t_ref: (0, 0, 0))] * 4,
            out_specs=pl.BlockSpec(
                (images, length, features), lambda a, t_ref: (t_ref[0] ^ a, 0, 0)
            ),
        ),
        out_shape=jax.ShapeDtypeStruct((4 * images, length, features), dtype),
        compiler_params=params(),
        cost_estimate=heavy,
        name="join_images",
    )(t, *parts)


def local(
    tokens,
    cotangent,
    region_ids,
    relative_index,
    shared_vectors,
    input_weight,
    head_bias,
    output_weight,
    expand_weight,
    expand_bias,
    reduce_weight,
    bias_table,
    moment_shared,
    moment_input,
    moment_head,
    moment_output,
    moment_expand,
    moment_bias,
    moment_reduce,
    moment_table,
):
    nt_axis = lax.axis_size("tensor")
    me_t = lax.axis_index("tensor")
    me_d = lax.axis_index("dp")
    nd = lax.axis_size("dp")
    all_images, length, features = tokens.shape
    images = all_images // nt_axis
    heads = bias_table.shape[1]
    head_size = head_bias.shape[1] // heads
    width = heads * head_size
    hidden_here = expand_weight.shape[1]
    table_rows = bias_table.shape[0]
    query_scale = head_size ** (-0.5)
    low_d = me_d % 2
    t_arr = jnp.stack([me_t, me_d, low_d]).astype(jnp.int32)
    rows = -(-images * ROWS // 128) * 128
    lanes = heads * WPAD

    pad_lanes = lambda x: jnp.pad(x, ((0, 0), (0, features - x.shape[1])))
    pack = jnp.concatenate(
        [
            pad_lanes(bias_table.T),
            pad_lanes(head_bias.reshape(1, 2 * width)),
            pad_lanes(expand_bias.reshape(1, hidden_here)),
            jnp.zeros((2, features), f32),
        ]
    )
    packs = [pack, xor_tensor(pack, 1), xor_tensor(pack, 2)]
    w_in = [input_weight, xor_tensor(input_weight, 1)]
    w_in.append(xor_tensor(after(input_weight, pack), 2))
    w_out = [output_weight, xor_tensor(output_weight, 1), xor_tensor(output_weight, 2)]
    w_exp = [expand_weight, xor_tensor(expand_weight, 1)]
    w_red = [reduce_weight, xor_tensor(reduce_weight, 1)]

    pick_np, place_np = window_tables()
    pick = jnp.asarray(pick_np, bf16)
    order = jnp.asarray(column_order(heads, head_size), bf16)
    rel_t = jnp.pad(relative_index.T, ((0, WPAD - WIN2), (0, WPAD - WIN2)), constant_values=-1)
    rel_wide = jnp.tile(rel_t, (1, heads))
    region = region_ids.reshape(2, WIN, 2, WIN).transpose(0, 2, 1, 3).reshape(4, WIN2)
    region = jnp.pad(region, ((0, 0), (0, WPAD - WIN2)))
    region_both = jnp.concatenate(
        [
            jnp.broadcast_to(region[:, :, None], (4, WPAD, lanes)),
            jnp.broadcast_to(jnp.tile(region, (1, heads))[:, None, :], (4, WPAD, lanes)),
        ]
    )
    spread = np.zeros((2 * heads, 2 * lanes), np.float32)
    for h in range(2 * heads):
        spread[h, h * WPAD : (h + 1) * WPAD] = 1.0
    sds = jax.ShapeDtypeStruct
    pack_spec = pl.BlockSpec((8, features), lambda i, *_: (0, 0))

    def bias_of(blocks):
        return pl.pallas_call(
            bias_kernel,
            grid=(1,),
            in_specs=[pack_spec] * 2
            + [
                pl.BlockSpec((2 * heads, 2 * lanes), lambda i: (0, 0)),
                pl.BlockSpec((WPAD, lanes), lambda i: (0, 0)),
            ],
            out_specs=pl.BlockSpec((2, WPAD, lanes), lambda i: (0, 0, 0)),
            out_shape=sds((2, WPAD, lanes), f32),
            scratch_shapes=[pltpu.VMEM((256, 2 * lanes), f32)],
            compiler_params=params(),
            cost_estimate=light,
            name="bias",
        )(*blocks, jnp.asarray(spread), rel_wide)

    mask = pl.pallas_call(
        mask_kernel,
        in_specs=[VMEM],
        out_specs=VMEM,
        out_shape=sds((4, WPAD, lanes), f32),
        compiler_params=params(),
        cost_estimate=light,
        name="mask",
    )(region_both)
    bias_a = bias_of(packs[:2])
    piece = features // nd
    row_at = me_d * piece
    moment_a = jnp.concatenate(
        [
            lax.dynamic_slice_in_dim(moment_expand, row_at, piece, 0),
            lax.dynamic_slice_in_dim(moment_reduce, row_at, piece, 1).T,
        ],
        axis=1,
    )
    moment_i = jnp.concatenate(
        [
            lax.dynamic_slice_in_dim(moment_input, row_at, piece, 0),
            lax.dynamic_slice_in_dim(moment_output, row_at, piece, 1).T,
        ],
        axis=1,
    )
    packs.append(xor_tensor(packs[2], 1))
    bias_b = bias_of(packs[2:])
    w_in[2], w_out[2], bias_a, bias_b, mask, moment_a, moment_i = barrier(
        w_in[2], w_out[2], bias_a, bias_b, mask, moment_a, moment_i
    )
    w_in.append(xor_tensor(w_in[2], 1))
    w_out.append(xor_tensor(w_out[2], 1))
    far_exp = xor_tensor(after(expand_weight, bias_b), 2)
    far_red = xor_tensor(after(reduce_weight, w_in[2]), 2)

    whole = lambda *shape: pl.BlockSpec(shape, lambda i, *_: (0,) * len(shape))
    one = lambda *shape: pl.BlockSpec((1,) + shape, lambda i, *_: (i,) + (0,) * len(shape))
    tok_one = pl.BlockSpec((1, length, features), lambda i, t: (t[0] * images + i, 0, 0))
    probs, qkv, sht, ctx = pl.pallas_call(
        functools.partial(attn_forward, query_scale, nd),
        grid_spec=pltpu.PrefetchScalarGridSpec(
            num_scalar_prefetch=1,
            grid=(images,),
            in_specs=[tok_one]
            + [whole(features, 3 * width)] * 4
            + [pack_spec] * 4
            + [
                whole(6, features),
                whole(2, WPAD, lanes),
                whole(2, WPAD, lanes),
                whole(4, WPAD, lanes),
                whole(WROWS, LEN),
                whole(3 * width, 3 * width),
            ],
            out_specs=[
                one(4, 4, WPAD, lanes),
                one(4, WROWS, 3 * width),
                one(features, WROWS),
                one(ROWS, 4 * width),
            ],
            scratch_shapes=[pltpu.VMEM((4, features, 3 * width), bf16)],
        ),
        out_shape=[
            sds((images, 4, 4, WPAD, lanes), f32),
            sds((images, 4, WROWS, 3 * width), bf16),
            sds((images, features, WROWS), bf16),
            sds((images, ROWS, 4 * width), bf16),
        ],
        compiler_params=params(),
        cost_estimate=heavy,
        name="attn_forward",
    )(t_arr, tokens, *w_in, *packs, shared_vectors, bias_a, bias_b, mask, pick, order)

    tok_all = pl.BlockSpec((images, length, features), lambda i, t: (t[0], 0, 0))
    token_f = (rows, features)
    wide = 2 * hidden_here
    hidden_scratch = [
        pltpu.VMEM((4, features, hidden_here // 2), bf16),
        pltpu.VMEM((4, hidden_here // 2, features), bf16),
        pltpu.VMEM((4, 1, hidden_here // 2), f32),
        pltpu.VMEM((2, rows, hidden_here // 2), f32),
        pltpu.VMEM((rows, hidden_here // 2), bf16),
        pltpu.VMEM((rows, hidden_here // 2), bf16),
    ]
    state_shapes = [
        ((4 * width, features), bf16),
        (token_f, f32),
        (token_f, bf16),
        (token_f[::-1], bf16),
        (token_f, bf16),
        (token_f[::-1], bf16),
        (token_f, f32),
        (token_f, f32),
    ]
    *carry, keep_0, send_1, geb_a = pl.pallas_call(
        functools.partial(feed_first, images, nd),
        grid_spec=pltpu.PrefetchScalarGridSpec(
            num_scalar_prefetch=1,
            grid=(1,),
            in_specs=[whole(images, ROWS, 4 * width), tok_all, tok_all]
            + [whole(width, features)] * 4
            + [whole(features, hidden_here)] * 2
            + [whole(hidden_here, features)] * 2
            + [pack_spec] * 2
            + [whole(6, features)],
            out_specs=[whole(*shape) for shape, _ in state_shapes]
            + [whole(features, wide), whole(features, wide), whole(4, 1, hidden_here // 2)],
            scratch_shapes=hidden_scratch + [pltpu.VMEM(token_f, f32)],
        ),
        out_shape=[sds(shape, dtype) for shape, dtype in state_shapes]
        + [sds((features, wide), f32)] * 2
        + [sds((4, 1, hidden_here // 2), f32)],
        compiler_params=params(),
        cost_estimate=heavy,
        name="feed_first",
    )(t_arr, ctx, tokens, cotangent, *w_out, *w_exp, *w_red, *packs[:2], shared_vectors)

    far_exp = after(far_exp, geb_a)
    w_exp += [far_exp, xor_tensor(far_exp, 1)]
    far_red = after(far_red, geb_a)
    w_red += [far_red, xor_tensor(far_red, 1)]
    got_1 = xor_tensor(send_1, 1)

    wo_low, mid, n2_low, n2_t, cot_low, cot_t, mix, gn2 = carry
    mix, gn2, keep_2, send_3, geb_b = pl.pallas_call(
        feed_second,
        grid_spec=pltpu.PrefetchScalarGridSpec(
            num_scalar_prefetch=1,
            grid=(1,),
            in_specs=[whole(features, hidden_here)] * 2
            + [whole(hidden_here, features)] * 2
            + [pack_spec] * 2
            + [whole(*shape) for shape, _ in state_shapes[2:]],
            out_specs=[
                whole(rows, features),
                whole(rows, features),
                whole(features, wide),
                whole(features, wide),
                whole(4, 1, hidden_here // 2),
            ],
            scratch_shapes=hidden_scratch,
        ),
        out_shape=[
            sds((rows, features), f32),
            sds((rows, features), f32),
            sds((features, wide), f32),
            sds((features, wide), f32),
            sds((4, 1, hidden_here // 2), f32),
        ],
        compiler_params=params(),
        cost_estimate=light,
        name="feed_second",
    )(
        t_arr,
        *w_exp[2:],
        *w_red[2:],
        *packs[2:],
        n2_low,
        n2_t,
        cot_low,
        cot_t,
        mix,
        gn2,
    )
    got_3 = xor_tensor(send_3, 1)

    block_part, gmid, gctx, keep_o, send_o, small_a = pl.pallas_call(
        functools.partial(feed_last, images, nd),
        grid_spec=pltpu.PrefetchScalarGridSpec(
            num_scalar_prefetch=1,
            grid=(1,),
            in_specs=[
                whole(images, ROWS, 4 * width),
                whole(6, features),
                whole(4 * width, features),
            ]
            + [whole(rows, features)] * 4,
            out_specs=[
                whole(images, length, features),
                whole(rows, features),
                whole(images, ROWS, 4 * width),
                whole(2, features, width),
                whole(2, features, width),
                whole(8, features),
            ],
            scratch_shapes=[pltpu.VMEM(token_f[::-1], bf16)],
        ),
        out_shape=[
            sds((images, length, features), f32),
            sds((rows, features), f32),
            sds((images, ROWS, 4 * width), bf16),
            sds((2, features, width), f32),
            sds((2, features, width), f32),
            sds((8, features), f32),
        ],
        compiler_params=params(),
        cost_estimate=light,
        name="feed_last",
    )(t_arr, ctx, shared_vectors, wo_low, mid, cot_low, mix, gn2)

    got_o = xor_tensor(send_o, 1)
    got_3, gctx = barrier(got_3, gctx)
    own_a = Summed(piece, (keep_0, got_1))
    far_a = Summed(piece, (keep_2, got_3))
    t1_a, d1_a = first_stage(own_a, far_a)
    gctx, t1_a, d1_a = barrier(gctx, t1_a, d1_a)
    got_t1_a, got_d1_a = xor_tensor(t1_a, 2), xor_dp(d1_a, 1)

    keep_i, send_i, plow, gbias, ghead = pl.pallas_call(
        functools.partial(attn_backward, query_scale),
        grid=(images,),
        in_specs=[
            one(4, 4, WPAD, lanes),
            one(4, WROWS, 3 * width),
            one(ROWS, 4 * width),
            one(features, WROWS),
            whole(WROWS, LEN),
            whole(3 * width, 3 * width),
        ],
        out_specs=[
            whole(2, features, 3 * width),
            whole(2, features, 3 * width),
            one(4, ROWS, 3 * width),
            whole(4, WPAD, lanes),
            whole(4, 2, width),
        ],
        out_shape=[
            sds((2, features, 3 * width), f32),
            sds((2, features, 3 * width), f32),
            sds((images, 4, ROWS, 3 * width), bf16),
            sds((4, WPAD, lanes), f32),
            sds((4, 2, width), f32),
        ],
        compiler_params=params(),
        cost_estimate=light,
        name="attn_backward",
    )(probs, qkv, gctx, sht, pick, order)

    got_i = xor_tensor(send_i, 1)

    grad_part, small_i = pl.pallas_call(
        input_backward,
        grid_spec=pltpu.PrefetchScalarGridSpec(
            num_scalar_prefetch=1,
            grid=(images,),
            in_specs=[
                tok_one,
                pl.BlockSpec((ROWS, features), lambda i, t: (i, 0)),
                one(4, ROWS, 3 * width),
            ]
            + [whole(features, 3 * width)] * 4
            + [whole(6, features)],
            out_specs=[one(length, features), whole(8, features)],
            scratch_shapes=[pltpu.VMEM((4, features, 3 * width), bf16)],
        ),
        out_shape=[sds((images, length, features), f32), sds((8, features), f32)],
        compiler_params=params(),
        cost_estimate=light,
        name="input_backward",
    )(t_arr, tokens, gmid, plow, *w_in, shared_vectors)

    got_t1_a, got_d1_a, send_small_i = barrier(got_t1_a, got_d1_a, small_i)
    small_i = send_small_i
    t2_a, d2_a, kept_a = second_stage(own_a, far_a, got_t1_a, got_d1_a)
    got_t2_a, got_d2_a = xor_tensor(t2_a, 2), xor_dp(d2_a, 1)
    got_i = barrier(got_i, t2_a, d2_a)[0]
    own_i = Summed(piece, (keep_i[0], got_i[0]), (keep_o[0], got_o[0]))
    far_i = Summed(piece, (keep_i[1], got_i[1]), (keep_o[1], got_o[1]))
    t1_i, d1_i = first_stage(own_i, far_i)
    got_t1_i, got_d1_i = xor_tensor(t1_i, 2), xor_dp(d1_i, 1)
    got_t2_a, got_d2_a, t1_i, d1_i = barrier(got_t2_a, got_d2_a, t1_i, d1_i)
    pieces_a = third_stage(own_a, kept_a, got_d1_a, got_t2_a, got_d2_a)
    got_a = send_groups(pieces_a)
    block_part = after(block_part, *pieces_a)
    block_parts = [block_part, xor_tensor(block_part, 1), xor_tensor(block_part, 2)]
    got_t1_i, got_d1_i, far_block = barrier(got_t1_i, got_d1_i, block_parts[2], *got_a)[:3]
    block_parts = [block_parts[0], block_parts[1], far_block, xor_tensor(far_block, 1)]
    t2_i, d2_i, kept_i = second_stage(own_i, far_i, got_t1_i, got_d1_i)
    got_t2_i, got_d2_i = xor_tensor(t2_i, 2), xor_dp(d2_i, 1)
    gbias, ghead, small_i, geb_a, geb_b, small_a = barrier(
        gbias, ghead, small_i, geb_a, geb_b, small_a, *pieces_a
    )[:6]

    pick_table = (
        jnp.arange(table_rows)[:, None] == rel_t[:WIN2].reshape(1, -1)
    ).astype(f32)
    gb = gbias[:, :WIN2].reshape(4, WIN2, heads, WPAD).transpose(0, 2, 1, 3)
    gtable = lax.dot_general(
        gb.reshape(4 * heads, -1), pick_table, (((1,), (1,)), ((), ())), precision=highest
    ).reshape(4, heads * table_rows)
    shared_rows = jnp.concatenate([small_i[0:2], small_a[0:4]])
    geb = jnp.concatenate([geb_a, geb_b]).reshape(4, hidden_here)
    block_small = jnp.concatenate([gtable, ghead.reshape(4, -1), geb], axis=1)
    n_small = block_small.shape[1]
    small_send = jnp.concatenate([block_small[1], block_small[3], shared_rows.reshape(-1)])
    got_small = xor_tensor(small_send, 1)
    got_a = barrier(*got_a, small_send)[: len(got_a)]
    grad_scale = (all_images * length * nd) ** (-0.5)
    grad_a = sum(got_a, pieces_a[0]) * grad_scale
    state_a = moment_decay * moment_a + (1.0 - moment_decay) * grad_a
    same_a = [state_a] + send_groups([state_a] * (nd // 2))
    got_small = barrier(got_small, *got_a)[0]
    own_small = block_small[0] + got_small[:n_small]
    far_small = block_small[2] + got_small[n_small : 2 * n_small]
    shared_sum = shared_rows.reshape(-1) + got_small[2 * n_small :]
    small_send = jnp.concatenate([far_small, shared_sum])
    got_small = xor_tensor(small_send, 2)
    got_small = barrier(got_small, t2_i, d2_i, state_a)[0]
    vector = jnp.concatenate([own_small, shared_sum]) + got_small
    got_small = xor_dp(vector, 1)
    *same_a, got_t2_i, got_d2_i, got_small = barrier(*same_a, got_t2_i, got_d2_i, got_small)
    same_a = jnp.concatenate(same_a)
    other_a = xor_dp(same_a, 1)
    vector = vector + got_small
    small_parts = send_groups([vector] * (nd // 2))
    grad_part = after(grad_part, same_a)
    grad_parts = [grad_part, xor_tensor(grad_part, 1), xor_tensor(grad_part, 2)]
    got_t2_i, got_d2_i = barrier(got_t2_i, got_d2_i, same_a)[:2]
    pieces_i = third_stage(own_i, kept_i, got_d1_i, got_t2_i, got_d2_i)
    got_i = send_groups(pieces_i)
    grad_i = sum(got_i, pieces_i[0]) * grad_scale
    state_i = moment_decay * moment_i + (1.0 - moment_decay) * grad_i
    same_i = [state_i] + send_groups([state_i] * (nd // 2))
    other_a = after(other_a, state_i)
    vector = sum(barrier(*small_parts, state_i)[: len(small_parts)], vector)
    block_parts[1], block_parts[3] = barrier(block_parts[1], block_parts[3], state_i)[:2]
    block_out = join_images(t_arr, block_parts, bf16)

    places = [
        (0, 0, 3 * width),
        (1, 0, hidden_here),
        (1, hidden_here, wide),
        (0, 3 * width, 4 * width),
    ]
    half = features // 2
    scalars = pl.BlockSpec(memory_space=pltpu.SMEM)

    def grams(group, *operands):
        spans = [(b, c) for a, b, c in places if a == group]
        return pl.pallas_call(
            functools.partial(gram_kernel, spans, group),
            in_specs=[scalars] + [VMEM] * 2,
            out_specs=VMEM,
            out_shape=sds((2, half, 3 * half), f32),
            compiler_params=params(),
            cost_estimate=heavy,
            name="gram",
        )(t_arr, *operands)

    gram_a = grams(1, same_a, other_a)
    near_a = xor_tensor(gram_a[1], 1)
    same_i = jnp.concatenate(barrier(*same_i, block_out)[: len(same_i)])
    other_i = xor_dp(same_i, 1)
    near_a = barrier(near_a, same_i)[0]
    send_far = gram_a[0] + near_a
    far_a = lax.ppermute(send_far, "tensor", [(0, 2), (3, 1)])
    other_i, grad_far = barrier(other_i, grad_parts[2], send_far)[:2]
    gram_i = grams(0, same_i, other_i)
    near_i = xor_tensor(gram_i[1], 1)
    grad_far = after(grad_far, gram_i)
    grad_last = xor_tensor(grad_far, 1)
    near_i, far_a = barrier(near_i, far_a)
    far_i = lax.ppermute(gram_i[0] + near_i, "tensor", [(2, 0), (1, 3)])
    grad_near, grad_last = barrier(grad_parts[1], grad_last, near_i)[:2]
    input_grad = join_images(t_arr, [grad_parts[0], grad_near, grad_far, grad_last], f32)
    far_i = barrier(far_i, input_grad)[0]
    own_rows = pl.pallas_call(
        newton_schulz,
        in_specs=[scalars] + [VMEM] * 6,
        out_specs=VMEM,
        out_shape=sds((piece, features), f32),
        scratch_shapes=[pltpu.VMEM((features, features), f32)] * 4,
        compiler_params=params(),
        cost_estimate=light,
        name="newton_schulz",
    )(t_arr, gram_a, near_a, far_a, gram_i, near_i, far_i)
    near_rows = xor_tensor(own_rows, 1)
    far_rows = xor_tensor(own_rows, 2)
    factor = lambda a, b: math.sqrt(max(1.0, a / b))
    update_m = pl.pallas_call(
        functools.partial(
            final_kernel,
            places,
            [
                factor(features, 3 * width * nt_axis),
                factor(features, hidden_here * nt_axis),
                factor(hidden_here * nt_axis, features),
                factor(width * nt_axis, features),
            ],
        ),
        in_specs=[scalars] + [VMEM] * 8,
        out_specs=[VMEM] * 4,
        out_shape=[
            sds((piece, 3 * width), f32),
            sds((piece, hidden_here), f32),
            sds((piece, hidden_here), f32),
            sds((piece, width), f32),
        ],
        scratch_shapes=[pltpu.VMEM((4, piece, features), f32)],
        compiler_params=params(),
        cost_estimate=light,
        name="update",
    )(
        t_arr,
        own_rows,
        near_rows,
        far_rows,
        xor_tensor(far_rows, 1),
        same_a,
        other_a,
        same_i,
        other_i,
    )
    update_m = (update_m[0], update_m[3].T, update_m[1], update_m[2].T)

    vector = after(vector, near_i)
    at = heads * table_rows
    gradients = {
        "table": vector[:at].reshape(heads, table_rows).T,
        "head": vector[at : at + 2 * width].reshape(2, width),
        "bias": vector[at + 2 * width : n_small],
        "shared": vector[n_small:].reshape(6, features),
    }
    moments = dict(table=moment_table, head=moment_head, bias=moment_bias, shared=moment_shared)
    gradients = {k: v * grad_scale for k, v in gradients.items()}
    states = {
        k: moment_decay * moments[k] + (1.0 - moment_decay) * gradients[k] for k in gradients
    }

    def split(part_i, part_a):
        a, b, c, d = [(part_i, part_a)[g][:, s:e] for g, s, e in places]
        return a, d.T, b, c.T

    grad_m = split(grad_i, grad_a)
    state_m = split(state_i, state_a)
    return (
        block_out,
        input_grad,
        gradients["shared"],
        grad_m[0],
        gradients["head"],
        grad_m[1],
        grad_m[2],
        gradients["bias"],
        grad_m[3],
        gradients["table"],
        -vector_rate * states["shared"],
        update_m[0],
        -vector_rate * states["head"],
        update_m[1],
        update_m[2],
        -vector_rate * states["bias"],
        update_m[3],
        -vector_rate * states["table"],
        states["shared"],
        state_m[0],
        states["head"],
        state_m[1],
        state_m[2],
        states["bias"],
        state_m[3],
        states["table"],
    )


def solution(mesh):
    return jax.shard_map(
        local,
        mesh=mesh,
        in_specs=(
            P("dp", None, None),
            P("dp", None, None),
            P(),
            P(),
            P(),
            P(None, "tensor"),
            P(None, "tensor"),
            P("tensor", None),
            P(None, "tensor"),
            P("tensor"),
            P("tensor", None),
            P(None, "tensor"),
            P(),
            P(None, "tensor"),
            P(None, "tensor"),
            P("tensor", None),
            P(None, "tensor"),
            P("tensor"),
            P("tensor", None),
            P(None, "tensor"),
        ),
        out_specs=(
            P("dp", None, None),
            P("dp", None, None),
            P(),
            P("dp", "tensor"),
            P(None, "tensor"),
            P("tensor", "dp"),
            P("dp", "tensor"),
            P("tensor"),
            P("tensor", "dp"),
            P(None, "tensor"),
            P(),
            P("dp", "tensor"),
            P(None, "tensor"),
            P("tensor", "dp"),
            P("dp", "tensor"),
            P("tensor"),
            P("tensor", "dp"),
            P(None, "tensor"),
            P(),
            P("dp", "tensor"),
            P(None, "tensor"),
            P("tensor", "dp"),
            P("dp", "tensor"),
            P("tensor"),
            P("tensor", "dp"),
            P(None, "tensor"),
        ),
        check_vma=False,
    )
```

```python
import functools
import math

import jax
import jax.numpy as jnp
import numpy as np
from jax import lax
from jax.experimental import pallas as pl
from jax.experimental.pallas import tpu as pltpu
from jax.sharding import PartitionSpec as P

SIDE = 14
WIN = 7
SHIFT = 3
NS_STEPS = 5
WIN2 = WIN * WIN
LEN = SIDE * SIDE
TABLE = (2 * WIN - 1) ** 2
ROWS = 208
WPAD = 64
WROWS = 4 * WPAD

highest = lax.Precision.HIGHEST
norm_epsilon = 1e-05
moment_decay = 0.8
matrix_rate = 1.0
vector_rate = 1.0
quintic_coef = (3.4445, -4.775, 2.0315)
masked_logit = -1e30
f32 = jnp.float32
bf16 = jnp.bfloat16
VMEM = pl.BlockSpec(memory_space=pltpu.VMEM)
light = pl.CostEstimate(flops=1000, bytes_accessed=1000, transcendentals=0)
heavy = pl.CostEstimate(flops=10_000_000_000, bytes_accessed=10_000_000, transcendentals=0)


def params(limit_mib=56, **kw):
    return pltpu.CompilerParams(vmem_limit_bytes=limit_mib * 1024 * 1024, **kw)


def nn(a, b, **kw):
    return lax.dot_general(a, b, (((1,), (0,)), ((), ())), preferred_element_type=f32, **kw)


def nt(a, b, **kw):
    return lax.dot_general(a, b, (((1,), (1,)), ((), ())), preferred_element_type=f32, **kw)


def tn(a, b, **kw):
    return lax.dot_general(a, b, (((0,), (0,)), ((), ())), preferred_element_type=f32, **kw)


def window_tables():
    pick = np.zeros((WROWS, LEN), np.float32)
    place = np.zeros((4, WIN2), np.int32)
    for r in range(SIDE):
        for c in range(SIDE):
            w = (r // WIN) * 2 + c // WIN
            i = (r % WIN) * WIN + c % WIN
            source = ((r + SHIFT) % SIDE) * SIDE + (c + SHIFT) % SIDE
            pick[w * WPAD + i, source] = 1.0
            place[w, i] = r * SIDE + c
    return pick, place


def column_order(heads, size):
    width = 3 * heads * size
    order = np.zeros((width, width), np.float32)
    for h in range(heads):
        for part in range(3):
            for e in range(size):
                order[(h * 3 + part) * size + e, part * heads * size + h * size + e] = 1.0
    return order


def norm_parts(x):
    centred = x - jnp.mean(x, axis=-1, keepdims=True)
    scale = lax.rsqrt(jnp.mean(centred * centred, axis=-1, keepdims=True) + norm_epsilon)
    return centred * scale, scale


def norm_back(n, scale, gain, u):
    w = u * gain
    return scale * (
        w - jnp.mean(w, axis=-1, keepdims=True) - n * jnp.mean(w * n, axis=-1, keepdims=True)
    )


def head_blocks(x, masks):
    return jnp.concatenate([x * m for m in masks], axis=0)


def head_diag(r, masks):
    rows = r.shape[0] // 4
    out = r[0:rows] * masks[0]
    for h in range(1, 4):
        out = out + r[h * rows : (h + 1) * rows] * masks[h]
    return out


def head_masks(dtype):
    lane = lax.broadcasted_iota(jnp.int32, (1, 128), 1) // 32
    return [jnp.where(lane == h, 1.0, 0.0).astype(dtype) for h in range(4)]


def row_place(index, count):
    group = index // 2
    quarter = count // 4
    return (group // quarter) * (2 * quarter) + (index % 2) * quarter + group % quarter


def store_rows(ref, values, me, count, at=None):
    piece = values.shape[0] // count
    for p in range(count):
        place = pl.multiple_of(row_place(p ^ me, count) * piece, piece)
        block = values[p * piece : (p + 1) * piece]
        if at is None:
            ref[pl.ds(place, piece)] = block
        else:
            ref[at, pl.ds(place, piece)] = block


def bias_kernel(k0, k1, expand, rel, bias_ref, rows_s):
    size = rel.shape[1]
    tables = jnp.concatenate([k[0:4, 0:256] for k in (k0, k1)], axis=0)
    rows_s[...] = tn(tables, expand[...], precision=highest)
    index = rel[...]
    step = 2 * WIN - 1
    for k in range(2):
        def body(n, acc):
            for m in range(step):
                at = n * step + m
                acc = jnp.where(index == at, rows_s[pl.ds(at, 1), k * size : (k + 1) * size], acc)
            return acc

        bias_ref[k] = lax.fori_loop(0, step, body, jnp.zeros(index.shape, f32))


def mask_kernel(region, mask_ref):
    shape = mask_ref.shape[1:]
    row = lax.broadcasted_iota(jnp.int32, shape, 0)
    col = lax.broadcasted_iota(jnp.int32, shape, 1) % WPAD
    for w in range(4):
        same = region[w] == region[4 + w]
        ok = (row < WIN2) & ((col >= WIN2) | same)
        mask_ref[w] = jnp.where(ok, 0.0, masked_logit)


def attn_forward(scale, count, t_ref, tok, w0, w1, w2, w3, k0, k1, k2, k3, sv, bias_a, bias_b, mask, pick, order, p_out,
                 qkv_out, sht_out, ctx_out, wcol):
    @pl.when(pl.program_id(0) == 0)
    def _():
        for k, w in enumerate((w0, w1, w2, w3)):
            wcol[k] = nn(w[...].astype(bf16), order[...]).astype(bf16)

    n, _ = norm_parts(tok[0].astype(f32))
    normed = (n * sv[0:1] + sv[1:2]).astype(bf16)
    shifted_f = nn(pick[...], normed)
    shifted = shifted_f.astype(bf16)
    store_rows(sht_out, shifted_f.T.astype(bf16), t_ref[1], count, 0)
    low_masks = head_masks(bf16)
    masks = head_masks(f32)
    for k in range(4):
        proj = nn(shifted, wcol[k])
        pack = (k0, k1, k2, k3)[k]
        bias = (bias_a, bias_b)[k // 2][k % 2]
        q = ((proj[:, 0:128] + pack[4:5, 0:128]) * scale).astype(bf16)
        kk = proj[:, 128:256].astype(bf16)
        v = (proj[:, 256:384] + pack[4:5, 128:256]).astype(bf16)
        qkv_out[0, k, :, 0:128] = q
        qkv_out[0, k, :, 128:256] = kk
        qkv_out[0, k, :, 256:384] = v
        spans = [slice(w * WPAD, (w + 1) * WPAD) for w in range(4)]
        logits = [
            nt(kk[rows], head_blocks(q[rows], low_masks)) + (bias + mask[w])
            for w, rows in enumerate(spans)
        ]
        exps = [jnp.exp(x - jnp.max(x, axis=0, keepdims=True)) for x in logits]
        probs = [e * (1.0 / jnp.sum(e, axis=0, keepdims=True)) for e in exps]
        mixes = [tn(p.astype(bf16), v[rows]) for p, rows in zip(probs, spans)]
        for w, p in enumerate(probs):
            p_out[0, k, w] = p
        windows = [head_diag(r, masks).astype(bf16) for r in mixes]
        ctx = jnp.concatenate(windows, axis=0)
        ctx_out[0, 0:LEN, k * 128 : (k + 1) * 128] = tn(pick[...], ctx).astype(bf16)
        ctx_out[0, LEN:ROWS, k * 128 : (k + 1) * 128] = jnp.zeros((ROWS - LEN, 128), bf16)


def hidden_blocks(we, wr, eb, hid_s, act_s, low_s, n2_s, n2t_s, cot_s, cott_s, mix_s, gn2_s, grads,
                  geb_ref):
    rows = hid_s.shape[1]
    chunk = 64

    def body(j, carry):
        hid_s[0] = nn(n2_s[...], we[j])
        hid_s[1] = nt(cot_s[...], wr[j])
        total = None
        for r in range(0, rows, chunk):
            hidden = hid_s[0, r : r + chunk] + eb[j]
            cdf = 0.5 * (1.0 + lax.erf(hidden * (1.0 / math.sqrt(2.0))))
            bell = jnp.exp(-0.5 * hidden * hidden) * (1.0 / math.sqrt(2.0 * math.pi))
            act_s[r : r + chunk] = (hidden * cdf).astype(bf16)
            g_hidden = hid_s[1, r : r + chunk] * (cdf + hidden * bell)
            low_s[r : r + chunk] = g_hidden.astype(bf16)
            total = g_hidden if r == 0 else total + g_hidden
        geb_ref[j] = jnp.sum(total, axis=0, keepdims=True)
        mix_s[...] += nn(act_s[...], wr[j])
        gn2_s[...] += nt(low_s[...], we[j])
        at = pl.multiple_of(lax.rem(j, 2) * 256, 256)
        g_exp = nn(n2t_s[...], low_s[...])
        g_red = nn(cott_s[...], act_s[...])
        for k in range(2):
            @pl.when(j // 2 == k)
            def _(k=k):
                grads[k][:, pl.ds(at, 256)] = g_exp
                grads[k][:, pl.ds(512 + at, 256)] = g_red
        return carry

    lax.fori_loop(0, 4, body, 0)


def load_bias(eb, packs):
    for k, pack in enumerate(packs):
        for half in range(2):
            eb[2 * k + half] = pack[5:6, half * 256 : (half + 1) * 256]


def load_hidden(we, wr, blocks):
    for k, (e, r) in enumerate(blocks):
        for half in range(2):
            we[2 * k + half] = e[:, half * 256 : (half + 1) * 256].astype(bf16)
            wr[2 * k + half] = r[half * 256 : (half + 1) * 256].astype(bf16)


def feed_first(images, count, t_ref, ctx, tok, cot, o0, o1, o2, o3, e0, e1, r0, r1, k0, k1, sv,
               wo, mid_s, n2_s, n2t_s, cot_s, cott_s, mix_s, gn2_s, keep_ref, send_ref, geb_ref,
               we, wr, eb, hid_s, act_s, low_s, x_s):
    rows = x_s.shape[0]
    x_s[...] = jnp.zeros_like(x_s)
    for i in range(images):
        x_s[i * ROWS : i * ROWS + LEN] = tok[i].astype(f32)
    for k, o in enumerate((o0, o1, o2, o3)):
        wo[k * 128 : (k + 1) * 128] = o[...].astype(bf16)
    load_bias(eb, (k0, k1))
    load_hidden(we, wr, ((e0, r0), (e1, r1)))
    attended = jnp.concatenate(
        [ctx[...].reshape(images * ROWS, 512), jnp.zeros((rows - images * ROWS, 512), bf16)], axis=0
    )
    mid_s[...] = x_s[...] + nn(attended, wo[...]) + sv[2:3]
    n2, _ = norm_parts(mid_s[...])
    n2f = n2 * sv[3:4] + sv[4:5]
    n2_s[...] = n2f.astype(bf16)
    store_rows(n2t_s, n2f.T.astype(bf16), t_ref[1], count)
    x_s[...] = jnp.zeros_like(x_s)
    for i in range(images):
        x_s[i * ROWS : i * ROWS + LEN] = cot[i].astype(f32)
    cot_s[...] = x_s[...].astype(bf16)
    store_rows(cott_s, x_s[...].T.astype(bf16), t_ref[1], count)
    mix_s[...] = jnp.zeros_like(mix_s)
    gn2_s[...] = jnp.zeros_like(gn2_s)
    hidden_blocks(
        we, wr, eb, hid_s, act_s, low_s, n2_s, n2t_s, cot_s, cott_s, mix_s, gn2_s,
        (keep_ref, send_ref), geb_ref,
    )


def feed_second(t_ref, e2, e3, r2, r3, k2, k3, n2_s, n2t_s, cot_s, cott_s, mix_in, gn2_in,
                mix_s, gn2_s, keep_ref, send_ref, geb_ref, we, wr, eb, hid_s,
                act_s, low_s):
    load_bias(eb, (k2, k3))
    load_hidden(we, wr, ((e2, r2), (e3, r3)))
    mix_s[...] = mix_in[...]
    gn2_s[...] = gn2_in[...]
    hidden_blocks(
        we, wr, eb, hid_s, act_s, low_s, n2_s, n2t_s, cot_s, cott_s, mix_s, gn2_s,
        (keep_ref, send_ref), geb_ref,
    )


def feed_last(images, count, t_ref, ctx, sv, wo, mid_s, cot_s, mix_s, gn2_s, out_ref, gmid_ref,
              gctx_ref, keep_o, send_o, small_ref, att_t):
    rows = mid_s.shape[0]
    result = mid_s[...] + mix_s[...] + sv[5:6]
    for i in range(images):
        out_ref[i] = result[i * ROWS : i * ROWS + LEN].astype(bf16).astype(f32)
    n2, scale2 = norm_parts(mid_s[...])
    u = gn2_s[...]
    cot = cot_s[...].astype(f32)
    gmid = cot + norm_back(n2, scale2, sv[3:4], u)
    gmid_ref[...] = gmid
    small_ref[0:1] = jnp.sum(gmid, axis=0, keepdims=True)
    small_ref[1:2] = jnp.sum(u * n2, axis=0, keepdims=True)
    small_ref[2:3] = jnp.sum(u, axis=0, keepdims=True)
    small_ref[3:4] = jnp.sum(cot, axis=0, keepdims=True)
    small_ref[4:8] = jnp.zeros((4, 512), f32)
    att_low = gmid.astype(bf16)
    gctx_ref[...] = nt(att_low, wo[...]).astype(bf16)[0 : images * ROWS].reshape(images, ROWS, 512)
    store_rows(att_t, gmid.T.astype(bf16), t_ref[1], count)
    attended = jnp.concatenate(
        [ctx[...].reshape(images * ROWS, 512), jnp.zeros((rows - images * ROWS, 512), bf16)], axis=0
    )
    g_out = nn(att_t[...], attended)
    for k in range(4):
        (keep_o, send_o)[k % 2][k // 2] = g_out[:, k * 128 : (k + 1) * 128]


def attn_backward(scale, p_in, qkv, gctx, sht, pick, order, keep_ref, send_ref, plow_ref, gbias_ref,
                  ghead_ref):
    @pl.when(pl.program_id(0) == 0)
    def _():
        keep_ref[...] = jnp.zeros_like(keep_ref)
        send_ref[...] = jnp.zeros_like(send_ref)
        gbias_ref[...] = jnp.zeros_like(gbias_ref)
        ghead_ref[...] = jnp.zeros_like(ghead_ref)

    gwin = nn(pick[...], gctx[0, 0:LEN]).astype(bf16)
    low_masks = head_masks(bf16)
    masks = head_masks(f32)
    for k in range(4):
        q = qkv[0, k, :, 0:128]
        kk = qkv[0, k, :, 128:256]
        v = qkv[0, k, :, 256:384]
        spans = [slice(w * WPAD, (w + 1) * WPAD) for w in range(4)]
        blocks = [head_blocks(gwin[rows, k * 128 : (k + 1) * 128], low_masks) for rows in spans]
        probs = [p_in[0, k, w] for w in range(4)]
        gps = [nt(v[rows], gbd) for rows, gbd in zip(spans, blocks)]
        gvs = [nn(p.astype(bf16), gbd) for p, gbd in zip(probs, blocks)]
        prods = [p * gp for p, gp in zip(probs, gps)]
        gls = [x - p * jnp.sum(x, axis=0, keepdims=True) for p, x in zip(probs, prods)]
        lows = [gl.astype(bf16) for gl in gls]
        gks = [nn(low, head_blocks(q[rows], low_masks)) for low, rows in zip(lows, spans)]
        gqs = [head_diag(tn(low, kk[rows]), masks) * scale for low, rows in zip(lows, spans)]
        bias_sum = gls[0] + gls[1] + gls[2] + gls[3]
        q_sum = jnp.sum(gqs[0] + gqs[1] + gqs[2] + gqs[3], axis=0, keepdims=True)
        v_sum = jnp.sum(gvs[0] + gvs[1] + gvs[2] + gvs[3], axis=0, keepdims=True)
        parts = [
            jnp.concatenate([gq, gk, gv], axis=1).astype(bf16) for gq, gk, gv in zip(gqs, gks, gvs)
        ]
        gbias_ref[k] += bias_sum
        ghead_ref[k, 0:1] += q_sum
        ghead_ref[k, 1:2] += v_sum
        plow = nt(jnp.concatenate(parts, axis=0), order[...]).astype(bf16)
        (keep_ref, send_ref)[k % 2][k // 2] += nn(sht[0], plow)
        plow_ref[0, k, 0:LEN] = tn(pick[...], plow).astype(bf16)
        plow_ref[0, k, LEN:ROWS] = jnp.zeros((ROWS - LEN, plow.shape[1]), bf16)


def input_backward(t_ref, tok, gmid, plow, w0, w1, w2, w3, sv, out_ref, small_ref, wlow):
    @pl.when(pl.program_id(0) == 0)
    def _():
        small_ref[...] = jnp.zeros_like(small_ref)
        for k, w in enumerate((w0, w1, w2, w3)):
            wlow[k] = w[...].astype(bf16)

    u = nt(plow[0, 0], wlow[0])
    for k in range(1, 4):
        u = u + nt(plow[0, k], wlow[k])
    u = u[0:LEN]
    n, scale = norm_parts(tok[0].astype(f32))
    small_ref[0:1] += jnp.sum(u * n, axis=0, keepdims=True)
    small_ref[1:2] += jnp.sum(u, axis=0, keepdims=True)
    out_ref[0] = gmid[0:LEN] + norm_back(n, scale, sv[0:1], u)


def assemble(t_ref, a0, a1, a2, a3, out):
    for k, a in enumerate((a0, a1, a2, a3)):
        @pl.when(pl.program_id(0) == k)
        def _(a=a):
            out[...] = a[...].astype(out.dtype)


def split_low(x, parts):
    out = []
    for _ in range(parts):
        low = x.astype(bf16)
        out.append(low)
        x = x - low.astype(f32)
    return out


def spread_product(left, right, terms, product=nn):
    total = None
    for i, j in terms:
        part = product(left[i], right[j])
        total = part if total is None else total + part
    return total


def symmetric_product(out, left, right, terms):
    half = out.shape[0] // 2
    top = [x[:half] for x in left]
    bottom = [x[half:] for x in left]
    first = [x[:, :half] for x in right]
    second = [x[:, half:] for x in right]
    out[:half, :half] = spread_product(top, first, terms)
    cross = spread_product(top, second, terms)
    out[:half, half:] = cross
    out[half:, :half] = cross.T
    out[half:, half:] = spread_product(bottom, second, terms)


three_terms = ((1, 0), (0, 1), (0, 0))
six_terms = ((2, 0), (0, 2), (1, 1)) + three_terms


def gram_kernel(spans, flip, t_ref, same, other, g_ref):
    for n, (start, stop) in enumerate(spans):
        a = split_low(same[:, start:stop], 3)
        b = split_low(other[:, start:stop], 3)
        half = same.shape[0]
        place = (t_ref[0] % 2) ^ (n ^ flip)
        for m, (left, right) in enumerate(((a, a), (a, b), (b, b))):
            g_ref[place, :, m * half : (m + 1) * half] = spread_product(left, right, six_terms, nt)


def newton_schulz(t_ref, keep_a, near_a, far_a, keep_i, near_i, far_i, rows_ref, a_s, p_s, t_s, q_s):
    inner = (t_ref[0] == 1) | (t_ref[0] == 2)
    g = jnp.where(
        inner, keep_a[0] + near_a[...] + far_a[...], keep_i[0] + near_i[...] + far_i[...]
    )
    half = g.shape[0]
    size = 2 * half
    cross = g[:, half:size]
    a_s[:half, :half] = g[:, :half]
    a_s[:half, half:] = cross
    a_s[half:, :half] = cross.T
    a_s[half:, half:] = g[:, size:]
    row = lax.broadcasted_iota(jnp.int32, (size, size), 0)
    col = lax.broadcasted_iota(jnp.int32, (size, size), 1)
    eye = jnp.where(row == col, 1.0, 0.0)
    whole = a_s[...]
    inv = 1.0 / (jnp.sum(jnp.sum(whole * eye, axis=0, keepdims=True), axis=1, keepdims=True) + 1e-07)
    a_s[...] = whole * inv
    c0, c1, c2 = quintic_coef
    for step in range(NS_STEPS - 1):
        exact = step < 3
        terms = six_terms if exact else three_terms
        parts = split_low(a_s[...], 3 if exact else 2)
        symmetric_product(t_s, parts, parts, terms)
        p_s[...] = c0 * eye + c1 * a_s[...] + c2 * t_s[...]
        poly = split_low(p_s[...], 3 if exact else 2)
        if step == 0:
            q_s[...] = p_s[...]
        else:
            symmetric_product(q_s, poly, split_low(q_s[...], 2), three_terms)
        symmetric_product(t_s, poly, parts, terms)
        symmetric_product(a_s, poly, split_low(t_s[...], 3 if exact else 2), terms)
    count = rows_ref.shape[0]
    parts = split_low(a_s[...], 2)
    square = spread_product([x[:count] for x in parts], parts, three_terms)
    poly = split_low(c0 * eye[:count] + c1 * a_s[0:count] + c2 * square, 2)
    rows_ref[...] = spread_product(poly, split_low(q_s[...], 2), three_terms) * jnp.sqrt(inv)


def final_kernel(places, factors, t_ref, q0, q1, q2, q3, same_a, other_a, same_i, other_i, u_in,
                 u_exp, u_red, u_out, q_s):
    for k, q in enumerate((q0, q1, q2, q3)):
        q_s[t_ref[0] ^ k] = q[...]
    for m, (group, start, stop) in enumerate(places):
        same = (same_i, same_a)[group][:, start:stop]
        other = (other_i, other_a)[group][:, start:stop]
        half = same.shape[0]
        u = (-matrix_rate * factors[m]) * (
            nn(q_s[m, :, 0:half], same, precision=highest)
            + nn(q_s[m, :, half:], other, precision=highest)
        )
        ref = (u_in, u_exp, u_red, u_out)[m]
        ref[...] = u


def after(value, *earlier):
    return lax.optimization_barrier((value, *earlier))[0]


def xor_tensor(x, k):
    return lax.ppermute(x, "tensor", [(i, i ^ k) for i in range(lax.axis_size("tensor"))])


def xor_dp(x, k):
    return lax.ppermute(x, "dp", [(i, i ^ k) for i in range(lax.axis_size("dp"))])


def gather_tensor(block, *earlier, late=None):
    near = xor_tensor(block, 1)
    far = xor_tensor(after(block, *earlier) if earlier else block, 2)
    return [block, near, far, xor_tensor(far if late is None else after(far, late), 1)]


def scatter_tensor(blocks):
    got = xor_tensor(jnp.stack([blocks[1], blocks[3]]), 1)
    own = blocks[0] + got[0]
    far = blocks[2] + got[1]
    return own + xor_tensor(far, 2)


def first_stage(own, far):
    rows = lax.axis_size("dp") * own.piece
    half, quarter = rows // 2, rows // 4
    return far(0, half), jnp.stack([own(half + quarter, rows), far(half + quarter, rows)])


def second_stage(own, far, got_t, got_d):
    rows = lax.axis_size("dp") * own.piece
    half, quarter = rows // 2, rows // 4
    last = own(quarter, half) + got_t[quarter:]
    return far(half, half + quarter) + got_d[1], last, own(0, quarter) + got_t[:quarter]


def third_stage(own, keep, got_d, last_t, last_d):
    piece = own.piece
    rows = lax.axis_size("dp") * piece
    half, quarter = rows // 2, rows // 4
    pieces = [keep[i : i + piece] + last_d[i : i + piece] for i in range(0, quarter, piece)]
    for i in range(0, quarter, piece):
        start = half + i
        pieces.append(
            own(start, start + piece) + got_d[0, i : i + piece] + last_t[i : i + piece]
        )
    return pieces


class Summed:
    def __init__(self, piece, *groups):
        self.piece = piece
        self.groups = groups

    def __call__(self, start, stop):
        return jnp.concatenate([a[start:stop] + b[start:stop] for a, b in self.groups], axis=1)


def low_bit_stage(own, far):
    rows = lax.axis_size("dp") * own.piece
    half, quarter = rows // 2, rows // 4
    spans = ((quarter, half), (half + quarter, rows))
    return jnp.stack([part(a, b) for part in (own, far) for a, b in spans])


def tensor_stage(far, got):
    rows = lax.axis_size("dp") * far.piece
    half, quarter = rows // 2, rows // 4
    return jnp.concatenate([far(0, quarter) + got[2], far(half, half + quarter) + got[3]])


def last_pieces(own, got, last):
    piece = own.piece
    rows = lax.axis_size("dp") * piece
    half, quarter = rows // 2, rows // 4
    pieces = []
    for n, start in enumerate((0, half)):
        for i in range(0, quarter, piece):
            at = n * quarter + i
            pieces.append(
                own(start + i, start + i + piece) + got[n, i : i + piece] + last[at : at + piece]
            )
    return pieces


def send_groups(pieces):
    return [xor_dp(p, 2 * g) for g, p in enumerate(pieces) if g > 0]


def barrier(*values):
    return lax.optimization_barrier(values)


def join_images(t, parts, dtype):
    images, length, features = parts[0].shape
    return pl.pallas_call(
        assemble,
        grid_spec=pltpu.PrefetchScalarGridSpec(
            num_scalar_prefetch=1,
            grid=(4,),
            in_specs=[pl.BlockSpec((images, length, features), lambda a, t_ref: (0, 0, 0))] * 4,
            out_specs=pl.BlockSpec(
                (images, length, features), lambda a, t_ref: (t_ref[0] ^ a, 0, 0)
            ),
        ),
        out_shape=jax.ShapeDtypeStruct((4 * images, length, features), dtype),
        compiler_params=params(),
        cost_estimate=heavy,
        name="join_images",
    )(t, *parts)


def local(
    tokens,
    cotangent,
    region_ids,
    relative_index,
    shared_vectors,
    input_weight,
    head_bias,
    output_weight,
    expand_weight,
    expand_bias,
    reduce_weight,
    bias_table,
    moment_shared,
    moment_input,
    moment_head,
    moment_output,
    moment_expand,
    moment_bias,
    moment_reduce,
    moment_table,
):
    nt_axis = lax.axis_size("tensor")
    me_t = lax.axis_index("tensor")
    me_d = lax.axis_index("dp")
    nd = lax.axis_size("dp")
    all_images, length, features = tokens.shape
    images = all_images // nt_axis
    heads = bias_table.shape[1]
    head_size = head_bias.shape[1] // heads
    width = heads * head_size
    hidden_here = expand_weight.shape[1]
    table_rows = bias_table.shape[0]
    query_scale = head_size ** (-0.5)
    low_d = me_d % 2
    t_arr = jnp.stack([me_t, me_d, low_d]).astype(jnp.int32)
    rows = -(-images * ROWS // 128) * 128
    lanes = heads * WPAD

    pad_lanes = lambda x: jnp.pad(x, ((0, 0), (0, features - x.shape[1])))
    pack = jnp.concatenate(
        [
            pad_lanes(bias_table.T),
            pad_lanes(head_bias.reshape(1, 2 * width)),
            pad_lanes(expand_bias.reshape(1, hidden_here)),
            jnp.zeros((2, features), f32),
        ]
    )
    packs = [pack, xor_tensor(pack, 1), xor_tensor(pack, 2)]
    w_in = [input_weight, xor_tensor(input_weight, 1)]
    w_in.append(xor_tensor(after(input_weight, pack), 2))
    w_out = [output_weight, xor_tensor(output_weight, 1), xor_tensor(output_weight, 2)]
    w_exp = [expand_weight, xor_tensor(expand_weight, 1)]
    w_red = [reduce_weight, xor_tensor(reduce_weight, 1)]

    pick_np, place_np = window_tables()
    pick = jnp.asarray(pick_np, bf16)
    order = jnp.asarray(column_order(heads, head_size), bf16)
    rel_t = jnp.pad(relative_index.T, ((0, WPAD - WIN2), (0, WPAD - WIN2)), constant_values=-1)
    rel_wide = jnp.tile(rel_t, (1, heads))
    region = region_ids.reshape(2, WIN, 2, WIN).transpose(0, 2, 1, 3).reshape(4, WIN2)
    region = jnp.pad(region, ((0, 0), (0, WPAD - WIN2)))
    region_both = jnp.concatenate(
        [
            jnp.broadcast_to(region[:, :, None], (4, WPAD, lanes)),
            jnp.broadcast_to(jnp.tile(region, (1, heads))[:, None, :], (4, WPAD, lanes)),
        ]
    )
    spread = np.zeros((2 * heads, 2 * lanes), np.float32)
    for h in range(2 * heads):
        spread[h, h * WPAD : (h + 1) * WPAD] = 1.0
    sds = jax.ShapeDtypeStruct
    pack_spec = pl.BlockSpec((8, features), lambda i, *_: (0, 0))

    def bias_of(blocks):
        return pl.pallas_call(
            bias_kernel,
            grid=(1,),
            in_specs=[pack_spec] * 2
            + [
                pl.BlockSpec((2 * heads, 2 * lanes), lambda i: (0, 0)),
                pl.BlockSpec((WPAD, lanes), lambda i: (0, 0)),
            ],
            out_specs=pl.BlockSpec((2, WPAD, lanes), lambda i: (0, 0, 0)),
            out_shape=sds((2, WPAD, lanes), f32),
            scratch_shapes=[pltpu.VMEM((256, 2 * lanes), f32)],
            compiler_params=params(),
            cost_estimate=light,
            name="bias",
        )(*blocks, jnp.asarray(spread), rel_wide)

    mask = pl.pallas_call(
        mask_kernel,
        in_specs=[VMEM],
        out_specs=VMEM,
        out_shape=sds((4, WPAD, lanes), f32),
        compiler_params=params(),
        cost_estimate=light,
        name="mask",
    )(region_both)
    bias_a = bias_of(packs[:2])
    piece = features // nd
    row_at = me_d * piece
    moment_a = jnp.concatenate(
        [
            lax.dynamic_slice_in_dim(moment_expand, row_at, piece, 0),
            lax.dynamic_slice_in_dim(moment_reduce, row_at, piece, 1).T,
        ],
        axis=1,
    )
    moment_i = jnp.concatenate(
        [
            lax.dynamic_slice_in_dim(moment_input, row_at, piece, 0),
            lax.dynamic_slice_in_dim(moment_output, row_at, piece, 1).T,
        ],
        axis=1,
    )
    packs.append(xor_tensor(packs[2], 1))
    bias_b = bias_of(packs[2:])
    w_in[2], w_out[2], bias_a, bias_b, mask, moment_a, moment_i = barrier(
        w_in[2], w_out[2], bias_a, bias_b, mask, moment_a, moment_i
    )
    w_in.append(xor_tensor(w_in[2], 1))
    w_out.append(xor_tensor(w_out[2], 1))
    far_exp = xor_tensor(after(expand_weight, bias_b), 2)
    far_red = xor_tensor(after(reduce_weight, w_in[2]), 2)

    whole = lambda *shape: pl.BlockSpec(shape, lambda i, *_: (0,) * len(shape))
    one = lambda *shape: pl.BlockSpec((1,) + shape, lambda i, *_: (i,) + (0,) * len(shape))
    tok_one = pl.BlockSpec((1, length, features), lambda i, t: (t[0] * images + i, 0, 0))
    probs, qkv, sht, ctx = pl.pallas_call(
        functools.partial(attn_forward, query_scale, nd),
        grid_spec=pltpu.PrefetchScalarGridSpec(
            num_scalar_prefetch=1,
            grid=(images,),
            in_specs=[tok_one]
            + [whole(features, 3 * width)] * 4
            + [pack_spec] * 4
            + [
                whole(6, features),
                whole(2, WPAD, lanes),
                whole(2, WPAD, lanes),
                whole(4, WPAD, lanes),
                whole(WROWS, LEN),
                whole(3 * width, 3 * width),
            ],
            out_specs=[
                one(4, 4, WPAD, lanes),
                one(4, WROWS, 3 * width),
                one(features, WROWS),
                one(ROWS, 4 * width),
            ],
            scratch_shapes=[pltpu.VMEM((4, features, 3 * width), bf16)],
        ),
        out_shape=[
            sds((images, 4, 4, WPAD, lanes), f32),
            sds((images, 4, WROWS, 3 * width), bf16),
            sds((images, features, WROWS), bf16),
            sds((images, ROWS, 4 * width), bf16),
        ],
        compiler_params=params(),
        cost_estimate=heavy,
        name="attn_forward",
    )(t_arr, tokens, *w_in, *packs, shared_vectors, bias_a, bias_b, mask, pick, order)

    tok_all = pl.BlockSpec((images, length, features), lambda i, t: (t[0], 0, 0))
    token_f = (rows, features)
    wide = 2 * hidden_here
    hidden_scratch = [
        pltpu.VMEM((4, features, hidden_here // 2), bf16),
        pltpu.VMEM((4, hidden_here // 2, features), bf16),
        pltpu.VMEM((4, 1, hidden_here // 2), f32),
        pltpu.VMEM((2, rows, hidden_here // 2), f32),
        pltpu.VMEM((rows, hidden_here // 2), bf16),
        pltpu.VMEM((rows, hidden_here // 2), bf16),
    ]
    state_shapes = [
        ((4 * width, features), bf16),
        (token_f, f32),
        (token_f, bf16),
        (token_f[::-1], bf16),
        (token_f, bf16),
        (token_f[::-1], bf16),
        (token_f, f32),
        (token_f, f32),
    ]
    *carry, keep_0, send_1, geb_a = pl.pallas_call(
        functools.partial(feed_first, images, nd),
        grid_spec=pltpu.PrefetchScalarGridSpec(
            num_scalar_prefetch=1,
            grid=(1,),
            in_specs=[whole(images, ROWS, 4 * width), tok_all, tok_all]
            + [whole(width, features)] * 4
            + [whole(features, hidden_here)] * 2
            + [whole(hidden_here, features)] * 2
            + [pack_spec] * 2
            + [whole(6, features)],
            out_specs=[whole(*shape) for shape, _ in state_shapes]
            + [whole(features, wide), whole(features, wide), whole(4, 1, hidden_here // 2)],
            scratch_shapes=hidden_scratch + [pltpu.VMEM(token_f, f32)],
        ),
        out_shape=[sds(shape, dtype) for shape, dtype in state_shapes]
        + [sds((features, wide), f32)] * 2
        + [sds((4, 1, hidden_here // 2), f32)],
        compiler_params=params(),
        cost_estimate=heavy,
        name="feed_first",
    )(t_arr, ctx, tokens, cotangent, *w_out, *w_exp, *w_red, *packs[:2], shared_vectors)

    far_exp = after(far_exp, geb_a)
    w_exp += [far_exp, xor_tensor(far_exp, 1)]
    far_red = after(far_red, geb_a)
    w_red += [far_red, xor_tensor(far_red, 1)]
    got_1 = xor_tensor(send_1, 1)

    wo_low, mid, n2_low, n2_t, cot_low, cot_t, mix, gn2 = carry
    mix, gn2, keep_2, send_3, geb_b = pl.pallas_call(
        feed_second,
        grid_spec=pltpu.PrefetchScalarGridSpec(
            num_scalar_prefetch=1,
            grid=(1,),
            in_specs=[whole(features, hidden_here)] * 2
            + [whole(hidden_here, features)] * 2
            + [pack_spec] * 2
            + [whole(*shape) for shape, _ in state_shapes[2:]],
            out_specs=[
                whole(rows, features),
                whole(rows, features),
                whole(features, wide),
                whole(features, wide),
                whole(4, 1, hidden_here // 2),
            ],
            scratch_shapes=hidden_scratch,
        ),
        out_shape=[
            sds((rows, features), f32),
            sds((rows, features), f32),
            sds((features, wide), f32),
            sds((features, wide), f32),
            sds((4, 1, hidden_here // 2), f32),
        ],
        compiler_params=params(),
        cost_estimate=light,
        name="feed_second",
    )(
        t_arr,
        *w_exp[2:],
        *w_red[2:],
        *packs[2:],
        n2_low,
        n2_t,
        cot_low,
        cot_t,
        mix,
        gn2,
    )
    got_3 = xor_tensor(send_3, 1)

    block_part, gmid, gctx, keep_o, send_o, small_a = pl.pallas_call(
        functools.partial(feed_last, images, nd),
        grid_spec=pltpu.PrefetchScalarGridSpec(
            num_scalar_prefetch=1,
            grid=(1,),
            in_specs=[
                whole(images, ROWS, 4 * width),
                whole(6, features),
                whole(4 * width, features),
            ]
            + [whole(rows, features)] * 4,
            out_specs=[
                whole(images, length, features),
                whole(rows, features),
                whole(images, ROWS, 4 * width),
                whole(2, features, width),
                whole(2, features, width),
                whole(8, features),
            ],
            scratch_shapes=[pltpu.VMEM(token_f[::-1], bf16)],
        ),
        out_shape=[
            sds((images, length, features), f32),
            sds((rows, features), f32),
            sds((images, ROWS, 4 * width), bf16),
            sds((2, features, width), f32),
            sds((2, features, width), f32),
            sds((8, features), f32),
        ],
        compiler_params=params(),
        cost_estimate=light,
        name="feed_last",
    )(t_arr, ctx, shared_vectors, wo_low, mid, cot_low, mix, gn2)

    got_o = xor_tensor(send_o, 1)
    got_3, gctx = barrier(got_3, gctx)
    own_a = Summed(piece, (keep_0, got_1))
    far_a = Summed(piece, (keep_2, got_3))
    t1_a, d1_a = first_stage(own_a, far_a)
    gctx, t1_a, d1_a = barrier(gctx, t1_a, d1_a)
    got_t1_a, got_d1_a = xor_tensor(t1_a, 2), xor_dp(d1_a, 1)

    keep_i, send_i, plow, gbias, ghead = pl.pallas_call(
        functools.partial(attn_backward, query_scale),
        grid=(images,),
        in_specs=[
            one(4, 4, WPAD, lanes),
            one(4, WROWS, 3 * width),
            one(ROWS, 4 * width),
            one(features, WROWS),
            whole(WROWS, LEN),
            whole(3 * width, 3 * width),
        ],
        out_specs=[
            whole(2, features, 3 * width),
            whole(2, features, 3 * width),
            one(4, ROWS, 3 * width),
            whole(4, WPAD, lanes),
            whole(4, 2, width),
        ],
        out_shape=[
            sds((2, features, 3 * width), f32),
            sds((2, features, 3 * width), f32),
            sds((images, 4, ROWS, 3 * width), bf16),
            sds((4, WPAD, lanes), f32),
            sds((4, 2, width), f32),
        ],
        compiler_params=params(),
        cost_estimate=light,
        name="attn_backward",
    )(probs, qkv, gctx, sht, pick, order)

    got_i = xor_tensor(send_i, 1)

    grad_part, small_i = pl.pallas_call(
        input_backward,
        grid_spec=pltpu.PrefetchScalarGridSpec(
            num_scalar_prefetch=1,
            grid=(images,),
            in_specs=[
                tok_one,
                pl.BlockSpec((ROWS, features), lambda i, t: (i, 0)),
                one(4, ROWS, 3 * width),
            ]
            + [whole(features, 3 * width)] * 4
            + [whole(6, features)],
            out_specs=[one(length, features), whole(8, features)],
            scratch_shapes=[pltpu.VMEM((4, features, 3 * width), bf16)],
        ),
        out_shape=[sds((images, length, features), f32), sds((8, features), f32)],
        compiler_params=params(),
        cost_estimate=light,
        name="input_backward",
    )(t_arr, tokens, gmid, plow, *w_in, shared_vectors)

    got_t1_a, got_d1_a, send_small_i = barrier(got_t1_a, got_d1_a, small_i)
    small_i = send_small_i
    t2_a, d2_a, kept_a = second_stage(own_a, far_a, got_t1_a, got_d1_a)
    got_t2_a, got_d2_a = xor_tensor(t2_a, 2), xor_dp(d2_a, 1)
    got_i, got_o = barrier(got_i, got_o, t2_a, d2_a)[:2]
    own_i = Summed(piece, (keep_i[0], got_i[0]), (keep_o[0], got_o[0]))
    far_i = Summed(piece, (keep_i[1], got_i[1]), (keep_o[1], got_o[1]))
    d1_i = low_bit_stage(own_i, far_i)
    got_d1_i = xor_dp(d1_i, 1)
    got_t2_a, got_d2_a, d1_i = barrier(got_t2_a, got_d2_a, d1_i)
    pieces_a = third_stage(own_a, kept_a, got_d1_a, got_t2_a, got_d2_a)
    got_a = send_groups(pieces_a)
    got_d1_i = barrier(got_d1_i, *got_a)[0]
    t2_i = tensor_stage(far_i, got_d1_i)
    got_t2_i = xor_tensor(t2_i, 2)
    gbias, ghead, small_i, geb_a, geb_b, small_a, rel_t = barrier(
        gbias, ghead, small_i, geb_a, geb_b, small_a, rel_t, *pieces_a
    )[:7]

    pick_table = (
        jnp.arange(table_rows)[:, None] == rel_t[:WIN2].reshape(1, -1)
    ).astype(f32)
    gb = gbias[:, :WIN2].reshape(4, WIN2, heads, WPAD).transpose(0, 2, 1, 3)
    gtable = lax.dot_general(
        gb.reshape(4 * heads, -1), pick_table, (((1,), (1,)), ((), ())), precision=highest
    ).reshape(4, heads * table_rows)
    shared_rows = jnp.concatenate([small_i[0:2], small_a[0:4]])
    geb = jnp.concatenate([geb_a, geb_b]).reshape(4, hidden_here)
    block_small = jnp.concatenate([gtable, ghead.reshape(4, -1), geb], axis=1)
    n_small = block_small.shape[1]
    small_send = jnp.concatenate([block_small[1], block_small[3], shared_rows.reshape(-1)])
    got_small = xor_tensor(small_send, 1)
    got_a = barrier(*got_a, small_send)[: len(got_a)]
    grad_scale = (all_images * length * nd) ** (-0.5)
    grad_a = sum(got_a, pieces_a[0]) * grad_scale
    state_a = moment_decay * moment_a + (1.0 - moment_decay) * grad_a
    same_a = [state_a] + send_groups([state_a] * (nd // 2))
    own_small = block_small[0] + got_small[:n_small]
    far_small = block_small[2] + got_small[n_small : 2 * n_small]
    shared_sum = shared_rows.reshape(-1) + got_small[2 * n_small :]
    small_send = jnp.concatenate([far_small, shared_sum])
    got_small = xor_tensor(small_send, 2)
    block_part = after(block_part, *pieces_a, got_small)
    block_parts = [block_part, xor_tensor(block_part, 1), xor_tensor(block_part, 2)]
    got_small = barrier(got_small, t2_i, state_a)[0]
    vector = jnp.concatenate([own_small, shared_sum]) + got_small
    got_small = xor_dp(vector, 1)
    *same_a, got_t2_i, got_small, far_block = barrier(
        *same_a, got_t2_i, got_small, block_parts[2]
    )
    block_parts = [block_parts[0], block_parts[1], far_block, xor_tensor(far_block, 1)]
    same_a = jnp.concatenate(same_a)
    other_a = xor_dp(same_a, 1)
    vector = vector + got_small
    small_parts = send_groups([vector] * (nd // 2))
    grad_part = after(grad_part, same_a)
    grad_parts = [grad_part, xor_tensor(grad_part, 1), xor_tensor(grad_part, 2)]
    got_t2_i = barrier(got_t2_i, same_a)[0]
    pieces_i = last_pieces(own_i, got_d1_i, got_t2_i)
    got_i = send_groups(pieces_i)
    grad_i = sum(got_i, pieces_i[0]) * grad_scale
    state_i = moment_decay * moment_i + (1.0 - moment_decay) * grad_i
    same_i = [state_i] + send_groups([state_i] * (nd // 2))
    other_a = after(other_a, state_i)
    vector = sum(barrier(*small_parts, state_i)[: len(small_parts)], vector)
    block_parts[1], block_parts[3] = barrier(block_parts[1], block_parts[3], state_i)[:2]
    block_out = join_images(t_arr, block_parts, bf16)

    places = [
        (0, 0, 3 * width),
        (1, 0, hidden_here),
        (1, hidden_here, wide),
        (0, 3 * width, 4 * width),
    ]
    half = features // 2
    scalars = pl.BlockSpec(memory_space=pltpu.SMEM)

    def grams(group, *operands):
        spans = [(b, c) for a, b, c in places if a == group]
        return pl.pallas_call(
            functools.partial(gram_kernel, spans, group),
            in_specs=[scalars] + [VMEM] * 2,
            out_specs=VMEM,
            out_shape=sds((2, half, 3 * half), f32),
            compiler_params=params(),
            cost_estimate=heavy,
            name="gram",
        )(t_arr, *operands)

    gram_a = grams(1, same_a, other_a)
    near_a = xor_tensor(gram_a[1], 1)
    same_i = jnp.concatenate(barrier(*same_i, block_out)[: len(same_i)])
    other_i = xor_dp(same_i, 1)
    near_a = barrier(near_a, same_i)[0]
    send_far = gram_a[0] + near_a
    far_a = lax.ppermute(send_far, "tensor", [(0, 2), (3, 1)])
    other_i, grad_far = barrier(other_i, grad_parts[2], send_far)[:2]
    gram_i = grams(0, same_i, other_i)
    near_i = xor_tensor(gram_i[1], 1)
    grad_far = after(grad_far, gram_i)
    grad_last = xor_tensor(grad_far, 1)
    near_i, far_a = barrier(near_i, far_a)
    far_i = lax.ppermute(gram_i[0] + near_i, "tensor", [(2, 0), (1, 3)])
    grad_near, grad_last = barrier(grad_parts[1], grad_last, near_i)[:2]
    input_grad = join_images(t_arr, [grad_parts[0], grad_near, grad_far, grad_last], f32)
    far_i = barrier(far_i, input_grad)[0]
    own_rows = pl.pallas_call(
        newton_schulz,
        in_specs=[scalars] + [VMEM] * 6,
        out_specs=VMEM,
        out_shape=sds((piece, features), f32),
        scratch_shapes=[pltpu.VMEM((features, features), f32)] * 4,
        compiler_params=params(),
        cost_estimate=light,
        name="newton_schulz",
    )(t_arr, gram_a, near_a, far_a, gram_i, near_i, far_i)
    near_rows = xor_tensor(own_rows, 1)
    far_rows = xor_tensor(own_rows, 2)
    factor = lambda a, b: math.sqrt(max(1.0, a / b))
    update_m = pl.pallas_call(
        functools.partial(
            final_kernel,
            places,
            [
                factor(features, 3 * width * nt_axis),
                factor(features, hidden_here * nt_axis),
                factor(hidden_here * nt_axis, features),
                factor(width * nt_axis, features),
            ],
        ),
        in_specs=[scalars] + [VMEM] * 8,
        out_specs=[VMEM] * 4,
        out_shape=[
            sds((piece, 3 * width), f32),
            sds((piece, hidden_here), f32),
            sds((piece, hidden_here), f32),
            sds((piece, width), f32),
        ],
        scratch_shapes=[pltpu.VMEM((4, piece, features), f32)],
        compiler_params=params(),
        cost_estimate=light,
        name="update",
    )(
        t_arr,
        own_rows,
        near_rows,
        far_rows,
        xor_tensor(far_rows, 1),
        same_a,
        other_a,
        same_i,
        other_i,
    )
    update_m = (update_m[0], update_m[3].T, update_m[1], update_m[2].T)

    vector = after(vector, near_i)
    at = heads * table_rows
    gradients = {
        "table": vector[:at].reshape(heads, table_rows).T,
        "head": vector[at : at + 2 * width].reshape(2, width),
        "bias": vector[at + 2 * width : n_small],
        "shared": vector[n_small:].reshape(6, features),
    }
    moments = dict(table=moment_table, head=moment_head, bias=moment_bias, shared=moment_shared)
    gradients = {k: v * grad_scale for k, v in gradients.items()}
    states = {
        k: moment_decay * moments[k] + (1.0 - moment_decay) * gradients[k] for k in gradients
    }

    def split(part_i, part_a):
        a, b, c, d = [(part_i, part_a)[g][:, s:e] for g, s, e in places]
        return a, d.T, b, c.T

    grad_m = split(grad_i, grad_a)
    state_m = split(state_i, state_a)
    return (
        block_out,
        input_grad,
        gradients["shared"],
        grad_m[0],
        gradients["head"],
        grad_m[1],
        grad_m[2],
        gradients["bias"],
        grad_m[3],
        gradients["table"],
        -vector_rate * states["shared"],
        update_m[0],
        -vector_rate * states["head"],
        update_m[1],
        update_m[2],
        -vector_rate * states["bias"],
        update_m[3],
        -vector_rate * states["table"],
        states["shared"],
        state_m[0],
        states["head"],
        state_m[1],
        state_m[2],
        states["bias"],
        state_m[3],
        states["table"],
    )


def solution(mesh):
    return jax.shard_map(
        local,
        mesh=mesh,
        in_specs=(
            P("dp", None, None),
            P("dp", None, None),
            P(),
            P(),
            P(),
            P(None, "tensor"),
            P(None, "tensor"),
            P("tensor", None),
            P(None, "tensor"),
            P("tensor"),
            P("tensor", None),
            P(None, "tensor"),
            P(),
            P(None, "tensor"),
            P(None, "tensor"),
            P("tensor", None),
            P(None, "tensor"),
            P("tensor"),
            P("tensor", None),
            P(None, "tensor"),
        ),
        out_specs=(
            P("dp", None, None),
            P("dp", None, None),
            P(),
            P("dp", "tensor"),
            P(None, "tensor"),
            P("tensor", "dp"),
            P("dp", "tensor"),
            P("tensor"),
            P("tensor", "dp"),
            P(None, "tensor"),
            P(),
            P("dp", "tensor"),
            P(None, "tensor"),
            P("tensor", "dp"),
            P("dp", "tensor"),
            P("tensor"),
            P("tensor", "dp"),
            P(None, "tensor"),
            P(),
            P("dp", "tensor"),
            P(None, "tensor"),
            P("tensor", "dp"),
            P("dp", "tensor"),
            P("tensor"),
            P("tensor", "dp"),
            P(None, "tensor"),
        ),
        check_vma=False,
    )
```

```python
import functools
import math

import jax
import jax.numpy as jnp
import numpy as np
from jax import lax
from jax.experimental import pallas as pl
from jax.experimental.pallas import tpu as pltpu
from jax.sharding import PartitionSpec as P

SIDE = 14
WIN = 7
SHIFT = 3
NS_STEPS = 5
WIN2 = WIN * WIN
LEN = SIDE * SIDE
TABLE = (2 * WIN - 1) ** 2
ROWS = 208
WPAD = 64
WROWS = 4 * WPAD

highest = lax.Precision.HIGHEST
norm_epsilon = 1e-05
moment_decay = 0.8
matrix_rate = 1.0
vector_rate = 1.0
quintic_coef = (3.4445, -4.775, 2.0315)
masked_logit = -1e30
f32 = jnp.float32
bf16 = jnp.bfloat16
VMEM = pl.BlockSpec(memory_space=pltpu.VMEM)
light = pl.CostEstimate(flops=1000, bytes_accessed=1000, transcendentals=0)
heavy = pl.CostEstimate(flops=10_000_000_000, bytes_accessed=10_000_000, transcendentals=0)


def params(limit_mib=56, **kw):
    return pltpu.CompilerParams(vmem_limit_bytes=limit_mib * 1024 * 1024, **kw)


def nn(a, b, **kw):
    return lax.dot_general(a, b, (((1,), (0,)), ((), ())), preferred_element_type=f32, **kw)


def nt(a, b, **kw):
    return lax.dot_general(a, b, (((1,), (1,)), ((), ())), preferred_element_type=f32, **kw)


def tn(a, b, **kw):
    return lax.dot_general(a, b, (((0,), (0,)), ((), ())), preferred_element_type=f32, **kw)


def window_tables():
    pick = np.zeros((WROWS, LEN), np.float32)
    place = np.zeros((4, WIN2), np.int32)
    for r in range(SIDE):
        for c in range(SIDE):
            w = (r // WIN) * 2 + c // WIN
            i = (r % WIN) * WIN + c % WIN
            source = ((r + SHIFT) % SIDE) * SIDE + (c + SHIFT) % SIDE
            pick[w * WPAD + i, source] = 1.0
            place[w, i] = r * SIDE + c
    return pick, place


def column_order(heads, size):
    width = 3 * heads * size
    order = np.zeros((width, width), np.float32)
    for h in range(heads):
        for part in range(3):
            for e in range(size):
                order[(h * 3 + part) * size + e, part * heads * size + h * size + e] = 1.0
    return order


def norm_parts(x):
    centred = x - jnp.mean(x, axis=-1, keepdims=True)
    scale = lax.rsqrt(jnp.mean(centred * centred, axis=-1, keepdims=True) + norm_epsilon)
    return centred * scale, scale


def norm_back(n, scale, gain, u):
    w = u * gain
    return scale * (
        w - jnp.mean(w, axis=-1, keepdims=True) - n * jnp.mean(w * n, axis=-1, keepdims=True)
    )


def head_blocks(x, masks):
    return jnp.concatenate([x * m for m in masks], axis=0)


def head_diag(r, masks):
    rows = r.shape[0] // 4
    out = r[0:rows] * masks[0]
    for h in range(1, 4):
        out = out + r[h * rows : (h + 1) * rows] * masks[h]
    return out


def head_masks(dtype):
    lane = lax.broadcasted_iota(jnp.int32, (1, 128), 1) // 32
    return [jnp.where(lane == h, 1.0, 0.0).astype(dtype) for h in range(4)]


def row_place(index, count):
    group = index // 2
    quarter = count // 4
    return (group // quarter) * (2 * quarter) + (index % 2) * quarter + group % quarter


def store_rows(ref, values, me, count, at=None):
    piece = values.shape[0] // count
    for p in range(count):
        place = pl.multiple_of(row_place(p ^ me, count) * piece, piece)
        block = values[p * piece : (p + 1) * piece]
        if at is None:
            ref[pl.ds(place, piece)] = block
        else:
            ref[at, pl.ds(place, piece)] = block


def bias_kernel(k0, k1, expand, rel, bias_ref, rows_s):
    size = rel.shape[1]
    tables = jnp.concatenate([k[0:4, 0:256] for k in (k0, k1)], axis=0)
    rows_s[...] = tn(tables, expand[...], precision=highest)
    index = rel[...]
    step = 2 * WIN - 1
    for k in range(2):
        def body(n, acc):
            for m in range(step):
                at = n * step + m
                acc = jnp.where(index == at, rows_s[pl.ds(at, 1), k * size : (k + 1) * size], acc)
            return acc

        bias_ref[k] = lax.fori_loop(0, step, body, jnp.zeros(index.shape, f32))


def mask_kernel(region, mask_ref):
    shape = mask_ref.shape[1:]
    row = lax.broadcasted_iota(jnp.int32, shape, 0)
    col = lax.broadcasted_iota(jnp.int32, shape, 1) % WPAD
    for w in range(4):
        same = region[w] == region[4 + w]
        ok = (row < WIN2) & ((col >= WIN2) | same)
        mask_ref[w] = jnp.where(ok, 0.0, masked_logit)


def attn_forward(scale, count, t_ref, tok, w0, w1, w2, w3, k0, k1, k2, k3, sv, bias_a, bias_b, mask, pick, order, p_out,
                 qkv_out, sht_out, ctx_out, wcol):
    @pl.when(pl.program_id(0) == 0)
    def _():
        for k, w in enumerate((w0, w1, w2, w3)):
            wcol[k] = nn(w[...].astype(bf16), order[...]).astype(bf16)

    n, _ = norm_parts(tok[0].astype(f32))
    normed = (n * sv[0:1] + sv[1:2]).astype(bf16)
    shifted_f = nn(pick[...], normed)
    shifted = shifted_f.astype(bf16)
    store_rows(sht_out, shifted_f.T.astype(bf16), t_ref[1], count, 0)
    low_masks = head_masks(bf16)
    masks = head_masks(f32)
    for k in range(4):
        proj = nn(shifted, wcol[k])
        pack = (k0, k1, k2, k3)[k]
        bias = (bias_a, bias_b)[k // 2][k % 2]
        q = ((proj[:, 0:128] + pack[4:5, 0:128]) * scale).astype(bf16)
        kk = proj[:, 128:256].astype(bf16)
        v = (proj[:, 256:384] + pack[4:5, 128:256]).astype(bf16)
        qkv_out[0, k, :, 0:128] = q
        qkv_out[0, k, :, 128:256] = kk
        qkv_out[0, k, :, 256:384] = v
        spans = [slice(w * WPAD, (w + 1) * WPAD) for w in range(4)]
        logits = [
            nt(kk[rows], head_blocks(q[rows], low_masks)) + (bias + mask[w])
            for w, rows in enumerate(spans)
        ]
        exps = [jnp.exp(x - jnp.max(x, axis=0, keepdims=True)) for x in logits]
        probs = [e * (1.0 / jnp.sum(e, axis=0, keepdims=True)) for e in exps]
        mixes = [tn(p.astype(bf16), v[rows]) for p, rows in zip(probs, spans)]
        for w, p in enumerate(probs):
            p_out[0, k, w] = p
        windows = [head_diag(r, masks).astype(bf16) for r in mixes]
        ctx = jnp.concatenate(windows, axis=0)
        ctx_out[0, 0:LEN, k * 128 : (k + 1) * 128] = tn(pick[...], ctx).astype(bf16)
        ctx_out[0, LEN:ROWS, k * 128 : (k + 1) * 128] = jnp.zeros((ROWS - LEN, 128), bf16)


def hidden_blocks(we, wr, eb, hid_s, act_s, low_s, n2_s, n2t_s, cot_s, cott_s, mix_s, gn2_s, grads,
                  geb_ref):
    rows = hid_s.shape[1]
    chunk = 32

    def body(j, carry):
        hid_s[0] = nn(n2_s[...], we[j])
        hid_s[1] = nt(cot_s[...], wr[j])
        total = None
        for r in range(0, rows, chunk):
            hidden = hid_s[0, r : r + chunk] + eb[j]
            cdf = 0.5 * (1.0 + lax.erf(hidden * (1.0 / math.sqrt(2.0))))
            bell = jnp.exp(-0.5 * hidden * hidden) * (1.0 / math.sqrt(2.0 * math.pi))
            act_s[r : r + chunk] = (hidden * cdf).astype(bf16)
            g_hidden = hid_s[1, r : r + chunk] * (cdf + hidden * bell)
            low_s[r : r + chunk] = g_hidden.astype(bf16)
            total = g_hidden if r == 0 else total + g_hidden
        geb_ref[j] = jnp.sum(total, axis=0, keepdims=True)
        mix_s[...] += nn(act_s[...], wr[j])
        gn2_s[...] += nt(low_s[...], we[j])
        at = pl.multiple_of(lax.rem(j, 2) * 256, 256)
        g_exp = nn(n2t_s[...], low_s[...])
        g_red = nn(cott_s[...], act_s[...])
        for k in range(2):
            @pl.when(j // 2 == k)
            def _(k=k):
                grads[k][:, pl.ds(at, 256)] = g_exp
                grads[k][:, pl.ds(512 + at, 256)] = g_red
        return carry

    lax.fori_loop(0, 4, body, 0)


def load_bias(eb, packs):
    for k, pack in enumerate(packs):
        for half in range(2):
            eb[2 * k + half] = pack[5:6, half * 256 : (half + 1) * 256]


def load_hidden(we, wr, blocks):
    for k, (e, r) in enumerate(blocks):
        for half in range(2):
            we[2 * k + half] = e[:, half * 256 : (half + 1) * 256].astype(bf16)
            wr[2 * k + half] = r[half * 256 : (half + 1) * 256].astype(bf16)


def feed_first(images, count, t_ref, ctx, tok, cot, o0, o1, o2, o3, e0, e1, r0, r1, k0, k1, sv,
               wo, mid_s, n2_s, n2t_s, cot_s, cott_s, mix_s, gn2_s, keep_ref, send_ref, geb_ref,
               we, wr, eb, hid_s, act_s, low_s, x_s):
    rows = x_s.shape[0]
    x_s[...] = jnp.zeros_like(x_s)
    for i in range(images):
        x_s[i * ROWS : i * ROWS + LEN] = tok[i].astype(f32)
    for k, o in enumerate((o0, o1, o2, o3)):
        wo[k * 128 : (k + 1) * 128] = o[...].astype(bf16)
    load_bias(eb, (k0, k1))
    load_hidden(we, wr, ((e0, r0), (e1, r1)))
    attended = jnp.concatenate(
        [ctx[...].reshape(images * ROWS, 512), jnp.zeros((rows - images * ROWS, 512), bf16)], axis=0
    )
    mid_s[...] = x_s[...] + nn(attended, wo[...]) + sv[2:3]
    n2, _ = norm_parts(mid_s[...])
    n2f = n2 * sv[3:4] + sv[4:5]
    n2_s[...] = n2f.astype(bf16)
    store_rows(n2t_s, n2f.T.astype(bf16), t_ref[1], count)
    x_s[...] = jnp.zeros_like(x_s)
    for i in range(images):
        x_s[i * ROWS : i * ROWS + LEN] = cot[i].astype(f32)
    cot_s[...] = x_s[...].astype(bf16)
    store_rows(cott_s, x_s[...].T.astype(bf16), t_ref[1], count)
    mix_s[...] = jnp.zeros_like(mix_s)
    gn2_s[...] = jnp.zeros_like(gn2_s)
    hidden_blocks(
        we, wr, eb, hid_s, act_s, low_s, n2_s, n2t_s, cot_s, cott_s, mix_s, gn2_s,
        (keep_ref, send_ref), geb_ref,
    )


def feed_second(t_ref, e2, e3, r2, r3, k2, k3, n2_s, n2t_s, cot_s, cott_s, mix_in, gn2_in,
                mix_s, gn2_s, keep_ref, send_ref, geb_ref, we, wr, eb, hid_s,
                act_s, low_s):
    load_bias(eb, (k2, k3))
    load_hidden(we, wr, ((e2, r2), (e3, r3)))
    mix_s[...] = mix_in[...]
    gn2_s[...] = gn2_in[...]
    hidden_blocks(
        we, wr, eb, hid_s, act_s, low_s, n2_s, n2t_s, cot_s, cott_s, mix_s, gn2_s,
        (keep_ref, send_ref), geb_ref,
    )


def feed_last(images, count, t_ref, ctx, sv, wo, mid_s, cot_s, mix_s, gn2_s, out_ref, gmid_ref,
              gctx_ref, keep_o, send_o, small_ref, att_t):
    rows = mid_s.shape[0]
    result = mid_s[...] + mix_s[...] + sv[5:6]
    for i in range(images):
        out_ref[i] = result[i * ROWS : i * ROWS + LEN].astype(bf16).astype(f32)
    n2, scale2 = norm_parts(mid_s[...])
    u = gn2_s[...]
    cot = cot_s[...].astype(f32)
    gmid = cot + norm_back(n2, scale2, sv[3:4], u)
    gmid_ref[...] = gmid
    small_ref[0:1] = jnp.sum(gmid, axis=0, keepdims=True)
    small_ref[1:2] = jnp.sum(u * n2, axis=0, keepdims=True)
    small_ref[2:3] = jnp.sum(u, axis=0, keepdims=True)
    small_ref[3:4] = jnp.sum(cot, axis=0, keepdims=True)
    small_ref[4:8] = jnp.zeros((4, 512), f32)
    att_low = gmid.astype(bf16)
    gctx_ref[...] = nt(att_low, wo[...]).astype(bf16)[0 : images * ROWS].reshape(images, ROWS, 512)
    store_rows(att_t, gmid.T.astype(bf16), t_ref[1], count)
    attended = jnp.concatenate(
        [ctx[...].reshape(images * ROWS, 512), jnp.zeros((rows - images * ROWS, 512), bf16)], axis=0
    )
    g_out = nn(att_t[...], attended)
    for k in range(4):
        (keep_o, send_o)[k % 2][k // 2] = g_out[:, k * 128 : (k + 1) * 128]


def attn_backward(scale, p_in, qkv, gctx, sht, pick, order, keep_ref, send_ref, plow_ref, gbias_ref,
                  ghead_ref):
    @pl.when(pl.program_id(0) == 0)
    def _():
        keep_ref[...] = jnp.zeros_like(keep_ref)
        send_ref[...] = jnp.zeros_like(send_ref)
        gbias_ref[...] = jnp.zeros_like(gbias_ref)
        ghead_ref[...] = jnp.zeros_like(ghead_ref)

    gwin = nn(pick[...], gctx[0, 0:LEN]).astype(bf16)
    low_masks = head_masks(bf16)
    masks = head_masks(f32)
    for k in range(4):
        q = qkv[0, k, :, 0:128]
        kk = qkv[0, k, :, 128:256]
        v = qkv[0, k, :, 256:384]
        spans = [slice(w * WPAD, (w + 1) * WPAD) for w in range(4)]
        blocks = [head_blocks(gwin[rows, k * 128 : (k + 1) * 128], low_masks) for rows in spans]
        probs = [p_in[0, k, w] for w in range(4)]
        gps = [nt(v[rows], gbd) for rows, gbd in zip(spans, blocks)]
        gvs = [nn(p.astype(bf16), gbd) for p, gbd in zip(probs, blocks)]
        prods = [p * gp for p, gp in zip(probs, gps)]
        gls = [x - p * jnp.sum(x, axis=0, keepdims=True) for p, x in zip(probs, prods)]
        lows = [gl.astype(bf16) for gl in gls]
        gks = [nn(low, head_blocks(q[rows], low_masks)) for low, rows in zip(lows, spans)]
        gqs = [head_diag(tn(low, kk[rows]), masks) * scale for low, rows in zip(lows, spans)]
        bias_sum = gls[0] + gls[1] + gls[2] + gls[3]
        q_sum = jnp.sum(gqs[0] + gqs[1] + gqs[2] + gqs[3], axis=0, keepdims=True)
        v_sum = jnp.sum(gvs[0] + gvs[1] + gvs[2] + gvs[3], axis=0, keepdims=True)
        parts = [
            jnp.concatenate([gq, gk, gv], axis=1).astype(bf16) for gq, gk, gv in zip(gqs, gks, gvs)
        ]
        gbias_ref[k] += bias_sum
        ghead_ref[k, 0:1] += q_sum
        ghead_ref[k, 1:2] += v_sum
        plow = nt(jnp.concatenate(parts, axis=0), order[...]).astype(bf16)
        (keep_ref, send_ref)[k % 2][k // 2] += nn(sht[0], plow)
        plow_ref[0, k, 0:LEN] = tn(pick[...], plow).astype(bf16)
        plow_ref[0, k, LEN:ROWS] = jnp.zeros((ROWS - LEN, plow.shape[1]), bf16)


def input_backward(t_ref, tok, gmid, plow, w0, w1, w2, w3, sv, out_ref, small_ref, wlow):
    @pl.when(pl.program_id(0) == 0)
    def _():
        small_ref[...] = jnp.zeros_like(small_ref)
        for k, w in enumerate((w0, w1, w2, w3)):
            wlow[k] = w[...].astype(bf16)

    u = nt(plow[0, 0], wlow[0])
    for k in range(1, 4):
        u = u + nt(plow[0, k], wlow[k])
    u = u[0:LEN]
    n, scale = norm_parts(tok[0].astype(f32))
    small_ref[0:1] += jnp.sum(u * n, axis=0, keepdims=True)
    small_ref[1:2] += jnp.sum(u, axis=0, keepdims=True)
    out_ref[0] = gmid[0:LEN] + norm_back(n, scale, sv[0:1], u)


def assemble(t_ref, a0, a1, a2, a3, out):
    for k, a in enumerate((a0, a1, a2, a3)):
        @pl.when(pl.program_id(0) == k)
        def _(a=a):
            out[...] = a[...].astype(out.dtype)


def split_low(x, parts):
    out = []
    for _ in range(parts):
        low = x.astype(bf16)
        out.append(low)
        x = x - low.astype(f32)
    return out


def spread_product(left, right, terms, product=nn):
    total = None
    for i, j in terms:
        part = product(left[i], right[j])
        total = part if total is None else total + part
    return total


def symmetric_product(out, left, right, terms):
    half = out.shape[0] // 2
    top = [x[:half] for x in left]
    bottom = [x[half:] for x in left]
    first = [x[:, :half] for x in right]
    second = [x[:, half:] for x in right]
    out[:half, :half] = spread_product(top, first, terms)
    cross = spread_product(top, second, terms)
    out[:half, half:] = cross
    out[half:, :half] = cross.T
    out[half:, half:] = spread_product(bottom, second, terms)


three_terms = ((1, 0), (0, 1), (0, 0))
six_terms = ((2, 0), (0, 2), (1, 1)) + three_terms


def gram_kernel(spans, flip, t_ref, same, other, g_ref):
    for n, (start, stop) in enumerate(spans):
        a = split_low(same[:, start:stop], 3)
        b = split_low(other[:, start:stop], 3)
        half = same.shape[0]
        place = (t_ref[0] % 2) ^ (n ^ flip)
        for m, (left, right) in enumerate(((a, a), (a, b), (b, b))):
            g_ref[place, :, m * half : (m + 1) * half] = spread_product(left, right, six_terms, nt)


def newton_schulz(t_ref, keep_a, near_a, far_a, keep_i, near_i, far_i, rows_ref, a_s, p_s, t_s, q_s):
    inner = (t_ref[0] == 1) | (t_ref[0] == 2)
    g = jnp.where(
        inner, keep_a[0] + near_a[...] + far_a[...], keep_i[0] + near_i[...] + far_i[...]
    )
    half = g.shape[0]
    size = 2 * half
    cross = g[:, half:size]
    a_s[:half, :half] = g[:, :half]
    a_s[:half, half:] = cross
    a_s[half:, :half] = cross.T
    a_s[half:, half:] = g[:, size:]
    row = lax.broadcasted_iota(jnp.int32, (size, size), 0)
    col = lax.broadcasted_iota(jnp.int32, (size, size), 1)
    eye = jnp.where(row == col, 1.0, 0.0)
    whole = a_s[...]
    inv = 1.0 / (jnp.sum(jnp.sum(whole * eye, axis=0, keepdims=True), axis=1, keepdims=True) + 1e-07)
    a_s[...] = whole * inv
    c0, c1, c2 = quintic_coef
    for step in range(NS_STEPS - 1):
        exact = step < 3
        terms = six_terms if exact else three_terms
        parts = split_low(a_s[...], 3 if exact else 2)
        symmetric_product(t_s, parts, parts, terms)
        p_s[...] = c0 * eye + c1 * a_s[...] + c2 * t_s[...]
        poly = split_low(p_s[...], 3 if exact else 2)
        if step == 0:
            q_s[...] = p_s[...]
        else:
            symmetric_product(q_s, poly, split_low(q_s[...], 2), three_terms)
        symmetric_product(t_s, poly, parts, terms)
        symmetric_product(a_s, poly, split_low(t_s[...], 3 if exact else 2), terms)
    count = rows_ref.shape[0]
    parts = split_low(a_s[...], 2)
    square = spread_product([x[:count] for x in parts], parts, three_terms)
    poly = split_low(c0 * eye[:count] + c1 * a_s[0:count] + c2 * square, 2)
    rows_ref[...] = spread_product(poly, split_low(q_s[...], 2), three_terms) * jnp.sqrt(inv)


def final_kernel(places, factors, t_ref, q0, q1, q2, q3, same_a, other_a, same_i, other_i, u_in,
                 u_exp, u_red, u_out, q_s):
    for k, q in enumerate((q0, q1, q2, q3)):
        q_s[t_ref[0] ^ k] = q[...]
    for m, (group, start, stop) in enumerate(places):
        same = (same_i, same_a)[group][:, start:stop]
        other = (other_i, other_a)[group][:, start:stop]
        half = same.shape[0]
        u = (-matrix_rate * factors[m]) * (
            nn(q_s[m, :, 0:half], same, precision=highest)
            + nn(q_s[m, :, half:], other, precision=highest)
        )
        ref = (u_in, u_exp, u_red, u_out)[m]
        ref[...] = u


def after(value, *earlier):
    return lax.optimization_barrier((value, *earlier))[0]


def xor_tensor(x, k):
    return lax.ppermute(x, "tensor", [(i, i ^ k) for i in range(lax.axis_size("tensor"))])


def xor_dp(x, k):
    return lax.ppermute(x, "dp", [(i, i ^ k) for i in range(lax.axis_size("dp"))])


def gather_tensor(block, *earlier, late=None):
    near = xor_tensor(block, 1)
    far = xor_tensor(after(block, *earlier) if earlier else block, 2)
    return [block, near, far, xor_tensor(far if late is None else after(far, late), 1)]


def scatter_tensor(blocks):
    got = xor_tensor(jnp.stack([blocks[1], blocks[3]]), 1)
    own = blocks[0] + got[0]
    far = blocks[2] + got[1]
    return own + xor_tensor(far, 2)


def first_stage(own, far):
    rows = lax.axis_size("dp") * own.piece
    half, quarter = rows // 2, rows // 4
    return far(0, half), jnp.stack([own(half + quarter, rows), far(half + quarter, rows)])


def second_stage(own, far, got_t, got_d):
    rows = lax.axis_size("dp") * own.piece
    half, quarter = rows // 2, rows // 4
    last = own(quarter, half) + got_t[quarter:]
    return far(half, half + quarter) + got_d[1], last, own(0, quarter) + got_t[:quarter]


def third_stage(own, keep, got_d, last_t, last_d):
    piece = own.piece
    rows = lax.axis_size("dp") * piece
    half, quarter = rows // 2, rows // 4
    pieces = [keep[i : i + piece] + last_d[i : i + piece] for i in range(0, quarter, piece)]
    for i in range(0, quarter, piece):
        start = half + i
        pieces.append(
            own(start, start + piece) + got_d[0, i : i + piece] + last_t[i : i + piece]
        )
    return pieces


class Summed:
    def __init__(self, piece, *groups):
        self.piece = piece
        self.groups = groups

    def __call__(self, start, stop):
        return jnp.concatenate([a[start:stop] + b[start:stop] for a, b in self.groups], axis=1)


def low_bit_stage(own, far):
    rows = lax.axis_size("dp") * own.piece
    half, quarter = rows // 2, rows // 4
    spans = ((quarter, half), (half + quarter, rows))
    return jnp.stack([part(a, b) for part in (own, far) for a, b in spans])


def tensor_stage(far, got):
    rows = lax.axis_size("dp") * far.piece
    half, quarter = rows // 2, rows // 4
    return jnp.concatenate([far(0, quarter) + got[2], far(half, half + quarter) + got[3]])


def last_pieces(own, got, last):
    piece = own.piece
    rows = lax.axis_size("dp") * piece
    half, quarter = rows // 2, rows // 4
    pieces = []
    for n, start in enumerate((0, half)):
        for i in range(0, quarter, piece):
            at = n * quarter + i
            pieces.append(
                own(start + i, start + i + piece) + got[n, i : i + piece] + last[at : at + piece]
            )
    return pieces


def send_groups(pieces):
    return [xor_dp(p, 2 * g) for g, p in enumerate(pieces) if g > 0]


def barrier(*values):
    return lax.optimization_barrier(values)


def join_images(t, parts, dtype):
    images, length, features = parts[0].shape
    return pl.pallas_call(
        assemble,
        grid_spec=pltpu.PrefetchScalarGridSpec(
            num_scalar_prefetch=1,
            grid=(4,),
            in_specs=[pl.BlockSpec((images, length, features), lambda a, t_ref: (0, 0, 0))] * 4,
            out_specs=pl.BlockSpec(
                (images, length, features), lambda a, t_ref: (t_ref[0] ^ a, 0, 0)
            ),
        ),
        out_shape=jax.ShapeDtypeStruct((4 * images, length, features), dtype),
        compiler_params=params(),
        cost_estimate=heavy,
        name="join_images",
    )(t, *parts)


def local(
    tokens,
    cotangent,
    region_ids,
    relative_index,
    shared_vectors,
    input_weight,
    head_bias,
    output_weight,
    expand_weight,
    expand_bias,
    reduce_weight,
    bias_table,
    moment_shared,
    moment_input,
    moment_head,
    moment_output,
    moment_expand,
    moment_bias,
    moment_reduce,
    moment_table,
):
    nt_axis = lax.axis_size("tensor")
    me_t = lax.axis_index("tensor")
    me_d = lax.axis_index("dp")
    nd = lax.axis_size("dp")
    all_images, length, features = tokens.shape
    images = all_images // nt_axis
    heads = bias_table.shape[1]
    head_size = head_bias.shape[1] // heads
    width = heads * head_size
    hidden_here = expand_weight.shape[1]
    table_rows = bias_table.shape[0]
    query_scale = head_size ** (-0.5)
    low_d = me_d % 2
    t_arr = jnp.stack([me_t, me_d, low_d]).astype(jnp.int32)
    rows = -(-images * ROWS // 128) * 128
    lanes = heads * WPAD

    pad_lanes = lambda x: jnp.pad(x, ((0, 0), (0, features - x.shape[1])))
    pack = jnp.concatenate(
        [
            pad_lanes(bias_table.T),
            pad_lanes(head_bias.reshape(1, 2 * width)),
            pad_lanes(expand_bias.reshape(1, hidden_here)),
            jnp.zeros((2, features), f32),
        ]
    )
    packs = [pack, xor_tensor(pack, 1), xor_tensor(pack, 2)]
    w_in = [input_weight, xor_tensor(input_weight, 1)]
    w_in.append(xor_tensor(after(input_weight, pack), 2))
    w_out = [output_weight, xor_tensor(output_weight, 1), xor_tensor(output_weight, 2)]
    w_exp = [expand_weight, xor_tensor(expand_weight, 1)]
    w_red = [reduce_weight, xor_tensor(reduce_weight, 1)]

    pick_np, place_np = window_tables()
    pick = jnp.asarray(pick_np, bf16)
    order = jnp.asarray(column_order(heads, head_size), bf16)
    rel_t = jnp.pad(relative_index.T, ((0, WPAD - WIN2), (0, WPAD - WIN2)), constant_values=-1)
    rel_wide = jnp.tile(rel_t, (1, heads))
    region = region_ids.reshape(2, WIN, 2, WIN).transpose(0, 2, 1, 3).reshape(4, WIN2)
    region = jnp.pad(region, ((0, 0), (0, WPAD - WIN2)))
    region_both = jnp.concatenate(
        [
            jnp.broadcast_to(region[:, :, None], (4, WPAD, lanes)),
            jnp.broadcast_to(jnp.tile(region, (1, heads))[:, None, :], (4, WPAD, lanes)),
        ]
    )
    spread = np.zeros((2 * heads, 2 * lanes), np.float32)
    for h in range(2 * heads):
        spread[h, h * WPAD : (h + 1) * WPAD] = 1.0
    sds = jax.ShapeDtypeStruct
    pack_spec = pl.BlockSpec((8, features), lambda i, *_: (0, 0))

    def bias_of(blocks):
        return pl.pallas_call(
            bias_kernel,
            grid=(1,),
            in_specs=[pack_spec] * 2
            + [
                pl.BlockSpec((2 * heads, 2 * lanes), lambda i: (0, 0)),
                pl.BlockSpec((WPAD, lanes), lambda i: (0, 0)),
            ],
            out_specs=pl.BlockSpec((2, WPAD, lanes), lambda i: (0, 0, 0)),
            out_shape=sds((2, WPAD, lanes), f32),
            scratch_shapes=[pltpu.VMEM((256, 2 * lanes), f32)],
            compiler_params=params(),
            cost_estimate=light,
            name="bias",
        )(*blocks, jnp.asarray(spread), rel_wide)

    mask = pl.pallas_call(
        mask_kernel,
        in_specs=[VMEM],
        out_specs=VMEM,
        out_shape=sds((4, WPAD, lanes), f32),
        compiler_params=params(),
        cost_estimate=light,
        name="mask",
    )(region_both)
    bias_a = bias_of(packs[:2])
    piece = features // nd
    row_at = me_d * piece
    moment_a = jnp.concatenate(
        [
            lax.dynamic_slice_in_dim(moment_expand, row_at, piece, 0),
            lax.dynamic_slice_in_dim(moment_reduce, row_at, piece, 1).T,
        ],
        axis=1,
    )
    moment_i = jnp.concatenate(
        [
            lax.dynamic_slice_in_dim(moment_input, row_at, piece, 0),
            lax.dynamic_slice_in_dim(moment_output, row_at, piece, 1).T,
        ],
        axis=1,
    )
    packs.append(xor_tensor(packs[2], 1))
    bias_b = bias_of(packs[2:])
    w_in[2], w_out[2], bias_a, bias_b, mask, moment_a, moment_i = barrier(
        w_in[2], w_out[2], bias_a, bias_b, mask, moment_a, moment_i
    )
    w_in.append(xor_tensor(w_in[2], 1))
    w_out.append(xor_tensor(w_out[2], 1))
    far_exp = xor_tensor(after(expand_weight, bias_b), 2)
    far_red = xor_tensor(after(reduce_weight, w_in[2]), 2)

    whole = lambda *shape: pl.BlockSpec(shape, lambda i, *_: (0,) * len(shape))
    one = lambda *shape: pl.BlockSpec((1,) + shape, lambda i, *_: (i,) + (0,) * len(shape))
    tok_one = pl.BlockSpec((1, length, features), lambda i, t: (t[0] * images + i, 0, 0))
    probs, qkv, sht, ctx = pl.pallas_call(
        functools.partial(attn_forward, query_scale, nd),
        grid_spec=pltpu.PrefetchScalarGridSpec(
            num_scalar_prefetch=1,
            grid=(images,),
            in_specs=[tok_one]
            + [whole(features, 3 * width)] * 4
            + [pack_spec] * 4
            + [
                whole(6, features),
                whole(2, WPAD, lanes),
                whole(2, WPAD, lanes),
                whole(4, WPAD, lanes),
                whole(WROWS, LEN),
                whole(3 * width, 3 * width),
            ],
            out_specs=[
                one(4, 4, WPAD, lanes),
                one(4, WROWS, 3 * width),
                one(features, WROWS),
                one(ROWS, 4 * width),
            ],
            scratch_shapes=[pltpu.VMEM((4, features, 3 * width), bf16)],
        ),
        out_shape=[
            sds((images, 4, 4, WPAD, lanes), f32),
            sds((images, 4, WROWS, 3 * width), bf16),
            sds((images, features, WROWS), bf16),
            sds((images, ROWS, 4 * width), bf16),
        ],
        compiler_params=params(),
        cost_estimate=heavy,
        name="attn_forward",
    )(t_arr, tokens, *w_in, *packs, shared_vectors, bias_a, bias_b, mask, pick, order)

    tok_all = pl.BlockSpec((images, length, features), lambda i, t: (t[0], 0, 0))
    token_f = (rows, features)
    wide = 2 * hidden_here
    hidden_scratch = [
        pltpu.VMEM((4, features, hidden_here // 2), bf16),
        pltpu.VMEM((4, hidden_here // 2, features), bf16),
        pltpu.VMEM((4, 1, hidden_here // 2), f32),
        pltpu.VMEM((2, rows, hidden_here // 2), f32),
        pltpu.VMEM((rows, hidden_here // 2), bf16),
        pltpu.VMEM((rows, hidden_here // 2), bf16),
    ]
    state_shapes = [
        ((4 * width, features), bf16),
        (token_f, f32),
        (token_f, bf16),
        (token_f[::-1], bf16),
        (token_f, bf16),
        (token_f[::-1], bf16),
        (token_f, f32),
        (token_f, f32),
    ]
    *carry, keep_0, send_1, geb_a = pl.pallas_call(
        functools.partial(feed_first, images, nd),
        grid_spec=pltpu.PrefetchScalarGridSpec(
            num_scalar_prefetch=1,
            grid=(1,),
            in_specs=[whole(images, ROWS, 4 * width), tok_all, tok_all]
            + [whole(width, features)] * 4
            + [whole(features, hidden_here)] * 2
            + [whole(hidden_here, features)] * 2
            + [pack_spec] * 2
            + [whole(6, features)],
            out_specs=[whole(*shape) for shape, _ in state_shapes]
            + [whole(features, wide), whole(features, wide), whole(4, 1, hidden_here // 2)],
            scratch_shapes=hidden_scratch + [pltpu.VMEM(token_f, f32)],
        ),
        out_shape=[sds(shape, dtype) for shape, dtype in state_shapes]
        + [sds((features, wide), f32)] * 2
        + [sds((4, 1, hidden_here // 2), f32)],
        compiler_params=params(),
        cost_estimate=heavy,
        name="feed_first",
    )(t_arr, ctx, tokens, cotangent, *w_out, *w_exp, *w_red, *packs[:2], shared_vectors)

    far_exp = after(far_exp, geb_a)
    w_exp += [far_exp, xor_tensor(far_exp, 1)]
    far_red = after(far_red, geb_a)
    w_red += [far_red, xor_tensor(far_red, 1)]
    got_1 = xor_tensor(send_1, 1)

    wo_low, mid, n2_low, n2_t, cot_low, cot_t, mix, gn2 = carry
    mix, gn2, keep_2, send_3, geb_b = pl.pallas_call(
        feed_second,
        grid_spec=pltpu.PrefetchScalarGridSpec(
            num_scalar_prefetch=1,
            grid=(1,),
            in_specs=[whole(features, hidden_here)] * 2
            + [whole(hidden_here, features)] * 2
            + [pack_spec] * 2
            + [whole(*shape) for shape, _ in state_shapes[2:]],
            out_specs=[
                whole(rows, features),
                whole(rows, features),
                whole(features, wide),
                whole(features, wide),
                whole(4, 1, hidden_here // 2),
            ],
            scratch_shapes=hidden_scratch,
        ),
        out_shape=[
            sds((rows, features), f32),
            sds((rows, features), f32),
            sds((features, wide), f32),
            sds((features, wide), f32),
            sds((4, 1, hidden_here // 2), f32),
        ],
        compiler_params=params(),
        cost_estimate=light,
        name="feed_second",
    )(
        t_arr,
        *w_exp[2:],
        *w_red[2:],
        *packs[2:],
        n2_low,
        n2_t,
        cot_low,
        cot_t,
        mix,
        gn2,
    )
    got_3 = xor_tensor(send_3, 1)

    block_part, gmid, gctx, keep_o, send_o, small_a = pl.pallas_call(
        functools.partial(feed_last, images, nd),
        grid_spec=pltpu.PrefetchScalarGridSpec(
            num_scalar_prefetch=1,
            grid=(1,),
            in_specs=[
                whole(images, ROWS, 4 * width),
                whole(6, features),
                whole(4 * width, features),
            ]
            + [whole(rows, features)] * 4,
            out_specs=[
                whole(images, length, features),
                whole(rows, features),
                whole(images, ROWS, 4 * width),
                whole(2, features, width),
                whole(2, features, width),
                whole(8, features),
            ],
            scratch_shapes=[pltpu.VMEM(token_f[::-1], bf16)],
        ),
        out_shape=[
            sds((images, length, features), f32),
            sds((rows, features), f32),
            sds((images, ROWS, 4 * width), bf16),
            sds((2, features, width), f32),
            sds((2, features, width), f32),
            sds((8, features), f32),
        ],
        compiler_params=params(),
        cost_estimate=light,
        name="feed_last",
    )(t_arr, ctx, shared_vectors, wo_low, mid, cot_low, mix, gn2)

    got_o = xor_tensor(send_o, 1)
    got_3, gctx = barrier(got_3, gctx)
    own_a = Summed(piece, (keep_0, got_1))
    far_a = Summed(piece, (keep_2, got_3))
    t1_a, d1_a = first_stage(own_a, far_a)
    gctx, t1_a, d1_a = barrier(gctx, t1_a, d1_a)
    got_t1_a, got_d1_a = xor_tensor(t1_a, 2), xor_dp(d1_a, 1)

    keep_i, send_i, plow, gbias, ghead = pl.pallas_call(
        functools.partial(attn_backward, query_scale),
        grid=(images,),
        in_specs=[
            one(4, 4, WPAD, lanes),
            one(4, WROWS, 3 * width),
            one(ROWS, 4 * width),
            one(features, WROWS),
            whole(WROWS, LEN),
            whole(3 * width, 3 * width),
        ],
        out_specs=[
            whole(2, features, 3 * width),
            whole(2, features, 3 * width),
            one(4, ROWS, 3 * width),
            whole(4, WPAD, lanes),
            whole(4, 2, width),
        ],
        out_shape=[
            sds((2, features, 3 * width), f32),
            sds((2, features, 3 * width), f32),
            sds((images, 4, ROWS, 3 * width), bf16),
            sds((4, WPAD, lanes), f32),
            sds((4, 2, width), f32),
        ],
        compiler_params=params(),
        cost_estimate=light,
        name="attn_backward",
    )(probs, qkv, gctx, sht, pick, order)

    got_i = xor_tensor(send_i, 1)

    grad_part, small_i = pl.pallas_call(
        input_backward,
        grid_spec=pltpu.PrefetchScalarGridSpec(
            num_scalar_prefetch=1,
            grid=(images,),
            in_specs=[
                tok_one,
                pl.BlockSpec((ROWS, features), lambda i, t: (i, 0)),
                one(4, ROWS, 3 * width),
            ]
            + [whole(features, 3 * width)] * 4
            + [whole(6, features)],
            out_specs=[one(length, features), whole(8, features)],
            scratch_shapes=[pltpu.VMEM((4, features, 3 * width), bf16)],
        ),
        out_shape=[sds((images, length, features), f32), sds((8, features), f32)],
        compiler_params=params(),
        cost_estimate=light,
        name="input_backward",
    )(t_arr, tokens, gmid, plow, *w_in, shared_vectors)

    got_t1_a, got_d1_a, send_small_i = barrier(got_t1_a, got_d1_a, small_i)
    small_i = send_small_i
    t2_a, d2_a, kept_a = second_stage(own_a, far_a, got_t1_a, got_d1_a)
    got_t2_a, got_d2_a = xor_tensor(t2_a, 2), xor_dp(d2_a, 1)
    got_i, got_o = barrier(got_i, got_o, t2_a, d2_a)[:2]
    own_i = Summed(piece, (keep_i[0], got_i[0]), (keep_o[0], got_o[0]))
    far_i = Summed(piece, (keep_i[1], got_i[1]), (keep_o[1], got_o[1]))
    d1_i = low_bit_stage(own_i, far_i)
    got_d1_i = xor_dp(d1_i, 1)
    got_t2_a, got_d2_a, d1_i = barrier(got_t2_a, got_d2_a, d1_i)
    pieces_a = third_stage(own_a, kept_a, got_d1_a, got_t2_a, got_d2_a)
    got_a = send_groups(pieces_a)
    got_d1_i = barrier(got_d1_i, *got_a)[0]
    t2_i = tensor_stage(far_i, got_d1_i)
    got_t2_i = xor_tensor(t2_i, 2)
    gbias, ghead, small_i, geb_a, geb_b, small_a, rel_t = barrier(
        gbias, ghead, small_i, geb_a, geb_b, small_a, rel_t, *pieces_a
    )[:7]

    pick_table = (
        jnp.arange(table_rows)[:, None] == rel_t[:WIN2].reshape(1, -1)
    ).astype(f32)
    gb = gbias[:, :WIN2].reshape(4, WIN2, heads, WPAD).transpose(0, 2, 1, 3)
    gtable = lax.dot_general(
        gb.reshape(4 * heads, -1), pick_table, (((1,), (1,)), ((), ())), precision=highest
    ).reshape(4, heads * table_rows)
    shared_rows = jnp.concatenate([small_i[0:2], small_a[0:4]])
    geb = jnp.concatenate([geb_a, geb_b]).reshape(4, hidden_here)
    block_small = jnp.concatenate([gtable, ghead.reshape(4, -1), geb], axis=1)
    n_small = block_small.shape[1]
    small_send = jnp.concatenate([block_small[1], block_small[3], shared_rows.reshape(-1)])
    got_small = xor_tensor(small_send, 1)
    got_a = barrier(*got_a, small_send)[: len(got_a)]
    grad_scale = (all_images * length * nd) ** (-0.5)
    grad_a = sum(got_a, pieces_a[0]) * grad_scale
    state_a = moment_decay * moment_a + (1.0 - moment_decay) * grad_a
    same_a = [state_a] + send_groups([state_a] * (nd // 2))
    own_small = block_small[0] + got_small[:n_small]
    far_small = block_small[2] + got_small[n_small : 2 * n_small]
    shared_sum = shared_rows.reshape(-1) + got_small[2 * n_small :]
    small_send = jnp.concatenate([far_small, shared_sum])
    got_small = xor_tensor(small_send, 2)
    block_part = after(block_part, *pieces_a, got_small)
    block_parts = [block_part, xor_tensor(block_part, 1), xor_tensor(block_part, 2)]
    got_small = barrier(got_small, t2_i, state_a)[0]
    vector = jnp.concatenate([own_small, shared_sum]) + got_small
    got_small = xor_dp(vector, 1)
    *same_a, got_t2_i, got_small, far_block = barrier(
        *same_a, got_t2_i, got_small, block_parts[2]
    )
    block_parts = [block_parts[0], block_parts[1], far_block, xor_tensor(far_block, 1)]
    same_a = jnp.concatenate(same_a)
    other_a = xor_dp(same_a, 1)
    vector = vector + got_small
    small_parts = send_groups([vector] * (nd // 2))
    grad_part = after(grad_part, same_a)
    grad_parts = [grad_part, xor_tensor(grad_part, 1), xor_tensor(grad_part, 2)]
    got_t2_i = barrier(got_t2_i, same_a)[0]
    pieces_i = last_pieces(own_i, got_d1_i, got_t2_i)
    got_i = send_groups(pieces_i)
    grad_i = sum(got_i, pieces_i[0]) * grad_scale
    state_i = moment_decay * moment_i + (1.0 - moment_decay) * grad_i
    same_i = [state_i] + send_groups([state_i] * (nd // 2))
    other_a = after(other_a, state_i)
    vector = sum(barrier(*small_parts, state_i)[: len(small_parts)], vector)
    block_parts[1], block_parts[3] = barrier(block_parts[1], block_parts[3], state_i)[:2]
    block_out = join_images(t_arr, block_parts, bf16)

    places = [
        (0, 0, 3 * width),
        (1, 0, hidden_here),
        (1, hidden_here, wide),
        (0, 3 * width, 4 * width),
    ]
    half = features // 2
    scalars = pl.BlockSpec(memory_space=pltpu.SMEM)

    def grams(group, *operands):
        spans = [(b, c) for a, b, c in places if a == group]
        return pl.pallas_call(
            functools.partial(gram_kernel, spans, group),
            in_specs=[scalars] + [VMEM] * 2,
            out_specs=VMEM,
            out_shape=sds((2, half, 3 * half), f32),
            compiler_params=params(),
            cost_estimate=heavy,
            name="gram",
        )(t_arr, *operands)

    gram_a = grams(1, same_a, other_a)
    near_a = xor_tensor(gram_a[1], 1)
    same_i = jnp.concatenate(barrier(*same_i, block_out)[: len(same_i)])
    other_i = xor_dp(same_i, 1)
    near_a = barrier(near_a, same_i)[0]
    send_far = gram_a[0] + near_a
    far_a = lax.ppermute(send_far, "tensor", [(0, 2), (3, 1)])
    other_i, grad_far = barrier(other_i, grad_parts[2], send_far)[:2]
    gram_i = grams(0, same_i, other_i)
    near_i = xor_tensor(gram_i[1], 1)
    grad_far = after(grad_far, gram_i)
    grad_last = xor_tensor(grad_far, 1)
    near_i, far_a = barrier(near_i, far_a)
    far_i = lax.ppermute(gram_i[0] + near_i, "tensor", [(2, 0), (1, 3)])
    grad_near, grad_last = barrier(grad_parts[1], grad_last, near_i)[:2]
    input_grad = join_images(t_arr, [grad_parts[0], grad_near, grad_far, grad_last], f32)
    far_i = barrier(far_i, input_grad)[0]
    own_rows = pl.pallas_call(
        newton_schulz,
        in_specs=[scalars] + [VMEM] * 6,
        out_specs=VMEM,
        out_shape=sds((piece, features), f32),
        scratch_shapes=[pltpu.VMEM((features, features), f32)] * 4,
        compiler_params=params(),
        cost_estimate=light,
        name="newton_schulz",
    )(t_arr, gram_a, near_a, far_a, gram_i, near_i, far_i)
    near_rows = xor_tensor(own_rows, 1)
    far_rows = xor_tensor(own_rows, 2)
    factor = lambda a, b: math.sqrt(max(1.0, a / b))
    update_m = pl.pallas_call(
        functools.partial(
            final_kernel,
            places,
            [
                factor(features, 3 * width * nt_axis),
                factor(features, hidden_here * nt_axis),
                factor(hidden_here * nt_axis, features),
                factor(width * nt_axis, features),
            ],
        ),
        in_specs=[scalars] + [VMEM] * 8,
        out_specs=[VMEM] * 4,
        out_shape=[
            sds((piece, 3 * width), f32),
            sds((piece, hidden_here), f32),
            sds((piece, hidden_here), f32),
            sds((piece, width), f32),
        ],
        scratch_shapes=[pltpu.VMEM((4, piece, features), f32)],
        compiler_params=params(),
        cost_estimate=light,
        name="update",
    )(
        t_arr,
        own_rows,
        near_rows,
        far_rows,
        xor_tensor(far_rows, 1),
        same_a,
        other_a,
        same_i,
        other_i,
    )
    update_m = (update_m[0], update_m[3].T, update_m[1], update_m[2].T)

    vector = after(vector, near_i)
    at = heads * table_rows
    gradients = {
        "table": vector[:at].reshape(heads, table_rows).T,
        "head": vector[at : at + 2 * width].reshape(2, width),
        "bias": vector[at + 2 * width : n_small],
        "shared": vector[n_small:].reshape(6, features),
    }
    moments = dict(table=moment_table, head=moment_head, bias=moment_bias, shared=moment_shared)
    gradients = {k: v * grad_scale for k, v in gradients.items()}
    states = {
        k: moment_decay * moments[k] + (1.0 - moment_decay) * gradients[k] for k in gradients
    }

    def split(part_i, part_a):
        a, b, c, d = [(part_i, part_a)[g][:, s:e] for g, s, e in places]
        return a, d.T, b, c.T

    grad_m = split(grad_i, grad_a)
    state_m = split(state_i, state_a)
    return (
        block_out,
        input_grad,
        gradients["shared"],
        grad_m[0],
        gradients["head"],
        grad_m[1],
        grad_m[2],
        gradients["bias"],
        grad_m[3],
        gradients["table"],
        -vector_rate * states["shared"],
        update_m[0],
        -vector_rate * states["head"],
        update_m[1],
        update_m[2],
        -vector_rate * states["bias"],
        update_m[3],
        -vector_rate * states["table"],
        states["shared"],
        state_m[0],
        states["head"],
        state_m[1],
        state_m[2],
        states["bias"],
        state_m[3],
        states["table"],
    )


def solution(mesh):
    return jax.shard_map(
        local,
        mesh=mesh,
        in_specs=(
            P("dp", None, None),
            P("dp", None, None),
            P(),
            P(),
            P(),
            P(None, "tensor"),
            P(None, "tensor"),
            P("tensor", None),
            P(None, "tensor"),
            P("tensor"),
            P("tensor", None),
            P(None, "tensor"),
            P(),
            P(None, "tensor"),
            P(None, "tensor"),
            P("tensor", None),
            P(None, "tensor"),
            P("tensor"),
            P("tensor", None),
            P(None, "tensor"),
        ),
        out_specs=(
            P("dp", None, None),
            P("dp", None, None),
            P(),
            P("dp", "tensor"),
            P(None, "tensor"),
            P("tensor", "dp"),
            P("dp", "tensor"),
            P("tensor"),
            P("tensor", "dp"),
            P(None, "tensor"),
            P(),
            P("dp", "tensor"),
            P(None, "tensor"),
            P("tensor", "dp"),
            P("dp", "tensor"),
            P("tensor"),
            P("tensor", "dp"),
            P(None, "tensor"),
            P(),
            P("dp", "tensor"),
            P(None, "tensor"),
            P("tensor", "dp"),
            P("dp", "tensor"),
            P("tensor"),
            P("tensor", "dp"),
            P(None, "tensor"),
        ),
        check_vma=False,
    )
```
